32 devices in a mesh: groups: 2 (over y), seq: 4 (over z), chan: 2 (over x), sub: 2 (over core).
Axes of the slice: x: 2, y: 2, z: 4, core: 2. Of those that a mesh axis runs over, the one named last changes fastest.
Arguments:
- features: bfloat16 [3, 4096, 2048], P(None, ('chan', 'sub'), ('groups', 'seq')), parts along dimension 2, may hold values from -6 to 6
- dout: bfloat16 [4096, 2048], P(('chan', 'sub'), ('groups', 'seq')), parts along dimension 1, may hold values from -6 to 6
- filters: bfloat16 [4096, 1024], P(('chan', 'sub'), 'seq'), may hold values from -0.1875 to 0.1875
- taps: float32 [3, 3, 4096], P(None, None, ('chan', 'sub')), may hold values from -3.5 to 3.5
- skip: float32 [4096], P(('chan', 'sub')), may hold values from -4 to 4
- lengths: int32 [32], P('groups'), parts along dimension 0, may hold values from 1 to 256, 1024 in all
Outputs:
- out: bfloat16 [4096, 2048], P(('chan', 'sub'), ('groups', 'seq')), parts along dimension 1
- dfeatures: bfloat16 [3, 4096, 2048], P(None, ('chan', 'sub'), ('groups', 'seq')), parts along dimension 2
The draws below stay inside these ranges and needn't reach their ends.
There are 2 independent parts, one for each index of `groups`. The reference program is written for one: setup_inputs(seed, part) draws one part's arguments, and reference() takes and returns one part's arrays. A program takes and returns all parts, laid end to end along the dimension named above; an argument that names none is the same for every part. Nothing has to cross between parts.
Inputs may be any that keep to these rules, and one draw needn't show every extreme that they name: The lengths of one part sum to 1024, and the longest genome has exactly 256 positions.
All inputs are finite; a program needn't handle non-finite values.
Results may differ from the reference program's by a relative error of at most 0.01.
Values may be sent and summed in bfloat16 or wider, within the bound.
No kernel may reach another device: no remote copies, remote signals or barrier semaphores. Data moves between devices by JAX's collectives and lax.ppermute only.
A program may use at most 64 MiB of HBM per device.

```python
import math
import jax
import jax.numpy as jnp
import numpy as np

D = 4096
TAPS = 3
GENOMES = 16
LEN = 1024
MOST = 256


def block_levels(own_key, shape, shards, low, high):
    def one(position, blocks):
        steps = jax.random.uniform(jax.random.fold_in(jax.random.fold_in(own_key, 6), position), (blocks,), jnp.float32, low / len(shards), high / len(shards))
        return jnp.repeat(jnp.exp(steps), shape[position] // blocks).reshape((-1,) + (1,) * (len(shape) - position - 1))

    loudness = one(*shards[0])
    for cut in shards[1:]:
        loudness = loudness * one(*cut)
    return loudness


def length_profile(amount, total, limit, slope):
    portions = [(1 << 20) // math.isqrt(standing ** slope) + 1 for standing in range(2, amount + 1)]
    surplus, counts = total - limit - (amount - 1), [1] * (amount - 1)
    while surplus > 0:
        free = [i for i in range(amount - 1) if counts[i] < limit]
        pool, budget = sum([portions[i] for i in free]), surplus
        for i in free:
            more = min(limit - counts[i], max(1, budget * portions[i] // pool), surplus)
            counts[i] = counts[i] + more
            surplus = surplus - more
    return np.array([limit] + counts)


def uneven(rng, amount, total, reach, skew):
    if amount == 2:
        one = jax.random.randint(rng, (), max(1, total - reach), min(reach, total - 1) + 1)
        return jnp.stack([one, total - one])
    tallies = jnp.asarray(length_profile(amount, total, reach, skew), jnp.int32)
    couples = (amount - 1) // 2
    source_of, sink = tallies[1:1 + 2 * couples:2], tallies[2:2 + 2 * couples:2]
    slack = jnp.minimum(source_of - 1, reach - sink)
    shifted = jax.random.randint(jax.random.fold_in(rng, 1), (couples,), 0, 1 << 20) % (slack + 1)
    tallies = tallies.at[1:1 + 2 * couples:2].set(source_of - shifted).at[2:2 + 2 * couples:2].set(sink + shifted)
    return tallies[jax.random.permutation(jax.random.fold_in(rng, 2), amount)]


def centred(own_key, extent, scale, reach, pieces=(), kind=jnp.bfloat16):
    array = jax.random.normal(own_key, extent, jnp.float32) * scale
    if len(pieces) > 0:
        array = block_levels(own_key, extent, pieces, -0.22, 0.18) * array
    return jnp.clip(array, min=-reach, max=reach).astype(kind)


def setup_inputs(seed: int = 0, part: int = 0) -> dict:
    key_of = jax.random.split(jax.random.key(seed), 7)
    part_keys = jax.random.split(jax.random.fold_in(key_of[6], part), 7)
    return {
        "features": centred(part_keys[0], (3, D, LEN), 1.0, 6.0, ((1, 4), (2, 4))),
        "dout": centred(part_keys[1], (D, LEN), 1.0, 6.0, ((0, 4), (1, 4))),
        "filters": centred(key_of[2], (D, LEN), LEN ** -0.5, 0.1875, ((0, 4), (1, 4))),
        "taps": centred(key_of[3], (3, TAPS, D), TAPS ** -0.5, 3.5, ((2, 4),), jnp.float32),
        "skip": centred(key_of[4], (D,), 1.0, 4.0, ((0, 4),), jnp.float32),
        "lengths": uneven(part_keys[5], GENOMES, LEN, MOST, 2).astype(jnp.int32),
    }


def genome_offsets(lengths, positions):
    ends_at = jnp.cumsum(lengths, dtype=jnp.int32)
    before = (ends_at[None, :] <= positions[:, None]).astype(jnp.int32)
    return positions - jnp.sum(before * lengths[None, :], axis=1, dtype=jnp.int32)


def short_forward(extended, taps_local, offsets):
    span_rows = offsets.shape[0]
    count = taps_local.shape[1]
    result = jnp.zeros(extended.shape[:2] + (span_rows,), jnp.float32)
    for tap_index in range(count):
        begin = count - 1 - tap_index
        window = extended[:, :, begin:begin + span_rows].astype(jnp.float32)
        keep_mask = (offsets >= tap_index).astype(jnp.float32)
        result = result + taps_local[:, tap_index, :, None] * window * keep_mask[None, None, :]
    return result


def short_backward(grads_ext, taps_local, offsets_ext):
    count = taps_local.shape[1]
    span_rows = offsets_ext.shape[0] - (count - 1)
    result = jnp.zeros(grads_ext.shape[:2] + (span_rows,), jnp.float32)
    for tap_index in range(count):
        window = grads_ext[:, :, tap_index:tap_index + span_rows]
        keep_mask = (offsets_ext[tap_index:tap_index + span_rows] >= tap_index).astype(jnp.float32)
        result = result + taps_local[:, tap_index, :, None] * window * keep_mask[None, None, :]
    return result


def reference(features, dout, filters, taps, skip, lengths):
    margin = TAPS - 1
    positions = jnp.arange(LEN, dtype=jnp.int32)
    offsets = genome_offsets(lengths, positions)
    extended = jnp.pad(features, ((0, 0), (0, 0), (margin, 0)))
    filtered = short_forward(extended, taps, offsets).astype(jnp.bfloat16)
    query_side = filtered[0].astype(jnp.float32)
    key_side = filtered[1].astype(jnp.float32)
    value_side = filtered[2].astype(jnp.float32)
    dout_f = dout.astype(jnp.float32)
    mixed = (key_side * value_side).astype(jnp.bfloat16).astype(jnp.float32)
    grad_in = (dout_f * query_side).astype(jnp.bfloat16).astype(jnp.float32)
    length_fft = 2 * LEN
    filt_spec = jnp.fft.rfft(filters.astype(jnp.float32), n=length_fft, axis=1)
    mixed_spec = jnp.fft.rfft(mixed, n=length_fft, axis=1)
    grad_spec = jnp.fft.rfft(grad_in, n=length_fft, axis=1)
    conv = jnp.fft.irfft(filt_spec * mixed_spec, n=length_fft, axis=1)[:, :LEN]
    corr = jnp.fft.irfft(jnp.conj(filt_spec) * grad_spec, n=length_fft, axis=1)[:, :LEN]
    conv = conv.astype(jnp.float32)
    corr = corr.astype(jnp.float32)
    y_out = (conv + skip[:, None] * mixed).astype(jnp.bfloat16).astype(jnp.float32)
    dmixed = (corr + skip[:, None] * grad_in).astype(jnp.bfloat16).astype(jnp.float32)
    out = (query_side * y_out).astype(jnp.bfloat16)
    grads = jnp.stack([dout_f * y_out, dmixed * value_side, dmixed * key_side])
    grads_ext = jnp.pad(grads, ((0, 0), (0, 0), (0, margin)))
    offsets_ext = genome_offsets(lengths, jnp.arange(LEN + margin, dtype=jnp.int32))
    dfeatures = short_backward(grads_ext, taps, offsets_ext).astype(jnp.bfloat16)
    return (out, dfeatures)
```

```python
import functools
import math

import jax
import jax.numpy as jnp
import numpy as np
from jax import lax
from jax.experimental import pallas as pl
from jax.experimental.pallas import tpu as pltpu
from jax.sharding import PartitionSpec as P

BF16 = jnp.bfloat16
F32 = jnp.float32
VMEM_LIMIT = 48 * 1024 * 1024
WHOLE = pl.BlockSpec(memory_space=pltpu.VMEM)
SCALARS = pl.BlockSpec(memory_space=pltpu.SMEM)


def split_bf16(table):
    high = table.astype(np.float32).astype(BF16)
    low = (table - high.astype(np.float64)).astype(np.float32).astype(BF16)
    return high, low


def block_tables(span):
    freq = np.concatenate([np.arange(0, span, 2), np.arange(1, span, 2)])
    angle = np.pi * (2 * freq[None, :] + 1) * np.arange(span)[:, None] / (2 * span)
    forward = np.concatenate([np.cos(angle), -np.sin(angle)], axis=1)
    inverse = np.concatenate([np.cos(angle), -np.sin(angle)], axis=1).T / span
    return split_bf16(forward) + split_bf16(inverse)


def dot(a, b):
    return jnp.dot(a, b, preferred_element_type=F32)


def call(body, outs, scratch=(), in_specs=None, grid=None, out_specs=None, aliases=None, cost=None):
    return pl.pallas_call(
        body,
        out_shape=outs,
        in_specs=in_specs,
        out_specs=out_specs,
        grid=grid or (),
        scratch_shapes=scratch,
        input_output_aliases=aliases or {},
        compiler_params=pltpu.CompilerParams(vmem_limit_bytes=VMEM_LIMIT),
        cost_estimate=cost,
    )


def estimate(flops, moved):
    return pl.CostEstimate(flops=int(flops), bytes_accessed=int(moved), transcendentals=0)


def offsets_row(lengths_ref, first, span, ahead):
    position = lax.broadcasted_iota(jnp.int32, (8, span), 1) + (first + ahead)

    def step(genome, carry):
        end, start = carry
        end = end + lengths_ref[genome]
        return end, jnp.where(position >= end, end, start)

    begin = (jnp.int32(0), jnp.zeros((8, span), jnp.int32))
    _, start = lax.fori_loop(0, lengths_ref.shape[0], step, begin)
    return position, position - start


def pack_body(parts, rank_ref, tail_ref, filt_ref, taps_ref, skip_ref, halo_ref, cols_ref, *rest):
    filt_out, rows_ref, halo_rows = rest[:parts], rest[parts], rest[parts + 1]
    rank = rank_ref[0]
    size = filt_out[0].shape[0]
    for step in range(parts):
        begin = pl.multiple_of(jnp.bitwise_xor(rank, step) * size, size)
        filt_out[step][...] = filt_ref[pl.ds(begin, size), :]
    halo_rows[...] = jnp.zeros(halo_rows.shape, F32)
    for which in range(3):
        turned = tail_ref[which].astype(F32).T
        halo_rows[2 * which : 2 * which + 2, :] = turned[-2:, :]
    halo_ref[...] = halo_rows[...].astype(BF16)
    rows_ref[...] = jnp.zeros(rows_ref.shape, F32)
    for which in range(3):
        rows_ref[3 * which : 3 * which + 3, :] = taps_ref[which]
    rows_ref[9:10, :] = skip_ref[...]
    cols_ref[...] = rows_ref[...].T


def pack(rank, features, filters, taps, skip, parts):
    _, channels, span = features.shape
    size = channels // parts
    outs = [
        jax.ShapeDtypeStruct((16, channels), BF16),
        jax.ShapeDtypeStruct((channels, 16), F32),
    ] + [jax.ShapeDtypeStruct((size, span), BF16)] * parts
    tail = pl.BlockSpec((3, channels, 128), lambda step: (0, 0, span // 128 - 1))
    found = call(
        functools.partial(pack_body, parts),
        outs,
        scratch=[pltpu.VMEM((16, channels), F32), pltpu.VMEM((16, channels), F32)],
        grid=(1,),
        in_specs=[SCALARS, tail, WHOLE, WHOLE, WHOLE],
        out_specs=[WHOLE] * len(outs),
        cost=estimate(0, 3 * channels * span * 2),
    )(rank, features, filters, taps, skip.reshape(1, channels))
    return found[0], found[1], found[2:]


def gate_body(parts, chunks, rank_ref, lengths_ref, feat_ref, dout_ref, halo_ref, cols_ref, qkv_ref, *rest):
    sent, edge = rest[: parts * chunks], rest[-1]
    rank = rank_ref[0]
    _, channels, span = feat_ref.shape
    rows = channels // parts // chunks
    group = min(32, rows)
    _, offset = offsets_row(lengths_ref, rank * span, span, 0)
    keep = [(offset[0:1, :] >= j).astype(F32) for j in (1, 2)]
    lane = lax.broadcasted_iota(jnp.int32, (group, span), 1)
    edge[...] = halo_ref[...].astype(F32).T
    for step in range(parts):
        for chunk in range(chunks):
            out = sent[step * chunks + chunk]
            base = (jnp.bitwise_xor(rank, step) * chunks + chunk) * rows

            def tile(index, _, base=base, out=out):
                place = pl.ds(pl.multiple_of(base + index * group, group), group)
                local_place = pl.ds(pl.multiple_of(index * group, group), group)
                cols = cols_ref[place, :]
                ends = edge[place, :]
                filtered = []
                for which in range(3):
                    here = feat_ref[which, place, :].astype(F32)
                    two_back = ends[:, 2 * which : 2 * which + 1]
                    one_back = ends[:, 2 * which + 1 : 2 * which + 2]
                    back = jnp.where(lane == 0, one_back, pltpu.roll(here, 1, 1))
                    twice = jnp.where(lane == 0, two_back, jnp.where(lane == 1, one_back, pltpu.roll(here, 2, 1)))
                    total = cols[:, 3 * which : 3 * which + 1] * here
                    total = total + cols[:, 3 * which + 1 : 3 * which + 2] * back * keep[0]
                    total = total + cols[:, 3 * which + 2 : 3 * which + 3] * twice * keep[1]
                    rounded = total.astype(BF16)
                    qkv_ref[which, place, :] = rounded
                    filtered.append(rounded.astype(F32))
                out[0, local_place, :] = (filtered[1] * filtered[2]).astype(BF16)
                out[1, local_place, :] = (dout_ref[place, :].astype(F32) * filtered[0]).astype(BF16)
                return 0

            lax.fori_loop(0, rows // group, tile, 0)


def gate(rank, lengths, features, dout, halo, cols, parts, chunks):
    _, channels, span = features.shape
    rows = channels // parts // chunks
    outs = [jax.ShapeDtypeStruct(features.shape, BF16)]
    outs += [jax.ShapeDtypeStruct((2, rows, span), BF16)] * (parts * chunks)
    found = call(
        functools.partial(gate_body, parts, chunks),
        outs,
        scratch=[pltpu.VMEM((channels, 16), F32)],
        in_specs=[SCALARS, SCALARS, WHOLE, WHOLE, WHOLE, WHOLE],
        out_specs=[WHOLE] * len(outs),
        cost=estimate(30 * channels * span, 9 * channels * span * 2),
    )(rank, lengths, features, dout, halo, cols)
    return found[0], [found[1 + step * chunks : 1 + (step + 1) * chunks] for step in range(parts)]


def conv_body(parts, rank_ref, cols_ref, fhi_ref, flo_ref, ihi_ref, ilo_ref, *rest):
    filt_in, moved_in = rest[:parts], rest[parts : 2 * parts]
    outs = rest[2 * parts : 3 * parts]
    raw, spec, high, low, back = rest[3 * parts :]
    rank = rank_ref[0]
    rows, span = filt_in[0].shape
    half = span // 2
    block = parts * rows
    for step in range(parts):
        slot = jnp.bitwise_xor(rank, step) * rows
        for kind in range(3):
            value = filt_in[step][...] if kind == 0 else moved_in[step][kind - 1]
            raw[pl.ds(pl.multiple_of(kind * block + slot, rows), rows), :] = value

    def forward(kind, _):
        place = pl.ds(pl.multiple_of(kind * block, block), block)
        value = raw[place, :]
        spec[place, :] = dot(value, fhi_ref[...]) + dot(value, flo_ref[...])
        return 0

    lax.fori_loop(0, 3, forward, 0)
    group = min(16, rows)

    def loop(count, body, init):
        if parts <= 4:
            for k in range(count):
                init = body(k, init)
            return init
        return lax.fori_loop(0, count, body, init)

    def products(index, _):
        def read(kind, k):
            begin = kind * block + k * rows + index * group
            place = pl.ds(pl.multiple_of(begin, group), group)
            return spec[place, :span], spec[place, span:]

        def store(kind, k, re, im):
            begin = kind * block + k * rows + index * group
            place = pl.ds(pl.multiple_of(begin, group), group)
            for begin_lane, part in ((0, re), (span, im)):
                top = part.astype(BF16)
                high[place, begin_lane : begin_lane + span] = top
                low[place, begin_lane : begin_lane + span] = (part - top.astype(F32)).astype(BF16)

        zero = jnp.zeros((group, span), F32)

        def turn(re, im):
            return (
                jnp.concatenate([-im[:, :half], im[:, half:]], axis=1),
                jnp.concatenate([re[:, :half], -re[:, half:]], axis=1),
            )

        before = None
        for place in range(parts):

            def add(k, total, place=place):
                f_re, f_im = read(0, k)
                m_re, m_im = read(1, place - k)
                return (total[0] + f_re * m_re - f_im * m_im, total[1] + f_re * m_im + f_im * m_re)

            re, im = loop(place + 1, add, (zero, zero))
            if before is None:
                store(0, place, re, im)
            else:
                t_re, t_im = turn(*before)
                store(0, place, re + t_re, im + t_im)
            before = (re, im)
        before = None
        for place in range(parts - 1, -1, -1):

            def add_conj(k, total, place=place):
                f_re, f_im = read(0, k)
                g_re, g_im = read(2, place + k)
                return (total[0] + f_re * g_re + f_im * g_im, total[1] + f_re * g_im - f_im * g_re)

            re, im = loop(parts - place, add_conj, (zero, zero))
            if before is None:
                store(1, place, re, im)
            else:
                t_re, t_im = turn(*before)
                store(1, place, re - t_re, im - t_im)
            before = (re, im)
        return 0

    lax.fori_loop(0, rows // group, products, 0)

    def inverse(kind, _):
        place = pl.ds(pl.multiple_of(kind * block, block), block)
        top = high[place, :]
        back[place, :] = dot(top, ihi_ref[...]) + dot(top, ilo_ref[...]) + dot(low[place, :], ihi_ref[...])
        return 0

    lax.fori_loop(0, 2, inverse, 0)
    skip = cols_ref[:, 9:10]
    for step in range(parts):
        slot = jnp.bitwise_xor(rank, step) * rows
        for kind in range(2):
            value = back[pl.ds(pl.multiple_of(kind * block + slot, rows), rows), :]
            direct = raw[pl.ds(pl.multiple_of((kind + 1) * block + slot, rows), rows), :].astype(F32)
            outs[step][kind] = (value + skip * direct).astype(BF16)


def conv(rank, cols, filt, moved, tables, chunk, chunks):
    parts = len(filt)
    _, rows, span = moved[0].shape
    block = parts * rows
    outs = [jax.ShapeDtypeStruct((2, rows, span), BF16)] * parts
    cols_spec = pl.BlockSpec((rows, 16), lambda step, rank_ref: (rank_ref[0] * chunks + chunk, 0))
    filt_spec = pl.BlockSpec((rows, span), lambda step, rank_ref: (chunk, 0))

    def fixed(shape):
        return pl.BlockSpec(shape, lambda step, rank_ref: (0,) * len(shape))

    in_specs = [cols_spec] + [fixed(t.shape) for t in tables] + [filt_spec] * parts + [fixed(moved[0].shape)] * parts
    flops = 2 * block * span * 2 * span * 12
    return pl.pallas_call(
        functools.partial(conv_body, parts),
        out_shape=outs,
        grid_spec=pltpu.PrefetchScalarGridSpec(
            num_scalar_prefetch=1,
            grid=(1,),
            in_specs=in_specs,
            out_specs=[fixed((2, rows, span))] * parts,
            scratch_shapes=[
                pltpu.VMEM((3 * block, span), BF16),
                pltpu.VMEM((3 * block, 2 * span), F32),
                pltpu.VMEM((2 * block, 2 * span), BF16),
                pltpu.VMEM((2 * block, 2 * span), BF16),
                pltpu.VMEM((2 * block, span), F32),
            ],
        ),
        compiler_params=pltpu.CompilerParams(vmem_limit_bytes=VMEM_LIMIT),
        cost_estimate=estimate(flops, 5 * block * span * 2),
    )(rank, cols, *tables, *filt, *moved)


def first_body(parts, chunk, chunks, rank_ref, qkv_ref, dout_ref, *rest):
    slots, out_ref, grads = rest[:parts], rest[parts], rest[parts + 1]
    rank = rank_ref[0]
    _, rows, lanes = slots[0].shape
    for step in range(parts):
        owner = jnp.bitwise_xor(rank, step)
        place = pl.ds(pl.multiple_of((owner * chunks + chunk) * rows, rows), rows)
        here = pl.ds(pl.multiple_of(owner * rows, rows), rows)
        y_out = slots[step][0].astype(F32)
        dmixed = slots[step][1].astype(F32)
        grads[0, here, :] = dout_ref[place, :].astype(F32) * y_out
        grads[1, here, :] = dmixed * qkv_ref[2, place, :].astype(F32)
        grads[2, here, :] = dmixed * qkv_ref[1, place, :].astype(F32)
    out_ref[...] = jnp.zeros(out_ref.shape, F32)
    for which in range(3):
        out_ref[2 * which : 2 * which + 2, :] = grads[which].T[0:2, :]


def first_grads(rank, qkv, dout, slots, chunk, chunks):
    parts = len(slots)
    _, rows, span = slots[0].shape
    channels = dout.shape[0]
    return call(
        functools.partial(first_body, parts, chunk, chunks),
        jax.ShapeDtypeStruct((8, parts * rows), F32),
        scratch=[pltpu.VMEM((3, parts * rows, 128), F32)],
        grid=(1,),
        in_specs=[
            SCALARS,
            pl.BlockSpec((3, channels, 128), lambda step: (0, 0, 0)),
            pl.BlockSpec((channels, 128), lambda step: (0, 0)),
        ]
        + [pl.BlockSpec((2, rows, 128), lambda step: (0, 0, 0))] * parts,
        out_specs=WHOLE,
        cost=estimate(0, 3 * channels * 128 * 2),
    )(rank, qkv, dout, *slots)


def final_body(parts, chunk, rank_ref, lengths_ref, qkv_ref, dout_ref, cols_ref, ahead_ref, *rest):
    slots = rest[:parts]
    out_ref, dfeat_ref, edge, moved = rest[-4:]
    rank = rank_ref[0]
    step = pl.program_id(0)
    _, rows, span = slots[0].shape

    @pl.when(step == 0)
    def _():
        edge[...] = ahead_ref[...].T

    for k in range(parts):

        @pl.when(step == k)
        def _(k=k):
            moved[...] = slots[k][...]

    owner = jnp.bitwise_xor(rank, step)
    group = min(32, rows)
    lane = lax.broadcasted_iota(jnp.int32, (group, span), 1)
    keep = []
    for j in (1, 2):
        position, offset = offsets_row(lengths_ref, rank * span, span, j)
        inside = (position < parts * span) & (offset >= j)
        keep.append(inside[0:1, :].astype(F32))

    def tile(index, _):
        place = pl.ds(pl.multiple_of(index * group, group), group)
        ends = edge[pl.ds(pl.multiple_of(owner * rows + index * group, group), group), :]
        cols = cols_ref[place, :]
        y_out = moved[0, place, :].astype(F32)
        dmixed = moved[1, place, :].astype(F32)
        out_ref[place, :] = (qkv_ref[0, place, :].astype(F32) * y_out).astype(BF16)
        grads = (
            dout_ref[place, :].astype(F32) * y_out,
            dmixed * qkv_ref[2, place, :].astype(F32),
            dmixed * qkv_ref[1, place, :].astype(F32),
        )
        for which in range(3):
            here = grads[which]
            first = ends[:, 2 * which : 2 * which + 1]
            second = ends[:, 2 * which + 1 : 2 * which + 2]
            next_one = jnp.where(lane == span - 1, first, pltpu.roll(here, span - 1, 1))
            next_two = jnp.where(
                lane == span - 1, second, jnp.where(lane == span - 2, first, pltpu.roll(here, span - 2, 1))
            )
            total = cols[:, 3 * which : 3 * which + 1] * here
            total = total + cols[:, 3 * which + 1 : 3 * which + 2] * next_one * keep[0]
            total = total + cols[:, 3 * which + 2 : 3 * which + 3] * next_two * keep[1]
            dfeat_ref[which, place, :] = total.astype(BF16)
        return 0

    lax.fori_loop(0, rows // group, tile, 0)


def final(rank, lengths, qkv, dout, cols, ahead, slots, chunk, chunks, earlier):
    parts = len(slots)
    _, rows, span = slots[0].shape
    channels = dout.shape[0]

    def block(step, rank_ref, lengths_ref):
        return jnp.bitwise_xor(rank_ref[0], step) * chunks + chunk

    def wide(step, *refs):
        return (0, block(step, *refs), 0)

    def flat(step, *refs):
        return (block(step, *refs), 0)

    def fixed(shape):
        return pl.BlockSpec(shape, lambda step, *refs: (0,) * len(shape))

    in_specs = [
        pl.BlockSpec((3, rows, span), wide),
        pl.BlockSpec((rows, span), flat),
        pl.BlockSpec((rows, 16), flat),
        fixed(ahead.shape),
    ] + [fixed(slots[0].shape)] * parts
    operands = [qkv, dout, cols, ahead, *slots]
    aliases = {}
    if earlier is not None:
        aliases = {2 + len(operands): 0, 3 + len(operands): 1}
        in_specs = in_specs + [pl.BlockSpec(memory_space=pl.ANY)] * 2
        operands = operands + list(earlier)
    return pl.pallas_call(
        functools.partial(final_body, parts, chunk),
        out_shape=[
            jax.ShapeDtypeStruct((channels, span), BF16),
            jax.ShapeDtypeStruct((3, channels, span), BF16),
        ],
        grid_spec=pltpu.PrefetchScalarGridSpec(
            num_scalar_prefetch=2,
            grid=(parts,),
            in_specs=in_specs,
            out_specs=[pl.BlockSpec((rows, span), flat), pl.BlockSpec((3, rows, span), wide)],
            scratch_shapes=[pltpu.VMEM((parts * rows, 8), F32), pltpu.VMEM((2, rows, span), BF16)],
        ),
        input_output_aliases=aliases,
        compiler_params=pltpu.CompilerParams(vmem_limit_bytes=VMEM_LIMIT),
        cost_estimate=estimate(40 * parts * rows * span, 10 * parts * rows * span * 2),
    )(rank, lengths, *operands)


def swap(value, step, parts):
    return lax.ppermute(value, "seq", [(source, source ^ step) for source in range(parts)])


def around(value, steps, parts):
    return lax.ppermute(value, "seq", [(source, (source + steps) % parts) for source in range(parts)])


def local(features, dout, filters, taps, skip, lengths):
    parts = lax.axis_size("seq")
    _, channels, span = features.shape
    chunks = 2 if channels // parts % 32 == 0 else 1
    rank = lax.axis_index("seq").astype(jnp.int32).reshape(1)
    tables = [jnp.asarray(t) for t in block_tables(span)]

    halo, cols, filt = pack(rank, features, filters, taps, skip, parts)
    halo = around(halo, 1, parts)
    filt = [filt[0]] + [swap(filt[step], step, parts) for step in range(1, parts)]
    qkv, sent = gate(rank, lengths, features, dout, halo, cols, parts, chunks)
    arrived = [
        [sent[0][c]] + [swap(sent[step][c], step, parts) for step in range(1, parts)] for c in range(chunks)
    ]
    done = None
    for c in range(chunks):
        back = conv(rank, cols, filt, arrived[c], tables, c, chunks)
        slots = [back[0]] + [swap(back[step], step, parts) for step in range(1, parts)]
        ahead = around(first_grads(rank, qkv, dout, slots, c, chunks), -1, parts)
        done = final(rank, lengths, qkv, dout, cols, ahead, slots, c, chunks, done)
    return tuple(done)


def solution(mesh):
    in_specs = (
        P(None, ("chan", "sub"), ("groups", "seq")),
        P(("chan", "sub"), ("groups", "seq")),
        P(("chan", "sub"), "seq"),
        P(None, None, ("chan", "sub")),
        P(("chan", "sub")),
        P("groups"),
    )
    out_specs = (P(("chan", "sub"), ("groups", "seq")), P(None, ("chan", "sub"), ("groups", "seq")))
    return jax.shard_map(local, mesh=mesh, in_specs=in_specs, out_specs=out_specs, check_vma=False)
```

```python
import functools
import math

import jax
import jax.numpy as jnp
import numpy as np
from jax import lax
from jax.experimental import pallas as pl
from jax.experimental.pallas import tpu as pltpu
from jax.sharding import PartitionSpec as P

BF16 = jnp.bfloat16
F32 = jnp.float32
VMEM_LIMIT = 48 * 1024 * 1024
WHOLE = pl.BlockSpec(memory_space=pltpu.VMEM)
SCALARS = pl.BlockSpec(memory_space=pltpu.SMEM)


def split_bf16(table):
    high = table.astype(np.float32).astype(BF16)
    low = (table - high.astype(np.float64)).astype(np.float32).astype(BF16)
    return high, low


def block_tables(span):
    freq = np.concatenate([np.arange(0, span, 2), np.arange(1, span, 2)])
    angle = np.pi * (2 * freq[None, :] + 1) * np.arange(span)[:, None] / (2 * span)
    forward = np.concatenate([np.cos(angle), -np.sin(angle)], axis=1)
    inverse = np.concatenate([np.cos(angle), -np.sin(angle)], axis=1).T / span
    return split_bf16(forward) + split_bf16(inverse)


def dot(a, b):
    return jnp.dot(a, b, preferred_element_type=F32)


def call(body, outs, scratch=(), in_specs=None, grid=None, out_specs=None, aliases=None, cost=None):
    return pl.pallas_call(
        body,
        out_shape=outs,
        in_specs=in_specs,
        out_specs=out_specs,
        grid=grid or (),
        scratch_shapes=scratch,
        input_output_aliases=aliases or {},
        compiler_params=pltpu.CompilerParams(vmem_limit_bytes=VMEM_LIMIT),
        cost_estimate=cost,
    )


def estimate(flops, moved):
    return pl.CostEstimate(flops=int(flops), bytes_accessed=int(moved), transcendentals=0)


def offsets_row(lengths_ref, first, span, ahead):
    position = lax.broadcasted_iota(jnp.int32, (8, span), 1) + (first + ahead)

    def step(genome, carry):
        end, start = carry
        end = end + lengths_ref[genome]
        return end, jnp.where(position >= end, end, start)

    begin = (jnp.int32(0), jnp.zeros((8, span), jnp.int32))
    _, start = lax.fori_loop(0, lengths_ref.shape[0], step, begin)
    return position, position - start


def masks_body(parts, rank_ref, lengths_ref, out_ref):
    _, span = out_ref.shape
    first = (rank_ref[0]) * span
    out_ref[...] = jnp.zeros(out_ref.shape, F32)
    _, offset = offsets_row(lengths_ref, first, span, 0)
    for j in (1, 2):
        out_ref[j - 1 : j, :] = (offset[0:1, :] >= j).astype(F32)
        position, later = offsets_row(lengths_ref, first, span, j)
        inside = (position < parts * span) & (later >= j)
        out_ref[1 + j : 2 + j, :] = inside[0:1, :].astype(F32)


def masks(place, lengths, parts, span):
    return call(
        functools.partial(masks_body, parts),
        jax.ShapeDtypeStruct((8, span), F32),
        in_specs=[SCALARS, SCALARS],
        out_specs=WHOLE,
        cost=estimate(0, 8192),
    )(place, lengths)


class Layout:
    def __init__(self, parts, channels, span):
        self.parts, self.channels, self.span = parts, channels, span
        self.half = parts // 2
        self.size = channels // self.half
        self.sub = self.size // 2


def fixed(shape):
    return pl.BlockSpec(shape, lambda *args: (0,) * len(shape))


def streamed(body, layout, place, operands, in_specs, outs, out_specs, scratch, grid, cost):
    return pl.pallas_call(
        functools.partial(body, layout),
        out_shape=outs,
        grid_spec=pltpu.PrefetchScalarGridSpec(
            num_scalar_prefetch=1,
            grid=grid,
            in_specs=in_specs,
            out_specs=out_specs,
            scratch_shapes=scratch,
        ),
        compiler_params=pltpu.CompilerParams(vmem_limit_bytes=VMEM_LIMIT),
        cost_estimate=cost,
    )(place, *operands)


def sides(place_ref, layout):
    rank = place_ref[0]
    return rank // layout.half, rank % layout.half


def sub_block(layout):
    def block(step, place_ref):
        _, own = sides(place_ref, layout)
        return jnp.bitwise_xor(own, step // 2) * 2 + step % 2

    return block


def pack_body(layout, place_ref, tail_ref, filt_ref, taps_ref, skip_ref, halo_ref, cols_ref, *rest):
    filt_out, turned = rest[: layout.half], rest[layout.half]
    _, own = sides(place_ref, layout)
    group = place_ref[1]
    for step in range(layout.half):
        begin = (jnp.bitwise_xor(own, step) * 2 + group) * layout.sub
        filt_out[step][...] = filt_ref[pl.ds(pl.multiple_of(begin, layout.sub), layout.sub), :]
    turned[...] = jnp.zeros(turned.shape, F32)
    for which in range(3):
        turned[2 * which : 2 * which + 2, :] = tail_ref[which].astype(F32).T[-2:, :]
    halo_ref[...] = turned[...].astype(BF16)
    turned[...] = jnp.zeros(turned.shape, F32)
    for which in range(3):
        turned[3 * which : 3 * which + 3, :] = taps_ref[which]
    turned[9:10, :] = skip_ref[...]
    cols_ref[...] = turned[...].T


def pack(layout, place, features, filters, taps, skip):
    channels, span = layout.channels, layout.span
    shapes = [((16, channels), BF16), ((channels, 16), F32)] + [((layout.sub, span), BF16)] * layout.half
    found = streamed(
        pack_body,
        layout,
        place,
        (features, filters, taps, skip.reshape(1, channels)),
        [
            pl.BlockSpec((3, channels, 128), lambda step, place_ref: (0, 0, span // 128 - 1)),
            fixed(filters.shape),
            fixed(taps.shape),
            fixed((1, channels)),
        ],
        [jax.ShapeDtypeStruct(*s) for s in shapes],
        [fixed(s[0]) for s in shapes],
        [pltpu.VMEM((16, channels), F32)],
        (1,),
        estimate(0, 3 * channels * span * 2),
    )
    return found[0], found[1], found[2:]


def gate_body(layout, place_ref, feat_ref, dout_ref, halo_ref, cols_ref, keep_ref, qkv_ref, *rest):
    half, rows, span = layout.half, layout.sub, layout.span
    inner, cross = rest[:half], rest[half : 2 * half]
    edge, made = rest[2 * half :]
    side, own = sides(place_ref, layout)
    step = pl.program_id(0)
    turn, sub = step // 2, step % 2
    base = sub_block(layout)(step, place_ref) * rows
    group = min(32, rows)

    @pl.when(step == 0)
    def _():
        edge[...] = halo_ref[...].astype(F32).T

    keep = keep_ref[0:1, :], keep_ref[1:2, :]
    lane = lax.broadcasted_iota(jnp.int32, (group, span), 1)

    def tile(index, _):
        here = pl.ds(pl.multiple_of(index * group, group), group)
        cols = cols_ref[here, :]
        ends = edge[pl.ds(pl.multiple_of(base + index * group, group), group), :]
        filtered = []
        for which in range(3):
            value = feat_ref[which, here, :].astype(F32)
            two_back = ends[:, 2 * which : 2 * which + 1]
            one_back = ends[:, 2 * which + 1 : 2 * which + 2]
            back = jnp.where(lane == 0, one_back, pltpu.roll(value, 1, 1))
            twice = jnp.where(lane == 0, two_back, jnp.where(lane == 1, one_back, pltpu.roll(value, 2, 1)))
            total = cols[:, 3 * which : 3 * which + 1] * value
            total = total + cols[:, 3 * which + 1 : 3 * which + 2] * back * keep[0]
            total = total + cols[:, 3 * which + 2 : 3 * which + 3] * twice * keep[1]
            rounded = total.astype(BF16)
            qkv_ref[which, here, :] = rounded
            filtered.append(rounded.astype(F32))
        made[0, here, :] = (filtered[1] * filtered[2]).astype(BF16)
        made[1, here, :] = (dout_ref[here, :].astype(F32) * filtered[0]).astype(BF16)
        return 0

    lax.fori_loop(0, rows // group, tile, 0, unroll=min(4, rows // group))
    for k in range(half):

        @pl.when(turn == k)
        def _(k=k):
            inner[k][:, pl.ds(pl.multiple_of(sub * rows, rows), rows), :] = made[...]

        @pl.when((turn == k) & (sub == side))
        def _(k=k):
            cross[k][...] = made[side]


def gate(layout, place, features, dout, halo, cols, keep):
    half, rows, span, channels = layout.half, layout.sub, layout.span, layout.channels
    block = sub_block(layout)
    wide = pl.BlockSpec((3, rows, span), lambda *a: (0, block(*a), 0))
    flat = pl.BlockSpec((rows, span), lambda *a: (block(*a), 0))
    columns = pl.BlockSpec((rows, 16), lambda *a: (block(*a), 0))
    shapes = [(2, layout.size, span)] * half + [(rows, span)] * half
    found = streamed(
        gate_body,
        layout,
        place,
        (features, dout, halo, cols, keep),
        [wide, flat, fixed(halo.shape), columns, fixed(keep.shape)],
        [jax.ShapeDtypeStruct(features.shape, BF16)] + [jax.ShapeDtypeStruct(s, BF16) for s in shapes],
        [wide] + [fixed(s) for s in shapes],
        [pltpu.VMEM((channels, 16), F32), pltpu.VMEM((2, rows, span), BF16)],
        (layout.parts,),
        estimate(30 * channels * span, 9 * channels * span * 2),
    )
    return found[0], found[1 : 1 + half], found[1 + half :]


def loop(count, body, init):
    if count <= 4:
        for k in range(count):
            init = body(k, init)
        return init
    return lax.fori_loop(0, count, body, init)


def add_product(total, f, x):
    return (total[0] + f[0] * x[0] - f[1] * x[1], total[1] + f[0] * x[1] + f[1] * x[0])


def add_conjugate(total, f, x):
    return (total[0] + f[0] * x[0] + f[1] * x[1], total[1] + f[0] * x[1] - f[1] * x[0])


def turned_sum(spectrum, neighbour, sign):
    half = spectrum[0].shape[1] // 2
    parts = []
    for lanes, flip in ((slice(0, half), sign), (slice(half, None), -sign)):
        n_re, n_im = neighbour[0][:, lanes], neighbour[1][:, lanes]
        s_re, s_im = spectrum[0][:, lanes], spectrum[1][:, lanes]
        parts.append((s_re - n_im, s_im + n_re) if flip > 0 else (s_re + n_im, s_im - n_re))
    return tuple(jnp.concatenate([p[k] for p in parts], axis=1) for k in range(2))


def forward(raw, spec, begin, target, rows, fhi_ref, flo_ref):
    value = raw[pl.ds(pl.multiple_of(begin, 16), rows), :]
    spec[pl.ds(pl.multiple_of(target, 16), rows), :] = dot(value, fhi_ref[...]) + dot(value, flo_ref[...])


def inverse(high, low, back, begin, rows, ihi_ref, ilo_ref):
    place = pl.ds(pl.multiple_of(begin, 16), rows)
    top = high[place, :]
    back[place, :] = dot(top, ihi_ref[...]) + dot(top, ilo_ref[...]) + dot(low[place, :], ihi_ref[...])


def spectrum_at(spec, begin, group, span):
    place = pl.ds(pl.multiple_of(begin, group), group)
    return spec[place, :span], spec[place, span:]


def store_split(high, low, begin, value, group, span):
    place = pl.ds(pl.multiple_of(begin, group), group)
    for lanes, part in ((slice(0, span), value[0]), (slice(span, 2 * span), value[1])):
        top = part.astype(BF16)
        high[place, lanes] = top
        low[place, lanes] = (part - top.astype(F32)).astype(BF16)


def own_body(layout, place_ref, cols_ref, fhi_ref, flo_ref, ihi_ref, ilo_ref, filt_ref, other_ref, *rest):
    parts, half, size, sub, span = layout.parts, layout.half, layout.size, layout.sub, layout.span
    filt_in, rest = rest[: parts - 1], rest[parts - 1 :]
    inner, returned, later = rest[:half], rest[half : 2 * half], rest[2 * half : 3 * half]
    raw, spec, high, low, back = rest[3 * half :]
    side, own = sides(place_ref, layout)
    rank, carried = place_ref[0], place_ref[1]
    kind_rows = half * size
    signals = parts * size

    def rows_at(begin, count):
        return pl.ds(pl.multiple_of(begin, sub), count)

    raw[rows_at(rank * size, size), :] = filt_ref[...]
    for step in range(1, parts):
        begin = jnp.bitwise_xor(rank, step) * size
        raw[rows_at(begin + carried * sub, sub), :] = filt_in[step - 1][...]
        raw[rows_at(begin + (1 - carried) * sub, sub), :] = other_ref[(step - 1) * sub : step * sub, :]
    for step in range(half):
        for kind in range(2):
            begin = signals + kind * kind_rows + jnp.bitwise_xor(own, step) * size
            raw[rows_at(begin, size), :] = inner[step][kind]

    def transform(index, _):
        kind, part = index // half, index % half
        begin = jnp.where(kind == 0, 0, signals + (kind - 1) * kind_rows) + part * size
        forward(raw, spec, begin, index * size, size, fhi_ref, flo_ref)
        return 0

    lax.fori_loop(0, 3 * half, transform, 0)
    group = 16
    zero = (jnp.zeros((group, span), F32),) * 2

    def products(index, _):
        def read(kind, k):
            return spectrum_at(spec, (kind * half + k) * size + index * group, group, span)

        def store(kind, k, value):
            store_split(high, low, (kind * half + k) * size + index * group, value, group, span)

        before = None
        for place in range(half):
            total = loop(place + 1, lambda k, t, p=place: add_product(t, read(0, k), read(1, p - k)), zero)
            store(0, place, total if before is None else turned_sum(total, before, 1))
            before = total
        before = None
        for place in range(half - 1, -1, -1):
            total = loop(half - place, lambda k, t, p=place: add_conjugate(t, read(0, k), read(2, p + k)), zero)
            store(1, place, total if before is None else turned_sum(total, before, -1))
            before = total
        return 0

    lax.fori_loop(0, size // group, products, 0)

    def restore(index, _):
        inverse(high, low, back, index * size, size, ihi_ref, ilo_ref)
        return 0

    lax.fori_loop(0, 2 * half, restore, 0)

    def result(kind, cls, part):
        begin = kind * kind_rows + part * size + cls * sub
        direct = raw[rows_at(signals + begin, sub), :].astype(F32)
        skip = cols_ref[rows_at(cls * sub, sub), 9:10]
        return back[rows_at(begin, sub), :] + skip * direct

    for step in range(half):
        part = jnp.bitwise_xor(own, step)
        returned[step][0] = result(side, 0, part).astype(BF16)
        returned[step][1] = result(side, 1, part).astype(BF16)
        returned[step][2] = result(1 - side, side, part).astype(BF16)
        later[step][...] = result(1 - side, 1 - side, part)


def own_half(layout, place, cols, tables, filters, other, filt, inner):
    half, size, sub, span, parts = layout.half, layout.size, layout.sub, layout.span, layout.parts
    own_class = lambda step, place_ref: (sides(place_ref, layout)[1], 0)
    shapes = [((3, sub, span), BF16)] * half + [((sub, span), F32)] * half
    rows = 3 * half * size
    found = streamed(
        own_body,
        layout,
        place,
        (cols, *tables, filters, other, *filt, *inner),
        [pl.BlockSpec((size, 16), own_class)]
        + [fixed(t.shape) for t in tables]
        + [pl.BlockSpec((size, span), own_class), fixed(other.shape)]
        + [fixed((sub, span))] * (parts - 1)
        + [fixed((2, size, span))] * half,
        [jax.ShapeDtypeStruct(*s) for s in shapes],
        [fixed(s[0]) for s in shapes],
        [
            pltpu.VMEM(((parts + 2 * half) * size, span), BF16),
            pltpu.VMEM((rows, 2 * span), F32),
            pltpu.VMEM((2 * half * size, 2 * span), BF16),
            pltpu.VMEM((2 * half * size, 2 * span), BF16),
            pltpu.VMEM((2 * half * size, span), F32),
        ],
        (1,),
        estimate(2 * rows * span * 2 * span * 4, 7 * half * size * span * 2),
    )
    return found[:half], found[half:]


def cross_body(arriving, layout, place_ref, fhi_ref, flo_ref, ihi_ref, ilo_ref, filt_ref, other_ref, *rest):
    parts, half, sub, span = layout.parts, layout.half, layout.sub, layout.span
    filt_in, rest = rest[: parts - 1], rest[parts - 1 :]
    signal, rest = rest[:half], rest[half:]
    partial, rest = (rest[:half], rest[half:]) if arriving else (None, rest)
    outs = rest[:half]
    raw, spec, high, low, back = rest[half:]
    side, own = sides(place_ref, layout)
    rank, carried = place_ref[0], place_ref[1]
    main = 1 - side
    block = parts * sub

    def rows_at(begin, count):
        return pl.ds(pl.multiple_of(begin, sub), count)

    raw[rows_at(rank * sub, sub), :] = filt_ref[...]
    for step in range(1, parts):
        place = rows_at(jnp.bitwise_xor(rank, step) * sub, sub)
        raw[place, :] = jnp.where(carried == main, filt_in[step - 1][...], other_ref[(step - 1) * sub : step * sub, :])
    for step in range(half):
        value = signal[step][...]
        raw[rows_at(block + jnp.bitwise_xor(own, step) * sub, sub), :] = value.reshape(sub, span)
    count = (parts + half) * sub
    chunk = math.gcd(count, 512)
    lax.fori_loop(
        0, count // chunk, lambda k, _: forward(raw, spec, k * chunk, k * chunk, chunk, fhi_ref, flo_ref) or 0, 0
    )
    group = 16
    zero = (jnp.zeros((group, span), F32),) * 2
    from_first = side == (1 if arriving else 0)

    def products(index, ahead):
        def filt(k):
            return spectrum_at(spec, k * sub + index * group, group, span)

        def sig(k):
            return spectrum_at(spec, block + k * sub + index * group, group, span)

        before = None
        if ahead:
            for place in range(half - 1, parts):
                total = loop(half, lambda k, t, p=place: add_product(t, filt(p - k), sig(k)), zero)
                if before is not None:
                    value = turned_sum(total, before, 1)
                    store_split(high, low, (place - half) * sub + index * group, value, group, span)
                before = total
        else:
            for place in range(half, -1, -1):
                total = loop(half, lambda k, t, p=place: add_conjugate(t, filt(half + k - p), sig(k)), zero)
                if before is not None:
                    value = turned_sum(total, before, -1)
                    store_split(high, low, place * sub + index * group, value, group, span)
                before = total
        return 0

    @pl.when(from_first)
    def _():
        lax.fori_loop(0, sub // group, lambda k, _: products(k, True), 0)

    @pl.when(jnp.logical_not(from_first))
    def _():
        lax.fori_loop(0, sub // group, lambda k, _: products(k, False), 0)

    inverse(high, low, back, 0, half * sub, ihi_ref, ilo_ref)
    for step in range(half):
        value = back[rows_at(jnp.bitwise_xor(own, step) * sub, sub), :]
        if arriving:
            value = value + partial[step][...]
        outs[step][...] = value.astype(BF16)


def cross_half(layout, place, tables, filters, other, filt, signal, partial):
    half, sub, span, parts = layout.half, layout.sub, layout.span, layout.parts
    arriving = partial is not None

    def main_class(step, place_ref):
        side, own = sides(place_ref, layout)
        return (own * 2 + 1 - side, 0)

    def main_signal(step, place_ref):
        side, own = sides(place_ref, layout)
        return (side, 1 - side, 0)

    signal_spec = fixed((sub, span)) if arriving else pl.BlockSpec((1, sub, span), main_signal)
    rows = (parts + half) * sub
    return streamed(
        functools.partial(cross_body, arriving),
        layout,
        place,
        (*tables, filters, other, *filt, *signal, *(partial or ())),
        [fixed(t.shape) for t in tables]
        + [pl.BlockSpec((sub, span), main_class), fixed(other.shape)]
        + [fixed((sub, span))] * (parts - 1)
        + [signal_spec] * half
        + [fixed((sub, span))] * (half if arriving else 0),
        [jax.ShapeDtypeStruct((sub, span), BF16)] * half,
        [fixed((sub, span))] * half,
        [
            pltpu.VMEM((rows, span), BF16),
            pltpu.VMEM((rows, 2 * span), F32),
            pltpu.VMEM((half * sub, 2 * span), BF16),
            pltpu.VMEM((half * sub, 2 * span), BF16),
            pltpu.VMEM((half * sub, span), F32),
        ],
        (1,),
        estimate(2 * rows * span * 2 * span * 3, 10 * half * sub * span * 2),
    )


def gather_results(layout, side, sub, returned, completed, crossed, which):
    plain = returned[sub].astype(F32)
    summed = (returned[2].astype(F32) + crossed[...].astype(F32)).astype(BF16).astype(F32)
    mixed = jnp.where(sub == side, summed, completed[...].astype(F32))
    return jnp.where(side == 0, plain, mixed), jnp.where(side == 0, mixed, plain)


def first_body(layout, place_ref, qkv_ref, dout_ref, *rest):
    half, sub = layout.half, layout.sub
    returned, completed, crossed = rest[:half], rest[half : 2 * half], rest[2 * half : 3 * half]
    out_ref, grads = rest[3 * half :]
    side, own = sides(place_ref, layout)
    for step in range(half):
        for part in range(2):
            begin = (jnp.bitwise_xor(own, step) * 2 + part) * sub
            place = pl.ds(pl.multiple_of(begin, sub), sub)
            y_out, dmixed = gather_results(
                layout, side, part, returned[step], completed[step], crossed[step], None
            )
            grads[0, place, :] = dout_ref[place, :].astype(F32) * y_out
            grads[1, place, :] = dmixed * qkv_ref[2, place, :].astype(F32)
            grads[2, place, :] = dmixed * qkv_ref[1, place, :].astype(F32)
    out_ref[...] = jnp.zeros(out_ref.shape, F32)
    for which in range(3):
        out_ref[2 * which : 2 * which + 2, :] = grads[which].T[0:2, :]


def first_grads(layout, place, qkv, dout, returned, completed, crossed):
    half, sub, channels = layout.half, layout.sub, layout.channels
    return streamed(
        first_body,
        layout,
        place,
        (qkv, dout, *returned, *completed, *crossed),
        [fixed((3, channels, 128)), fixed((channels, 128))]
        + [fixed((3, sub, 128))] * half
        + [fixed((sub, 128))] * (2 * half),
        jax.ShapeDtypeStruct((8, channels), F32),
        fixed((8, channels)),
        [pltpu.VMEM((3, channels, 128), F32)],
        (1,),
        estimate(0, 3 * channels * 128 * 2),
    )


def final_body(layout, place_ref, qkv_ref, dout_ref, cols_ref, ahead_ref, keep_ref, *rest):
    half, rows, span = layout.half, layout.sub, layout.span
    returned, completed, crossed = rest[:half], rest[half : 2 * half], rest[2 * half : 3 * half]
    out_ref, dfeat_ref, edge, moved = rest[3 * half :]
    side, own = sides(place_ref, layout)
    step = pl.program_id(0)
    turn, sub = step // 2, step % 2
    base = sub_block(layout)(step, place_ref) * rows

    @pl.when(step == 0)
    def _():
        edge[...] = ahead_ref[...].T

    for k in range(half):

        @pl.when(turn == k)
        def _(k=k):
            moved[side] = returned[k][sub]

        @pl.when((turn == k) & (sub == side))
        def _(k=k):
            moved[1 - side] = (returned[k][2].astype(F32) + crossed[k][...].astype(F32)).astype(BF16)

        @pl.when((turn == k) & (sub != side))
        def _(k=k):
            moved[1 - side] = completed[k][...]

    group = min(32, rows)
    lane = lax.broadcasted_iota(jnp.int32, (group, span), 1)
    keep = keep_ref[2:3, :], keep_ref[3:4, :]

    def tile(index, _):
        here = pl.ds(pl.multiple_of(index * group, group), group)
        ends = edge[pl.ds(pl.multiple_of(base + index * group, group), group), :]
        cols = cols_ref[here, :]
        y_out = moved[0, here, :].astype(F32)
        dmixed = moved[1, here, :].astype(F32)
        out_ref[here, :] = (qkv_ref[0, here, :].astype(F32) * y_out).astype(BF16)
        grads = (
            dout_ref[here, :].astype(F32) * y_out,
            dmixed * qkv_ref[2, here, :].astype(F32),
            dmixed * qkv_ref[1, here, :].astype(F32),
        )
        for which in range(3):
            value = grads[which]
            first = ends[:, 2 * which : 2 * which + 1]
            second = ends[:, 2 * which + 1 : 2 * which + 2]
            next_one = jnp.where(lane == span - 1, first, pltpu.roll(value, span - 1, 1))
            next_two = jnp.where(
                lane == span - 1, second, jnp.where(lane == span - 2, first, pltpu.roll(value, span - 2, 1))
            )
            total = cols[:, 3 * which : 3 * which + 1] * value
            total = total + cols[:, 3 * which + 1 : 3 * which + 2] * next_one * keep[0]
            total = total + cols[:, 3 * which + 2 : 3 * which + 3] * next_two * keep[1]
            dfeat_ref[which, here, :] = total.astype(BF16)
        return 0

    lax.fori_loop(0, rows // group, tile, 0, unroll=min(4, rows // group))


def final(layout, place, qkv, dout, cols, ahead, keep, returned, completed, crossed):
    half, rows, span, channels = layout.half, layout.sub, layout.span, layout.channels
    block = sub_block(layout)
    wide = pl.BlockSpec((3, rows, span), lambda *a: (0, block(*a), 0))
    flat = pl.BlockSpec((rows, span), lambda *a: (block(*a), 0))
    columns = pl.BlockSpec((rows, 16), lambda *a: (block(*a), 0))
    return streamed(
        final_body,
        layout,
        place,
        (qkv, dout, cols, ahead, keep, *returned, *completed, *crossed),
        [wide, flat, columns, fixed(ahead.shape), fixed(keep.shape)]
        + [fixed((3, rows, span))] * half
        + [fixed((rows, span))] * (2 * half),
        [jax.ShapeDtypeStruct((channels, span), BF16), jax.ShapeDtypeStruct((3, channels, span), BF16)],
        [flat, wide],
        [pltpu.VMEM((channels, 8), F32), pltpu.VMEM((2, rows, span), BF16)],
        (layout.parts,),
        estimate(40 * channels * span, 10 * channels * span * 2),
    )


def swap(value, step, parts, axis="seq"):
    return lax.ppermute(value, axis, [(source, source ^ step) for source in range(parts)])


def around(value, steps, parts):
    return lax.ppermute(value, "seq", [(source, (source + steps) % parts) for source in range(parts)])


def local(features, dout, filters, taps, skip, lengths):
    parts = lax.axis_size("seq")
    _, channels, span = features.shape
    layout = Layout(parts, channels, span)
    half = layout.half
    place = jnp.stack([lax.axis_index("seq"), lax.axis_index("groups")]).astype(jnp.int32)
    tables = [jnp.asarray(t) for t in block_tables(span)]

    halo, cols, filt_out = pack(layout, place, features, filters, taps, skip)
    halo = around(halo, 1, parts)
    filt = [swap(filt_out[step % half], step, parts) for step in range(1, parts)]
    other = swap(jnp.concatenate(filt, axis=0), 1, 2, "groups")
    keep = masks(place, lengths, parts, span)
    qkv, inner, cross = gate(layout, place, features, dout, halo, cols, keep)
    inner = [inner[0]] + [swap(inner[step], step, parts) for step in range(1, half)]
    cross = [swap(cross[step], step + half, parts) for step in range(half)]

    sent = cross_half(layout, place, tables, filters, other, filt, inner, None)
    crossed = [swap(sent[step], step + half, parts) for step in range(half)]
    returned, later = own_half(layout, place, cols, tables, filters, other, filt, inner)
    returned = [returned[0]] + [swap(returned[step], step, parts) for step in range(1, half)]
    completed = cross_half(layout, place, tables, filters, other, filt, cross, later)
    completed = [completed[0]] + [swap(completed[step], step, parts) for step in range(1, half)]

    ahead = around(first_grads(layout, place, qkv, dout, returned, completed, crossed), -1, parts)
    return tuple(final(layout, place, qkv, dout, cols, ahead, keep, returned, completed, crossed))


def solution(mesh):
    in_specs = (
        P(None, ("chan", "sub"), ("groups", "seq")),
        P(("chan", "sub"), ("groups", "seq")),
        P(("chan", "sub"), "seq"),
        P(None, None, ("chan", "sub")),
        P(("chan", "sub")),
        P("groups"),
    )
    out_specs = (P(("chan", "sub"), ("groups", "seq")), P(None, ("chan", "sub"), ("groups", "seq")))
    return jax.shard_map(local, mesh=mesh, in_specs=in_specs, out_specs=out_specs, check_vma=False)
```

```python
import functools
import math

import jax
import jax.numpy as jnp
import numpy as np
from jax import lax
from jax.experimental import pallas as pl
from jax.experimental.pallas import tpu as pltpu
from jax.sharding import PartitionSpec as P

BF16 = jnp.bfloat16
F32 = jnp.float32
VMEM_LIMIT = 24 * 1024 * 1024
SCALARS = pl.BlockSpec(memory_space=pltpu.SMEM)
IN_HBM = pl.BlockSpec(memory_space=pltpu.HBM)
ANYWHERE = pl.BlockSpec(memory_space=pl.ANY)


def split_bf16(table):
    high = table.astype(np.float32).astype(BF16)
    low = (table - high.astype(np.float64)).astype(np.float32).astype(BF16)
    return high, low


def block_tables(span):
    freq = np.concatenate([np.arange(0, span, 2), np.arange(1, span, 2)])
    angle = np.pi * (2 * freq[None, :] + 1) * np.arange(span)[:, None] / (2 * span)
    forward = np.concatenate([np.cos(angle), -np.sin(angle)], axis=1)
    inverse = np.concatenate([np.cos(angle), -np.sin(angle)], axis=1).T / span
    return np.concatenate(split_bf16(forward), axis=0), split_bf16(inverse)[0]


def dot(a, b):
    return jnp.dot(a, b, preferred_element_type=F32)


def estimate(flops, moved):
    return pl.CostEstimate(flops=int(flops), bytes_accessed=int(moved), transcendentals=0)


def offsets_row(lengths_ref, first, span, ahead):
    position = lax.broadcasted_iota(jnp.int32, (8, span), 1) + (first + ahead)

    def step(genome, carry):
        end, start = carry
        end = end + lengths_ref[genome]
        return end, jnp.where(position >= end, end, start)

    begin = (jnp.int32(0), jnp.zeros((8, span), jnp.int32))
    _, start = lax.fori_loop(0, lengths_ref.shape[0], step, begin)
    return position, position - start


class Layout:
    def __init__(self, parts, channels, span):
        self.parts, self.channels, self.span = parts, channels, span
        self.half = parts // 2
        self.size = channels // self.half
        self.sub = self.size // 2


def where_am_i(place_ref, layout):
    rank, group = place_ref[0], place_ref[1]
    side = rank // layout.half
    return side, rank % layout.half, jnp.where(side == 0, 1 - group, group)


def channel_block(place_ref, layout, turn, other):
    _, own, main = where_am_i(place_ref, layout)
    return jnp.bitwise_xor(own, turn) * 2 + jnp.bitwise_xor(main, other)


def fixed(shape):
    return pl.BlockSpec(shape, lambda *args: (0,) * len(shape))


def streamed(body, layout, place, operands, in_specs, outs, out_specs, scratch, grid, cost, aliases=None):
    return pl.pallas_call(
        functools.partial(body, layout),
        out_shape=outs,
        grid_spec=pltpu.PrefetchScalarGridSpec(
            num_scalar_prefetch=1,
            grid=grid,
            in_specs=in_specs,
            out_specs=out_specs,
            scratch_shapes=scratch,
        ),
        input_output_aliases=aliases or {},
        compiler_params=pltpu.CompilerParams(vmem_limit_bytes=VMEM_LIMIT),
        cost_estimate=cost,
    )(place, *operands)


def pack_body(layout, place_ref, feat_ref, filt_ref, halo_ref, *rest):
    filt_out, (tail, turned, sems) = rest[: layout.parts - 1], rest[layout.parts - 1 :]
    span, half, sub = layout.span, layout.half, layout.sub
    copies = [pltpu.make_async_copy(feat_ref.at[:, :, span - 128 : span], tail, sems.at[0])]
    for step in range(1, layout.parts):
        begin = channel_block(place_ref, layout, step % half, step // half) * sub
        source = filt_ref.at[pl.ds(pl.multiple_of(begin, sub), sub), :]
        copies.append(pltpu.make_async_copy(source, filt_out[step - 1], sems.at[step]))
    for copy in copies:
        copy.start()
    turned[...] = jnp.zeros(turned.shape, F32)
    copies[0].wait()
    for which in range(3):
        turned[2 * which : 2 * which + 2, :] = tail[which].astype(F32).T[-2:, :]
    halo_ref[...] = turned[...].astype(BF16)
    for copy in copies[1:]:
        copy.wait()


def pack(layout, place, features, filters):
    channels, span, parts = layout.channels, layout.span, layout.parts
    shapes = [(16, channels)] + [(layout.sub, span)] * (parts - 1)
    found = streamed(
        pack_body,
        layout,
        place,
        (features, filters),
        [IN_HBM, IN_HBM],
        [jax.ShapeDtypeStruct(s, BF16) for s in shapes],
        [fixed(s) for s in shapes],
        [
            pltpu.VMEM((3, channels, 128), BF16),
            pltpu.VMEM((16, channels), F32),
            pltpu.SemaphoreType.DMA((parts,)),
        ],
        (1,),
        estimate(0, 3 * channels * span),
    )
    return found[0], found[1:]


def small_body(layout, place_ref, lengths_ref, taps_ref, skip_ref, keep_ref, cols_ref, turned):
    span = layout.span
    first = place_ref[0] * span
    keep_ref[...] = jnp.zeros(keep_ref.shape, F32)
    _, offset = offsets_row(lengths_ref, first, span, 0)
    for j in (1, 2):
        keep_ref[j - 1 : j, :] = (offset[0:1, :] >= j).astype(F32)
        position, later = offsets_row(lengths_ref, first, span, j)
        inside = (position < layout.parts * span) & (later >= j)
        keep_ref[1 + j : 2 + j, :] = inside[0:1, :].astype(F32)
    turned[...] = jnp.zeros(turned.shape, F32)
    for which in range(3):
        turned[3 * which : 3 * which + 3, :] = taps_ref[which]
    turned[9:10, :] = skip_ref[...]
    cols_ref[...] = turned[...].T


def small(layout, place, lengths, taps, skip):
    channels = layout.channels
    shapes = [(8, layout.span), (channels, 16)]
    return streamed(
        small_body,
        layout,
        place,
        (lengths, taps, skip.reshape(1, channels)),
        [SCALARS, fixed(taps.shape), fixed((1, channels))],
        [jax.ShapeDtypeStruct(s, F32) for s in shapes],
        [fixed(s) for s in shapes],
        [pltpu.VMEM((16, channels), F32)],
        (1,),
        estimate(0, 100 * channels),
    )


def gate_body(other, layout, place_ref, feat_ref, dout_ref, halo_ref, cols_ref, keep_ref, *rest):
    half, rows, span = layout.half, layout.sub, layout.span
    if other:
        main_rest, rest = rest[:half], rest[half + 1 :]
    qkv_ref, rest = rest[0], rest[1:]
    firsts, seconds = rest[:half], rest[half : 2 * half]
    edge, made = rest[2 * half :]
    side, _, _ = where_am_i(place_ref, layout)
    turn = pl.program_id(0)
    base = channel_block(place_ref, layout, turn, other) * rows
    group = min(128, rows)

    @pl.when(turn == 0)
    def _():
        edge[...] = halo_ref[...].astype(F32).T

    keep = keep_ref[0:1, :], keep_ref[1:2, :]
    lane = lax.broadcasted_iota(jnp.int32, (group, span), 1)

    def tile(index, _):
        here = pl.ds(pl.multiple_of(index * group, group), group)
        cols = cols_ref[here, :]
        ends = edge[pl.ds(pl.multiple_of(base + index * group, group), group), :]
        filtered = []
        for which in range(3):
            value = feat_ref[which, here, :].astype(F32)
            two_back = ends[:, 2 * which : 2 * which + 1]
            one_back = ends[:, 2 * which + 1 : 2 * which + 2]
            back = jnp.where(lane == 0, one_back, pltpu.roll(value, 1, 1))
            twice = jnp.where(lane == 0, two_back, jnp.where(lane == 1, one_back, pltpu.roll(value, 2, 1)))
            total = cols[:, 3 * which : 3 * which + 1] * value
            total = total + cols[:, 3 * which + 1 : 3 * which + 2] * back * keep[0]
            total = total + cols[:, 3 * which + 2 : 3 * which + 3] * twice * keep[1]
            rounded = total.astype(BF16)
            qkv_ref[which, here, :] = rounded
            filtered.append(rounded.astype(F32))
        made[0, here, :] = (filtered[1] * filtered[2]).astype(BF16)
        made[1, here, :] = (dout_ref[here, :].astype(F32) * filtered[0]).astype(BF16)
        return 0

    lax.fori_loop(0, rows // group, tile, 0)
    for k in range(half):

        @pl.when(turn == k)
        def _(k=k):
            firsts[k][...] = made[side]
            if other:
                seconds[k][0] = main_rest[k][...]
                seconds[k][1] = made[side]
                seconds[k][2] = made[1 - side]
            else:
                seconds[k][...] = made[1 - side]


def gate(other, layout, place, features, dout, halo, cols, keep, qkv, main_rest):
    half, rows, span, channels = layout.half, layout.sub, layout.span, layout.channels

    def block(turn, place_ref):
        return channel_block(place_ref, layout, turn, other)

    wide = pl.BlockSpec((3, rows, span), lambda *a: (0, block(*a), 0))
    flat = pl.BlockSpec((rows, span), lambda *a: (block(*a), 0))
    columns = pl.BlockSpec((rows, 16), lambda *a: (block(*a), 0))
    shapes = [(rows, span)] * half + [(3, rows, span) if other else (rows, span)] * half
    operands = [features, dout, halo, cols, keep]
    in_specs = [wide, flat, fixed(halo.shape), columns, fixed(keep.shape)]
    if other:
        operands += [*main_rest, qkv]
        in_specs += [fixed((rows, span))] * half + [ANYWHERE]
    found = streamed(
        functools.partial(gate_body, other),
        layout,
        place,
        operands,
        in_specs,
        [jax.ShapeDtypeStruct(features.shape, BF16)] + [jax.ShapeDtypeStruct(s, BF16) for s in shapes],
        [wide] + [fixed(s) for s in shapes],
        [pltpu.VMEM((channels, 16), F32), pltpu.VMEM((2, rows, span), BF16)],
        (half,),
        estimate(15 * channels * span, 9 * channels * span),
        {len(operands): 0} if other else None,
    )
    return found[0], found[1 : 1 + half], found[1 + half :]


def loop(count, body, init):
    if count <= 4:
        for k in range(count):
            init = body(k, init)
        return init
    return lax.fori_loop(0, count, body, init)


def add_product(total, f, x):
    return (total[0] + f[0] * x[0] - f[1] * x[1], total[1] + f[0] * x[1] + f[1] * x[0])


def add_conjugate(total, f, x):
    return (total[0] + f[0] * x[0] + f[1] * x[1], total[1] + f[0] * x[1] - f[1] * x[0])


def turned_sum(spectrum, neighbour, sign):
    half = spectrum[0].shape[1] // 2
    parts = []
    for lanes, flip in ((slice(0, half), sign), (slice(half, None), -sign)):
        n_re, n_im = neighbour[0][:, lanes], neighbour[1][:, lanes]
        s_re, s_im = spectrum[0][:, lanes], spectrum[1][:, lanes]
        parts.append((s_re - n_im, s_im + n_re) if flip > 0 else (s_re + n_im, s_im - n_re))
    return tuple(jnp.concatenate([p[k] for p in parts], axis=1) for k in range(2))


def forward(raw, spec, begin, target, rows, table_ref):
    value = raw[pl.ds(pl.multiple_of(begin, 16), rows), :]
    spec[pl.ds(pl.multiple_of(target, 16), rows), :] = dot(jnp.concatenate([value, value], axis=1), table_ref[...])


def spectrum_at(spec, begin, group, span):
    place = pl.ds(pl.multiple_of(begin, group), group)
    return spec[place, :span], spec[place, span:]


def store_spectrum(ready, begin, value, group, span):
    place = pl.ds(pl.multiple_of(begin, group), group)
    ready[place, :span] = value[0].astype(BF16)
    ready[place, span:] = value[1].astype(BF16)


def own_body(layout, place_ref, cols_ref, forward_ref, inverse_ref, filt_ref, other_ref, *rest):
    parts, half, size, sub, span = layout.parts, layout.half, layout.size, layout.sub, layout.span
    filt_in, rest = rest[: parts - 1], rest[parts - 1 :]
    firsts, seconds, rest = rest[:half], rest[half : 2 * half], rest[2 * half + 1 :]
    returned, later = rest[:half], rest[half : 2 * half]
    raw, spec, ready, back = rest[2 * half :]
    side, own, main = where_am_i(place_ref, layout)
    rank = place_ref[0]
    kind_rows = half * size
    signals = parts * size

    def rows_at(begin, count):
        return pl.ds(pl.multiple_of(begin, sub), count)

    for cls in range(2):
        source = rows_at(jnp.bitwise_xor(main, cls) * sub, sub)
        raw[rows_at(rank * size + cls * sub, sub), :] = filt_ref[source, :]
    for step in range(1, parts):
        begin = jnp.bitwise_xor(rank, step) * size
        raw[rows_at(begin, sub), :] = filt_in[step - 1][...]
        raw[rows_at(begin + sub, sub), :] = other_ref[(step - 1) * sub : step * sub, :]
    for step in range(half):
        block = signals + jnp.bitwise_xor(own, step) * size
        raw[rows_at(block + side * kind_rows, sub), :] = firsts[step][...]
        raw[rows_at(block + (1 - side) * kind_rows, sub), :] = seconds[step][0]
        raw[rows_at(block + side * kind_rows + sub, sub), :] = seconds[step][1]
        raw[rows_at(block + (1 - side) * kind_rows + sub, sub), :] = seconds[step][2]

    def transform(index, _):
        kind, part = index // half, index % half
        begin = jnp.where(kind == 0, 0, signals + (kind - 1) * kind_rows) + part * size
        forward(raw, spec, begin, index * size, size, forward_ref)
        return 0

    lax.fori_loop(0, 3 * half, transform, 0)
    group = 16
    zero = (jnp.zeros((group, span), F32),) * 2

    def products(index, _):
        def read(kind, k):
            return spectrum_at(spec, (kind * half + k) * size + index * group, group, span)

        def store(kind, k, value):
            store_spectrum(ready, (kind * half + k) * size + index * group, value, group, span)

        before = None
        for place in range(half):
            total = loop(place + 1, lambda k, t, p=place: add_product(t, read(0, k), read(1, p - k)), zero)
            store(0, place, total if before is None else turned_sum(total, before, 1))
            before = total
        before = None
        for place in range(half - 1, -1, -1):
            total = loop(half - place, lambda k, t, p=place: add_conjugate(t, read(0, k), read(2, p + k)), zero)
            store(1, place, total if before is None else turned_sum(total, before, -1))
            before = total
        return 0

    lax.fori_loop(0, size // group, products, 0)

    def restore(index, _):
        place = rows_at(index * size, size)
        back[place, :] = dot(ready[place, :], inverse_ref[...])
        return 0

    lax.fori_loop(0, 2 * half, restore, 0)

    def result(kind, cls, part):
        begin = kind * kind_rows + part * size + cls * sub
        direct = raw[rows_at(signals + begin, sub), :].astype(F32)
        skip = cols_ref[rows_at(jnp.bitwise_xor(main, cls) * sub, sub), 9:10]
        return back[rows_at(begin, sub), :] + skip * direct

    for step in range(half):
        part = jnp.bitwise_xor(own, step)
        returned[step][0] = result(side, 0, part).astype(BF16)
        returned[step][1] = result(side, 1, part).astype(BF16)
        returned[step][2] = result(1 - side, 1, part).astype(BF16)
        later[step][...] = result(1 - side, 0, part)


def own_half(layout, place, cols, tables, filters, other, filt, firsts, seconds, after):
    half, size, sub, span, parts = layout.half, layout.size, layout.sub, layout.span, layout.parts
    own_class = lambda step, place_ref: (where_am_i(place_ref, layout)[1], 0)
    shapes = [((3, sub, span), BF16)] * half + [((sub, span), F32)] * half
    rows = 3 * half * size
    found = streamed(
        own_body,
        layout,
        place,
        (cols, *tables, filters, other, *filt, *firsts, *seconds, after),
        [pl.BlockSpec((size, 16), own_class)]
        + [fixed(t.shape) for t in tables]
        + [pl.BlockSpec((size, span), own_class), fixed(other.shape)]
        + [fixed((sub, span))] * (parts - 1 + half)
        + [fixed((3, sub, span))] * half
        + [ANYWHERE],
        [jax.ShapeDtypeStruct(*s) for s in shapes],
        [fixed(s[0]) for s in shapes],
        [
            pltpu.VMEM(((parts + 2 * half) * size, span), BF16),
            pltpu.VMEM((rows, 2 * span), F32),
            pltpu.VMEM((2 * half * size, 2 * span), BF16),
            pltpu.VMEM((2 * half * size, span), F32),
        ],
        (1,),
        estimate(2 * rows * span * 2 * span * 3, 7 * half * size * span * 2),
    )
    return found[:half], found[half:]


def cross_body(arriving, layout, place_ref, forward_ref, inverse_ref, filt_ref, *rest):
    parts, half, sub, span = layout.parts, layout.half, layout.sub, layout.span
    filt_in, rest = rest[: parts - 1], rest[parts - 1 :]
    signal, rest = rest[:half], rest[half:]
    partial, rest = (rest[:half], rest[half:]) if arriving else (None, rest)
    outs = rest[:half]
    raw, spec, ready, back = rest[half:]
    side, own, _ = where_am_i(place_ref, layout)
    rank = place_ref[0]
    block = parts * sub

    def rows_at(begin, count):
        return pl.ds(pl.multiple_of(begin, sub), count)

    raw[rows_at(rank * sub, sub), :] = filt_ref[...]
    for step in range(1, parts):
        raw[rows_at(jnp.bitwise_xor(rank, step) * sub, sub), :] = filt_in[step - 1][...]
    for step in range(half):
        raw[rows_at(block + jnp.bitwise_xor(own, step) * sub, sub), :] = signal[step][...]
    count = (parts + half) * sub
    chunk = math.gcd(count, 512)

    def transform(index, _):
        forward(raw, spec, index * chunk, index * chunk, chunk, forward_ref)
        return 0

    lax.fori_loop(0, count // chunk, transform, 0)
    group = 16
    zero = (jnp.zeros((group, span), F32),) * 2
    from_first = side == (1 if arriving else 0)

    def products(index, ahead):
        def filt(k):
            return spectrum_at(spec, k * sub + index * group, group, span)

        def sig(k):
            return spectrum_at(spec, block + k * sub + index * group, group, span)

        before = None
        if ahead:
            for place in range(half - 1, parts):
                total = loop(half, lambda k, t, p=place: add_product(t, filt(p - k), sig(k)), zero)
                if before is not None:
                    value = turned_sum(total, before, 1)
                    store_spectrum(ready, (place - half) * sub + index * group, value, group, span)
                before = total
        else:
            for place in range(half, -1, -1):
                total = loop(half, lambda k, t, p=place: add_conjugate(t, filt(half + k - p), sig(k)), zero)
                if before is not None:
                    value = turned_sum(total, before, -1)
                    store_spectrum(ready, place * sub + index * group, value, group, span)
                before = total
        return 0

    @pl.when(from_first)
    def _():
        lax.fori_loop(0, sub // group, lambda k, _: products(k, True), 0)

    @pl.when(jnp.logical_not(from_first))
    def _():
        lax.fori_loop(0, sub // group, lambda k, _: products(k, False), 0)

    back[...] = dot(ready[...], inverse_ref[...])
    for step in range(half):
        value = back[rows_at(jnp.bitwise_xor(own, step) * sub, sub), :]
        if arriving:
            value = value + partial[step][...]
        outs[step][...] = value.astype(BF16)


def cross_half(layout, place, tables, filters, filt, signal, partial):
    half, sub, span, parts = layout.half, layout.sub, layout.span, layout.parts
    arriving = partial is not None
    rows = (parts + half) * sub
    main_class = pl.BlockSpec((sub, span), lambda step, place_ref: (channel_block(place_ref, layout, 0, 0), 0))
    return streamed(
        functools.partial(cross_body, arriving),
        layout,
        place,
        (*tables, filters, *filt, *signal, *(partial or ())),
        [fixed(t.shape) for t in tables]
        + [main_class]
        + [fixed((sub, span))] * (parts - 1 + half + (half if arriving else 0)),
        [jax.ShapeDtypeStruct((sub, span), BF16)] * half,
        [fixed((sub, span))] * half,
        [
            pltpu.VMEM((rows, span), BF16),
            pltpu.VMEM((rows, 2 * span), F32),
            pltpu.VMEM((half * sub, 2 * span), BF16),
            pltpu.VMEM((half * sub, span), F32),
        ],
        (1,),
        estimate(2 * rows * span * 2 * span * 3, 10 * half * sub * span * 2),
    )


def first_body(layout, place_ref, qkv_ref, dout_ref, *rest):
    half, sub = layout.half, layout.sub
    returned, completed, crossed = rest[:half], rest[half : 2 * half], rest[2 * half : 3 * half]
    out_ref, grads = rest[3 * half :]
    side, _, _ = where_am_i(place_ref, layout)
    for turn in range(half):
        for other in range(2):
            begin = channel_block(place_ref, layout, turn, other) * sub
            place = pl.ds(pl.multiple_of(begin, sub), sub)
            plain = returned[turn][other].astype(F32)
            if other:
                mixed = returned[turn][2].astype(F32) + crossed[turn][...].astype(F32)
                mixed = mixed.astype(BF16).astype(F32)
            else:
                mixed = completed[turn][...].astype(F32)
            y_out = jnp.where(side == 0, plain, mixed)
            dmixed = jnp.where(side == 0, mixed, plain)
            grads[0, place, :] = dout_ref[place, :].astype(F32) * y_out
            grads[1, place, :] = dmixed * qkv_ref[2, place, :].astype(F32)
            grads[2, place, :] = dmixed * qkv_ref[1, place, :].astype(F32)
    out_ref[...] = jnp.zeros(out_ref.shape, F32)
    for which in range(3):
        out_ref[2 * which : 2 * which + 2, :] = grads[which].T[0:2, :]


def first_grads(layout, place, qkv, dout, returned, completed, crossed):
    half, sub, channels = layout.half, layout.sub, layout.channels
    return streamed(
        first_body,
        layout,
        place,
        (qkv, dout, *returned, *completed, *crossed),
        [fixed((3, channels, 128)), fixed((channels, 128))]
        + [fixed((3, sub, 128))] * half
        + [fixed((sub, 128))] * (2 * half),
        jax.ShapeDtypeStruct((8, channels), F32),
        fixed((8, channels)),
        [pltpu.VMEM((3, channels, 128), F32)],
        (1,),
        estimate(0, 3 * channels * 128 * 2),
    )


def final_body(last, layout, place_ref, qkv_ref, dout_ref, cols_ref, keep_ref, *rest):
    half, rows, span = layout.half, layout.sub, layout.span
    returned, completed, crossed = rest[:half], rest[half : 2 * half], rest[2 * half : 3 * half]
    rest = rest[3 * half :]
    ahead_ref, rest = (rest[0], rest[3:]) if last else (None, rest)
    out_ref, dfeat_ref, edge, moved = rest
    width = 128 if last else span
    written = 128 if last else span - 128
    begin = span - 128 if last else 0
    side, _, _ = where_am_i(place_ref, layout)
    turn, other = pl.program_id(0) // 2, pl.program_id(0) % 2
    base = channel_block(place_ref, layout, turn, other) * rows

    if last:

        @pl.when(pl.program_id(0) == 0)
        def _():
            edge[...] = ahead_ref[...].T

    for k in range(half):

        @pl.when(turn == k)
        def _(k=k):
            moved[side] = returned[k][other]

        @pl.when((turn == k) & (other == 1))
        def _(k=k):
            moved[1 - side] = (returned[k][2].astype(F32) + crossed[k][...].astype(F32)).astype(BF16)

        @pl.when((turn == k) & (other == 0))
        def _(k=k):
            moved[1 - side] = completed[k][...]

    group = min(128, rows)
    lane = lax.broadcasted_iota(jnp.int32, (group, width), 1)
    keep = [keep_ref[j : j + 1, begin : begin + written] for j in (2, 3)]

    def tile(index, _):
        here = pl.ds(pl.multiple_of(index * group, group), group)
        cols = cols_ref[here, :]
        y_out = moved[0, here, :].astype(F32)
        dmixed = moved[1, here, :].astype(F32)
        q_out = qkv_ref[0, here, :].astype(F32) * y_out
        out_ref[here, :] = q_out[:, :written].astype(BF16)
        grads = (
            dout_ref[here, :].astype(F32) * y_out,
            dmixed * qkv_ref[2, here, :].astype(F32),
            dmixed * qkv_ref[1, here, :].astype(F32),
        )
        for which in range(3):
            value = grads[which]
            next_one = pltpu.roll(value, width - 1, 1)
            next_two = pltpu.roll(value, width - 2, 1)
            if last:
                ends = edge[pl.ds(pl.multiple_of(base + index * group, group), group), :]
                first = ends[:, 2 * which : 2 * which + 1]
                second = ends[:, 2 * which + 1 : 2 * which + 2]
                next_one = jnp.where(lane == width - 1, first, next_one)
                next_two = jnp.where(lane == width - 1, second, jnp.where(lane == width - 2, first, next_two))
            total = cols[:, 3 * which : 3 * which + 1] * value[:, :written]
            total = total + cols[:, 3 * which + 1 : 3 * which + 2] * next_one[:, :written] * keep[0]
            total = total + cols[:, 3 * which + 2 : 3 * which + 3] * next_two[:, :written] * keep[1]
            dfeat_ref[which, here, :] = total.astype(BF16)
        return 0

    lax.fori_loop(0, rows // group, tile, 0)


def final(layout, place, qkv, dout, cols, keep, returned, completed, crossed, ahead, earlier):
    half, rows, span, channels = layout.half, layout.sub, layout.span, layout.channels
    last = ahead is not None
    width = 128 if last else span
    written = 128 if last else span - 128
    lanes = span // 128 - 1 if last else 0

    def block(step, place_ref):
        return channel_block(place_ref, layout, step // 2, step % 2)

    def wide(size, index):
        return pl.BlockSpec((3, rows, size), lambda *a: (0, block(*a), index))

    def flat(size, index):
        return pl.BlockSpec((rows, size), lambda *a: (block(*a), index))

    def held(shape):
        return pl.BlockSpec(shape, lambda *a: (0,) * (len(shape) - 1) + (lanes,))

    operands = [qkv, dout, cols, keep, *returned, *completed, *crossed]
    in_specs = (
        [wide(width, lanes), flat(width, lanes), flat(16, 0), fixed(keep.shape)]
        + [held((3, rows, width))] * half
        + [held((rows, width))] * (2 * half)
    )
    aliases = {}
    if last:
        operands += [ahead, *earlier]
        in_specs += [fixed(ahead.shape), ANYWHERE, ANYWHERE]
        aliases = {len(operands) - 1: 0, len(operands): 1}
    return streamed(
        functools.partial(final_body, last),
        layout,
        place,
        operands,
        in_specs,
        [jax.ShapeDtypeStruct((channels, span), BF16), jax.ShapeDtypeStruct((3, channels, span), BF16)],
        [flat(written, lanes), wide(written, lanes)],
        [pltpu.VMEM((channels, 8), F32), pltpu.VMEM((2, rows, width), BF16)],
        (layout.parts,),
        estimate(20 * channels * span, 10 * channels * span),
        aliases,
    )


def swap(value, step, parts, axis="seq"):
    return lax.ppermute(value, axis, [(source, source ^ step) for source in range(parts)])


def around(value, steps, parts):
    return lax.ppermute(value, "seq", [(source, (source + steps) % parts) for source in range(parts)])


def local(features, dout, filters, taps, skip, lengths):
    parts = lax.axis_size("seq")
    _, channels, span = features.shape
    layout = Layout(parts, channels, span)
    half = layout.half
    place = jnp.stack([lax.axis_index("seq"), lax.axis_index("groups")]).astype(jnp.int32)
    tables = [jnp.asarray(t) for t in block_tables(span)]

    halo, filt = pack(layout, place, features, filters)
    halo = around(halo, 1, parts)
    filt = [swap(filt[step - 1], step, parts) for step in range(1, parts)]
    other = swap(jnp.concatenate(filt, axis=0), 1, 2, "groups")
    keep, cols = small(layout, place, lengths, taps, skip)
    qkv, firsts, main_rest = gate(0, layout, place, features, dout, halo, cols, keep, None, None)
    firsts = [firsts[0]] + [swap(firsts[step], step, parts) for step in range(1, half)]
    qkv, cross, seconds = gate(1, layout, place, features, dout, halo, cols, keep, qkv, main_rest)
    seconds = [seconds[0]] + [swap(seconds[step], step, parts) for step in range(1, half)]
    cross = [swap(cross[step], step + half, parts) for step in range(half)]

    sent = cross_half(layout, place, tables, filters, filt, firsts, None)
    crossed = [swap(sent[step], step + half, parts) for step in range(half)]
    returned, later = own_half(layout, place, cols, tables, filters, other, filt, firsts, seconds, sent[0])
    returned = [returned[0]] + [swap(returned[step], step, parts) for step in range(1, half)]
    completed = cross_half(layout, place, tables, filters, filt, cross, later)
    completed = [completed[0]] + [swap(completed[step], step, parts) for step in range(1, half)]

    ahead = around(first_grads(layout, place, qkv, dout, returned, completed, crossed), -1, parts)
    done = final(layout, place, qkv, dout, cols, keep, returned, completed, crossed, None, None)
    return tuple(final(layout, place, qkv, dout, cols, keep, returned, completed, crossed, ahead, done))


def solution(mesh):
    in_specs = (
        P(None, ("chan", "sub"), ("groups", "seq")),
        P(("chan", "sub"), ("groups", "seq")),
        P(("chan", "sub"), "seq"),
        P(None, None, ("chan", "sub")),
        P(("chan", "sub")),
        P("groups"),
    )
    out_specs = (P(("chan", "sub"), ("groups", "seq")), P(None, ("chan", "sub"), ("groups", "seq")))
    return jax.shard_map(local, mesh=mesh, in_specs=in_specs, out_specs=out_specs, check_vma=False)
```

```python
import functools
import math

import jax
import jax.numpy as jnp
import numpy as np
from jax import lax
from jax.experimental import pallas as pl
from jax.experimental.pallas import tpu as pltpu
from jax.sharding import PartitionSpec as P

BF16 = jnp.bfloat16
F32 = jnp.float32
VMEM_LIMIT = 24 * 1024 * 1024
SCALARS = pl.BlockSpec(memory_space=pltpu.SMEM)
IN_HBM = pl.BlockSpec(memory_space=pltpu.HBM)
ANYWHERE = pl.BlockSpec(memory_space=pl.ANY)


def split_bf16(table):
    high = table.astype(np.float32).astype(BF16)
    low = (table - high.astype(np.float64)).astype(np.float32).astype(BF16)
    return high, low


def block_tables(span):
    freq = np.concatenate([np.arange(0, span, 2), np.arange(1, span, 2)])
    angle = np.pi * (2 * freq[None, :] + 1) * np.arange(span)[:, None] / (2 * span)
    forward = np.concatenate([np.cos(angle), -np.sin(angle)], axis=1)
    inverse = np.concatenate([np.cos(angle), -np.sin(angle)], axis=1).T / span
    return np.concatenate(split_bf16(forward), axis=0), split_bf16(inverse)[0]


def dot(a, b):
    return jnp.dot(a, b, preferred_element_type=F32)


def estimate(flops, moved):
    return pl.CostEstimate(flops=int(flops) * 16, bytes_accessed=int(moved) * 16, transcendentals=0)


def offsets_row(lengths_ref, first, span, ahead):
    position = lax.broadcasted_iota(jnp.int32, (8, span), 1) + (first + ahead)

    def step(genome, carry):
        end, start = carry
        end = end + lengths_ref[genome]
        return end, jnp.where(position >= end, end, start)

    begin = (jnp.int32(0), jnp.zeros((8, span), jnp.int32))
    _, start = lax.fori_loop(0, lengths_ref.shape[0], step, begin)
    return position, position - start


class Layout:
    def __init__(self, parts, channels, span):
        self.parts, self.channels, self.span = parts, channels, span
        self.half = parts // 2
        self.size = channels // self.half
        self.sub = self.size // 2


def where_am_i(place_ref, layout):
    rank, group = place_ref[0], place_ref[1]
    side = rank // layout.half
    return side, rank % layout.half, jnp.where(side == 0, 1 - group, group)


def channel_block(place_ref, layout, turn, other):
    _, own, main = where_am_i(place_ref, layout)
    return jnp.bitwise_xor(own, turn) * 2 + jnp.bitwise_xor(main, other)


def fixed(shape):
    return pl.BlockSpec(shape, lambda *args: (0,) * len(shape))


def streamed(body, layout, place, operands, in_specs, outs, out_specs, scratch, grid, cost, aliases=None):
    return pl.pallas_call(
        functools.partial(body, layout),
        out_shape=outs,
        grid_spec=pltpu.PrefetchScalarGridSpec(
            num_scalar_prefetch=1,
            grid=grid,
            in_specs=in_specs,
            out_specs=out_specs,
            scratch_shapes=scratch,
        ),
        input_output_aliases=aliases or {},
        compiler_params=pltpu.CompilerParams(vmem_limit_bytes=VMEM_LIMIT),
        cost_estimate=cost,
    )(place, *operands)


def halo_body(layout, place_ref, feat_ref, halo_ref, tail, turned, sem):
    copy = pltpu.make_async_copy(feat_ref.at[:, :, layout.span - 128 : layout.span], tail, sem)
    copy.start()
    turned[...] = jnp.zeros(turned.shape, F32)
    copy.wait()
    for which in range(3):
        turned[2 * which : 2 * which + 2, :] = tail[which].astype(F32).T[-2:, :]
    halo_ref[...] = turned[...].astype(BF16)


def pack_halo(layout, place, features):
    channels = layout.channels
    return streamed(
        halo_body,
        layout,
        place,
        (features,),
        [IN_HBM],
        jax.ShapeDtypeStruct((16, channels), BF16),
        fixed((16, channels)),
        [pltpu.VMEM((3, channels, 128), BF16), pltpu.VMEM((16, channels), F32), pltpu.SemaphoreType.DMA],
        (1,),
        estimate(0, 3 * channels * 128),
    )


def pack_body(layout, place_ref, filt_ref, after_ref, *rest):
    filt_out, sems = rest[: layout.parts - 1], rest[layout.parts - 1]
    half, sub = layout.half, layout.sub
    copies = []
    for step in range(1, layout.parts):
        begin = channel_block(place_ref, layout, step % half, step // half) * sub
        source = filt_ref.at[pl.ds(pl.multiple_of(begin, sub), sub), :]
        copies.append(pltpu.make_async_copy(source, filt_out[step - 1], sems.at[step - 1]))
    for copy in copies:
        copy.start()
    for copy in copies:
        copy.wait()


def pack_filters(layout, place, filters, after):
    parts = layout.parts
    shape = (layout.sub, layout.span)
    return streamed(
        pack_body,
        layout,
        place,
        (filters, after),
        [IN_HBM, ANYWHERE],
        [jax.ShapeDtypeStruct(shape, BF16)] * (parts - 1),
        [fixed(shape)] * (parts - 1),
        [pltpu.SemaphoreType.DMA((parts - 1,))],
        (1,),
        estimate(0, parts * layout.sub * layout.span),
    )


def lane_table(channel_columns):
    table = np.zeros((3, channel_columns, 9, 128), np.float32)
    for column in range(9):
        table[:, column, column, :] = 1.0
    return table.reshape(3 * channel_columns, 9 * 128).astype(BF16)


def three_parts(value):
    top = value.astype(BF16).astype(F32)
    middle = (value - top).astype(BF16).astype(F32)
    return [top, middle, value - top - middle]


def shift_table(rows, first_row, lanes, first_lane, back, keep):
    row = lax.broadcasted_iota(jnp.int32, (rows, lanes), 0) + first_row
    lane = lax.broadcasted_iota(jnp.int32, (rows, lanes), 1) + first_lane
    return jnp.where(row == lane - back, keep, 0.0).astype(BF16)


def edge_table(table_rows, lanes, entries):
    row = lax.broadcasted_iota(jnp.int32, (table_rows, lanes), 0)
    lane = lax.broadcasted_iota(jnp.int32, (table_rows, lanes), 1)
    table = jnp.zeros((table_rows, lanes), F32)
    for rows, where, keep in entries:
        for own_row in rows:
            table = jnp.where((row == own_row) & (lane == where), keep, table)
    return table.astype(BF16)


def small_body(layout, place_ref, lengths_ref, taps_ref, skip_ref, cols_ref, split_ref, fwd_ref, fwd_edge_ref, most_ref, last_ref, last_edge_ref, turned):
    span = layout.span
    first = place_ref[0] * span
    _, offset = offsets_row(lengths_ref, first, span, 0)
    keep, keep_back = [], []
    for j in (1, 2):
        keep.append((offset[0:1, :] >= j).astype(F32))
        position, later = offsets_row(lengths_ref, first, span, j)
        inside = (position < layout.parts * span) & (later >= j)
        keep_back.append(inside[0:1, :].astype(F32))
    most = span - 128
    for j in (0, 1):
        fwd_ref[:, j * span : (j + 1) * span] = shift_table(span, 0, span, 0, j + 1, keep[j])
        most_ref[:, j * most : (j + 1) * most] = shift_table(span, 0, most, 0, -j - 1, keep_back[j][:, :most])
        last_ref[:, j * 128 : (j + 1) * 128] = shift_table(128, most, 128, most, -j - 1, keep_back[j][:, most:])
    for which in range(3):
        begin = which * 256
        two, one = [2 * which], [2 * which + 1]
        fwd_edge_ref[:, begin : begin + 128] = edge_table(16, 128, [(one, 0, keep[0][:, :128])])
        fwd_edge_ref[:, begin + 128 : begin + 256] = edge_table(
            16, 128, [(two, 0, keep[1][:, :128]), (one, 1, keep[1][:, :128])]
        )
        near = [2 * which + 8 * k for k in range(3)]
        far = [2 * which + 1 + 8 * k for k in range(3)]
        last_edge_ref[:, begin : begin + 128] = edge_table(32, 128, [(near, 127, keep_back[0][:, most:])])
        last_edge_ref[:, begin + 128 : begin + 256] = edge_table(
            32, 128, [(far, 127, keep_back[1][:, most:]), (near, 126, keep_back[1][:, most:])]
        )
    turned[...] = jnp.zeros(turned.shape, F32)
    for which in range(3):
        turned[3 * which : 3 * which + 3, :] = taps_ref[which]
    turned[9:10, :] = skip_ref[...]
    value = turned[...]
    cols_ref[...] = value.T
    split_ref[...] = jnp.concatenate(three_parts(value), axis=0).T.astype(BF16)


def small(layout, place, lengths, taps, skip):
    channels, span = layout.channels, layout.span
    most = span - 128
    shapes = [
        ((channels, 16), F32),
        ((channels, 48), BF16),
        ((span, 2 * span), BF16),
        ((16, 768), BF16),
        ((span, 2 * most), BF16),
        ((128, 256), BF16),
        ((32, 768), BF16),
    ]
    return streamed(
        small_body,
        layout,
        place,
        (lengths, taps, skip.reshape(1, channels)),
        [SCALARS, fixed(taps.shape), fixed((1, channels))],
        [jax.ShapeDtypeStruct(*s) for s in shapes],
        [fixed(s[0]) for s in shapes],
        [pltpu.VMEM((16, channels), F32)],
        (1,),
        estimate(0, 100 * channels),
    )


def gate_body(other, layout, place_ref, feat_ref, dout_ref, halo_ref, split_ref, lanes_ref, shift_ref, shift_edge_ref, *rest):
    half, rows, span = layout.half, layout.sub, layout.span
    if other:
        main_rest, rest = rest[:half], rest[half + 1 :]
    qkv_ref, rest = rest[0], rest[1:]
    firsts, seconds = rest[:half], rest[half : 2 * half]
    edge, made = rest[2 * half :]
    side, _, _ = where_am_i(place_ref, layout)
    turn = pl.program_id(0)
    base = channel_block(place_ref, layout, turn, other) * rows
    group = min(128, rows)

    @pl.when(turn == 0)
    def _():
        edge[...] = halo_ref[...].astype(F32).T.astype(BF16)

    def tile(index, _):
        here = pl.ds(pl.multiple_of(index * group, group), group)
        spread = dot(split_ref[here, :], lanes_ref[...])
        ends = dot(edge[pl.ds(pl.multiple_of(base + index * group, group), group), :], shift_edge_ref[...])
        filtered = []
        for which in range(3):
            value = feat_ref[which, here, :]
            moved = dot(value, shift_ref[...])
            parts = []
            for lane in range(0, span, 128):
                taps = [spread[:, (3 * which + j) * 128 : (3 * which + j + 1) * 128] for j in range(3)]
                back = [moved[:, j * span + lane : j * span + lane + 128] for j in range(2)]
                if lane == 0:
                    back = [back[j] + ends[:, which * 256 + j * 128 : which * 256 + j * 128 + 128] for j in range(2)]
                total = taps[0] * value[:, lane : lane + 128].astype(F32)
                parts.append((total + taps[1] * back[0] + taps[2] * back[1]).astype(BF16))
            rounded = jnp.concatenate(parts, axis=1)
            qkv_ref[which, here, :] = rounded
            filtered.append(rounded.astype(F32))
        made[0, here, :] = (filtered[1] * filtered[2]).astype(BF16)
        made[1, here, :] = (dout_ref[here, :].astype(F32) * filtered[0]).astype(BF16)
        return 0

    lax.fori_loop(0, rows // group, tile, 0)
    for k in range(half):

        @pl.when(turn == k)
        def _(k=k):
            firsts[k][...] = made[side]
            if other:
                seconds[k][0] = main_rest[k][...]
                seconds[k][1] = made[side]
                seconds[k][2] = made[1 - side]
            else:
                seconds[k][...] = made[1 - side]


def gate(other, layout, place, features, dout, halo, split, lanes, shift, shift_edge, qkv, main_rest):
    half, rows, span, channels = layout.half, layout.sub, layout.span, layout.channels

    def block(turn, place_ref):
        return channel_block(place_ref, layout, turn, other)

    wide = pl.BlockSpec((3, rows, span), lambda *a: (0, block(*a), 0))
    flat = pl.BlockSpec((rows, span), lambda *a: (block(*a), 0))
    columns = pl.BlockSpec((rows, 48), lambda *a: (block(*a), 0))
    shapes = [(rows, span)] * half + [(3, rows, span) if other else (rows, span)] * half
    operands = [features, dout, halo, split, lanes, shift, shift_edge]
    in_specs = [wide, flat, fixed(halo.shape), columns] + [fixed(t.shape) for t in (lanes, shift, shift_edge)]
    if other:
        operands += [*main_rest, qkv]
        in_specs += [fixed((rows, span))] * half + [ANYWHERE]
    found = streamed(
        functools.partial(gate_body, other),
        layout,
        place,
        operands,
        in_specs,
        [jax.ShapeDtypeStruct(features.shape, BF16)] + [jax.ShapeDtypeStruct(s, BF16) for s in shapes],
        [wide] + [fixed(s) for s in shapes],
        [pltpu.VMEM((channels, 16), BF16), pltpu.VMEM((2, rows, span), BF16)],
        (half,),
        estimate(15 * channels * span, 9 * channels * span),
        {len(operands): 0} if other else None,
    )
    return found[0], found[1 : 1 + half], found[1 + half :]


def loop(count, body, init):
    if count <= 4:
        for k in range(count):
            init = body(k, init)
        return init
    return lax.fori_loop(0, count, body, init)


def add_product(total, f, x):
    return (total[0] + f[0] * x[0] - f[1] * x[1], total[1] + f[0] * x[1] + f[1] * x[0])


def add_conjugate(total, f, x):
    return (total[0] + f[0] * x[0] + f[1] * x[1], total[1] + f[0] * x[1] - f[1] * x[0])


def turned_sum(spectrum, neighbour, sign):
    half = spectrum[0].shape[1] // 2
    parts = []
    for lanes, flip in ((slice(0, half), sign), (slice(half, None), -sign)):
        n_re, n_im = neighbour[0][:, lanes], neighbour[1][:, lanes]
        s_re, s_im = spectrum[0][:, lanes], spectrum[1][:, lanes]
        parts.append((s_re - n_im, s_im + n_re) if flip > 0 else (s_re + n_im, s_im - n_re))
    return tuple(jnp.concatenate([p[k] for p in parts], axis=1) for k in range(2))


def forward(raw, spec, begin, target, rows, table_ref):
    value = raw[pl.ds(pl.multiple_of(begin, 16), rows), :]
    spec[pl.ds(pl.multiple_of(target, 16), rows), :] = dot(jnp.concatenate([value, value], axis=1), table_ref[...])


def spectrum_at(spec, begin, group, span):
    place = pl.ds(pl.multiple_of(begin, group), group)
    return spec[place, :span], spec[place, span:]


def store_spectrum(ready, begin, value, group, span):
    place = pl.ds(pl.multiple_of(begin, group), group)
    ready[place, :span] = value[0].astype(BF16)
    ready[place, span:] = value[1].astype(BF16)


def own_body(layout, place_ref, cols_ref, forward_ref, inverse_ref, filt_ref, other_ref, *rest):
    parts, half, size, sub, span = layout.parts, layout.half, layout.size, layout.sub, layout.span
    filt_in, rest = rest[: parts - 1], rest[parts - 1 :]
    firsts, seconds, rest = rest[:half], rest[half : 2 * half], rest[2 * half + 1 :]
    returned, later = rest[:half], rest[half : 2 * half]
    raw, spec, ready, back = rest[2 * half :]
    side, own, main = where_am_i(place_ref, layout)
    rank = place_ref[0]
    kind_rows = half * size
    signals = parts * size

    def rows_at(begin, count):
        return pl.ds(pl.multiple_of(begin, sub), count)

    for cls in range(2):
        source = rows_at(jnp.bitwise_xor(main, cls) * sub, sub)
        raw[rows_at(rank * size + cls * sub, sub), :] = filt_ref[source, :]
    for step in range(1, parts):
        begin = jnp.bitwise_xor(rank, step) * size
        raw[rows_at(begin, sub), :] = filt_in[step - 1][...]
        raw[rows_at(begin + sub, sub), :] = other_ref[(step - 1) * sub : step * sub, :]
    for step in range(half):
        block = signals + jnp.bitwise_xor(own, step) * size
        raw[rows_at(block + side * kind_rows, sub), :] = firsts[step][...]
        raw[rows_at(block + (1 - side) * kind_rows, sub), :] = seconds[step][0]
        raw[rows_at(block + side * kind_rows + sub, sub), :] = seconds[step][1]
        raw[rows_at(block + (1 - side) * kind_rows + sub, sub), :] = seconds[step][2]

    def transform(index, _):
        kind, part = index // half, index % half
        begin = jnp.where(kind == 0, 0, signals + (kind - 1) * kind_rows) + part * size
        forward(raw, spec, begin, index * size, size, forward_ref)
        return 0

    lax.fori_loop(0, 3 * half, transform, 0)
    group = 16
    zero = (jnp.zeros((group, span), F32),) * 2

    def products(index, _):
        def read(kind, k):
            return spectrum_at(spec, (kind * half + k) * size + index * group, group, span)

        def store(kind, k, value):
            store_spectrum(ready, (kind * half + k) * size + index * group, value, group, span)

        before = None
        for place in range(half):
            total = loop(place + 1, lambda k, t, p=place: add_product(t, read(0, k), read(1, p - k)), zero)
            store(0, place, total if before is None else turned_sum(total, before, 1))
            before = total
        before = None
        for place in range(half - 1, -1, -1):
            total = loop(half - place, lambda k, t, p=place: add_conjugate(t, read(0, k), read(2, p + k)), zero)
            store(1, place, total if before is None else turned_sum(total, before, -1))
            before = total
        return 0

    lax.fori_loop(0, size // group, products, 0)

    def restore(index, _):
        place = rows_at(index * size, size)
        back[place, :] = dot(ready[place, :], inverse_ref[...])
        return 0

    lax.fori_loop(0, 2 * half, restore, 0)

    def result(kind, cls, part):
        begin = kind * kind_rows + part * size + cls * sub
        direct = raw[rows_at(signals + begin, sub), :].astype(F32)
        skip = cols_ref[rows_at(jnp.bitwise_xor(main, cls) * sub, sub), 9:10]
        return back[rows_at(begin, sub), :] + skip * direct

    for step in range(half):
        part = jnp.bitwise_xor(own, step)
        returned[step][0] = result(side, 0, part).astype(BF16)
        returned[step][1] = result(side, 1, part).astype(BF16)
        returned[step][2] = result(1 - side, 1, part).astype(BF16)
        later[step][...] = result(1 - side, 0, part)


def own_half(layout, place, cols, tables, filters, other, filt, firsts, seconds, after):
    half, size, sub, span, parts = layout.half, layout.size, layout.sub, layout.span, layout.parts
    own_class = lambda step, place_ref: (where_am_i(place_ref, layout)[1], 0)
    shapes = [((3, sub, span), BF16)] * half + [((sub, span), F32)] * half
    rows = 3 * half * size
    found = streamed(
        own_body,
        layout,
        place,
        (cols, *tables, filters, other, *filt, *firsts, *seconds, after),
        [pl.BlockSpec((size, 16), own_class)]
        + [fixed(t.shape) for t in tables]
        + [pl.BlockSpec((size, span), own_class), fixed(other.shape)]
        + [fixed((sub, span))] * (parts - 1 + half)
        + [fixed((3, sub, span))] * half
        + [ANYWHERE],
        [jax.ShapeDtypeStruct(*s) for s in shapes],
        [fixed(s[0]) for s in shapes],
        [
            pltpu.VMEM(((parts + 2 * half) * size, span), BF16),
            pltpu.VMEM((rows, 2 * span), F32),
            pltpu.VMEM((2 * half * size, 2 * span), BF16),
            pltpu.VMEM((2 * half * size, span), F32),
        ],
        (1,),
        estimate(2 * rows * span * 2 * span * 3, 7 * half * size * span * 2),
    )
    return found[:half], found[half:]


def cross_body(arriving, layout, place_ref, forward_ref, inverse_ref, filt_ref, *rest):
    parts, half, sub, span = layout.parts, layout.half, layout.sub, layout.span
    filt_in, rest = rest[: parts - 1], rest[parts - 1 :]
    signal, rest = rest[:half], rest[half:]
    partial, rest = (rest[:half], rest[half:]) if arriving else (None, rest)
    outs = rest[:half]
    raw, spec, ready, back = rest[half:]
    side, own, _ = where_am_i(place_ref, layout)
    rank = place_ref[0]
    block = parts * sub

    def rows_at(begin, count):
        return pl.ds(pl.multiple_of(begin, sub), count)

    raw[rows_at(rank * sub, sub), :] = filt_ref[...]
    for step in range(1, parts):
        raw[rows_at(jnp.bitwise_xor(rank, step) * sub, sub), :] = filt_in[step - 1][...]
    for step in range(half):
        raw[rows_at(block + jnp.bitwise_xor(own, step) * sub, sub), :] = signal[step][...]
    count = (parts + half) * sub
    chunk = math.gcd(count, 512)

    def transform(index, _):
        forward(raw, spec, index * chunk, index * chunk, chunk, forward_ref)
        return 0

    lax.fori_loop(0, count // chunk, transform, 0)
    group = 16
    zero = (jnp.zeros((group, span), F32),) * 2
    from_first = side == (1 if arriving else 0)

    def products(index, ahead):
        def filt(k):
            return spectrum_at(spec, k * sub + index * group, group, span)

        def sig(k):
            return spectrum_at(spec, block + k * sub + index * group, group, span)

        before = None
        if ahead:
            for place in range(half - 1, parts):
                total = loop(half, lambda k, t, p=place: add_product(t, filt(p - k), sig(k)), zero)
                if before is not None:
                    value = turned_sum(total, before, 1)
                    store_spectrum(ready, (place - half) * sub + index * group, value, group, span)
                before = total
        else:
            for place in range(half, -1, -1):
                total = loop(half, lambda k, t, p=place: add_conjugate(t, filt(half + k - p), sig(k)), zero)
                if before is not None:
                    value = turned_sum(total, before, -1)
                    store_spectrum(ready, place * sub + index * group, value, group, span)
                before = total
        return 0

    @pl.when(from_first)
    def _():
        lax.fori_loop(0, sub // group, lambda k, _: products(k, True), 0)

    @pl.when(jnp.logical_not(from_first))
    def _():
        lax.fori_loop(0, sub // group, lambda k, _: products(k, False), 0)

    back[...] = dot(ready[...], inverse_ref[...])
    for step in range(half):
        value = back[rows_at(jnp.bitwise_xor(own, step) * sub, sub), :]
        if arriving:
            value = value + partial[step][...]
        outs[step][...] = value.astype(BF16)


def cross_half(layout, place, tables, filters, filt, signal, partial):
    half, sub, span, parts = layout.half, layout.sub, layout.span, layout.parts
    arriving = partial is not None
    rows = (parts + half) * sub
    main_class = pl.BlockSpec((sub, span), lambda step, place_ref: (channel_block(place_ref, layout, 0, 0), 0))
    return streamed(
        functools.partial(cross_body, arriving),
        layout,
        place,
        (*tables, filters, *filt, *signal, *(partial or ())),
        [fixed(t.shape) for t in tables]
        + [main_class]
        + [fixed((sub, span))] * (parts - 1 + half + (half if arriving else 0)),
        [jax.ShapeDtypeStruct((sub, span), BF16)] * half,
        [fixed((sub, span))] * half,
        [
            pltpu.VMEM((rows, span), BF16),
            pltpu.VMEM((rows, 2 * span), F32),
            pltpu.VMEM((half * sub, 2 * span), BF16),
            pltpu.VMEM((half * sub, span), F32),
        ],
        (1,),
        estimate(2 * rows * span * 2 * span * 3, 10 * half * sub * span * 2),
    )


def first_body(layout, place_ref, qkv_ref, dout_ref, *rest):
    half, sub = layout.half, layout.sub
    returned, completed, crossed = rest[:half], rest[half : 2 * half], rest[2 * half : 3 * half]
    out_ref, grads = rest[3 * half :]
    side, _, _ = where_am_i(place_ref, layout)
    for turn in range(half):
        for other in range(2):
            begin = channel_block(place_ref, layout, turn, other) * sub
            place = pl.ds(pl.multiple_of(begin, sub), sub)
            plain = returned[turn][other].astype(F32)
            if other:
                mixed = returned[turn][2].astype(F32) + crossed[turn][...].astype(F32)
                mixed = mixed.astype(BF16).astype(F32)
            else:
                mixed = completed[turn][...].astype(F32)
            y_out = jnp.where(side == 0, plain, mixed)
            dmixed = jnp.where(side == 0, mixed, plain)
            grads[0, place, :] = dout_ref[place, :].astype(F32) * y_out
            grads[1, place, :] = dmixed * qkv_ref[2, place, :].astype(F32)
            grads[2, place, :] = dmixed * qkv_ref[1, place, :].astype(F32)
    out_ref[...] = jnp.zeros(out_ref.shape, F32)
    for which in range(3):
        out_ref[2 * which : 2 * which + 2, :] = grads[which].T[0:2, :]


def first_grads(layout, place, qkv, dout, returned, completed, crossed):
    half, sub, channels = layout.half, layout.sub, layout.channels
    return streamed(
        first_body,
        layout,
        place,
        (qkv, dout, *returned, *completed, *crossed),
        [fixed((3, channels, 128)), fixed((channels, 128))]
        + [fixed((3, sub, 128))] * half
        + [fixed((sub, 128))] * (2 * half),
        jax.ShapeDtypeStruct((8, channels), F32),
        fixed((8, channels)),
        [pltpu.VMEM((3, channels, 128), F32)],
        (1,),
        estimate(0, 3 * channels * 128 * 2),
    )


def final_body(last, layout, place_ref, qkv_ref, dout_ref, split_ref, lanes_ref, shift_ref, *rest):
    half, rows, span = layout.half, layout.sub, layout.span
    returned, completed, crossed = rest[:half], rest[half : 2 * half], rest[2 * half : 3 * half]
    rest = rest[3 * half :]
    ahead_ref, edge_ref, rest = (rest[0], rest[1], rest[4:]) if last else (None, None, rest)
    out_ref, dfeat_ref, edge, moved = rest
    width = 128 if last else span
    written = 128 if last else span - 128
    side, _, _ = where_am_i(place_ref, layout)
    turn, other = pl.program_id(0) // 2, pl.program_id(0) % 2
    base = channel_block(place_ref, layout, turn, other) * rows

    if last:

        @pl.when(pl.program_id(0) == 0)
        def _():
            value = ahead_ref[...]
            edge[...] = jnp.concatenate(three_parts(value) + [jnp.zeros_like(value)], axis=0).T.astype(BF16)

    for k in range(half):

        @pl.when(turn == k)
        def _(k=k):
            moved[side] = returned[k][other]

        @pl.when((turn == k) & (other == 1))
        def _(k=k):
            moved[1 - side] = (returned[k][2].astype(F32) + crossed[k][...].astype(F32)).astype(BF16)

        @pl.when((turn == k) & (other == 0))
        def _(k=k):
            moved[1 - side] = completed[k][...]

    group = min(128, rows)

    def tile(index, _):
        here = pl.ds(pl.multiple_of(index * group, group), group)
        spread = dot(split_ref[here, :], lanes_ref[...])
        if last:
            ends = dot(edge[pl.ds(pl.multiple_of(base + index * group, group), group), :], edge_ref[...])
        arrays = [moved[0, here, :], moved[1, here, :], dout_ref[here, :], qkv_ref[1, here, :], qkv_ref[2, here, :]]
        ahead = [dot(a, shift_ref[...]) for a in arrays]
        query = qkv_ref[0, here, :]
        for lane in range(0, written, 128):

            def three(a):
                begins = (lane, lane + written)
                return [arrays[a][:, lane : lane + 128].astype(F32)] + [ahead[a][:, b : b + 128] for b in begins]

            y_out, dmixed, dout_f, key, value = [three(a) for a in range(5)]
            lanes = slice(lane, lane + 128)
            out_ref[here, lanes] = (query[:, lanes].astype(F32) * y_out[0]).astype(BF16)
            for which, pair in enumerate(((dout_f, y_out), (dmixed, value), (dmixed, key))):
                grads = [pair[0][j] * pair[1][j] for j in range(3)]
                if last:
                    for j in (1, 2):
                        grads[j] = grads[j] + ends[:, which * 256 + (j - 1) * 128 : which * 256 + j * 128]
                taps = [spread[:, (3 * which + j) * 128 : (3 * which + j + 1) * 128] for j in range(3)]
                total = taps[0] * grads[0] + taps[1] * grads[1] + taps[2] * grads[2]
                dfeat_ref[which, here, lanes] = total.astype(BF16)
        return 0

    lax.fori_loop(0, rows // group, tile, 0)


def final(layout, place, qkv, dout, split, lane_sum, shift, returned, completed, crossed, ahead, edge, earlier):
    half, rows, span, channels = layout.half, layout.sub, layout.span, layout.channels
    last = ahead is not None
    width = 128 if last else span
    written = 128 if last else span - 128
    lanes = span // 128 - 1 if last else 0

    def block(step, place_ref):
        return channel_block(place_ref, layout, step // 2, step % 2)

    def wide(size, index):
        return pl.BlockSpec((3, rows, size), lambda *a: (0, block(*a), index))

    def flat(size, index):
        return pl.BlockSpec((rows, size), lambda *a: (block(*a), index))

    def held(shape):
        return pl.BlockSpec(shape, lambda *a: (0,) * (len(shape) - 1) + (lanes,))

    operands = [qkv, dout, split, lane_sum, shift, *returned, *completed, *crossed]
    in_specs = (
        [wide(width, lanes), flat(width, lanes), flat(48, 0), fixed(lane_sum.shape), fixed(shift.shape)]
        + [held((3, rows, width))] * half
        + [held((rows, width))] * (2 * half)
    )
    aliases = {}
    if last:
        operands += [ahead, edge, *earlier]
        in_specs += [fixed(ahead.shape), fixed(edge.shape), ANYWHERE, ANYWHERE]
        aliases = {len(operands) - 1: 0, len(operands): 1}
    return streamed(
        functools.partial(final_body, last),
        layout,
        place,
        operands,
        in_specs,
        [jax.ShapeDtypeStruct((channels, span), BF16), jax.ShapeDtypeStruct((3, channels, span), BF16)],
        [flat(written, lanes), wide(written, lanes)],
        [pltpu.VMEM((channels, 32), BF16), pltpu.VMEM((2, rows, width), BF16)],
        (layout.parts,),
        estimate(20 * channels * span, 10 * channels * span),
        aliases,
    )


def swap(value, step, parts, axis="seq"):
    return lax.ppermute(value, axis, [(source, source ^ step) for source in range(parts)])


def around(value, steps, parts):
    return lax.ppermute(value, "seq", [(source, (source + steps) % parts) for source in range(parts)])


def local(features, dout, filters, taps, skip, lengths):
    parts = lax.axis_size("seq")
    _, channels, span = features.shape
    layout = Layout(parts, channels, span)
    half = layout.half
    place = jnp.stack([lax.axis_index("seq"), lax.axis_index("groups")]).astype(jnp.int32)
    tables = [jnp.asarray(t) for t in block_tables(span)]

    lanes = jnp.asarray(lane_table(16))

    halo = around(pack_halo(layout, place, features), 1, parts)
    filt = pack_filters(layout, place, filters, halo)
    filt = [swap(filt[step - 1], step, parts) for step in range(1, parts)]
    other = swap(jnp.concatenate(filt, axis=0), 1, 2, "groups")
    cols, split, shift, shift_edge, most, last, last_edge = small(layout, place, lengths, taps, skip)
    first_args = (layout, place, features, dout, halo, split, lanes, shift, shift_edge)
    qkv, firsts, main_rest = gate(0, *first_args, None, None)
    firsts = [firsts[0]] + [swap(firsts[step], step, parts) for step in range(1, half)]
    qkv, cross, seconds = gate(1, *first_args, qkv, main_rest)
    seconds = [seconds[0]] + [swap(seconds[step], step, parts) for step in range(1, half)]
    cross = [swap(cross[step], step + half, parts) for step in range(half)]

    sent = cross_half(layout, place, tables, filters, filt, firsts, None)
    crossed = [swap(sent[step], step + half, parts) for step in range(half)]
    returned, later = own_half(layout, place, cols, tables, filters, other, filt, firsts, seconds, sent[0])
    returned = [returned[0]] + [swap(returned[step], step, parts) for step in range(1, half)]
    completed = cross_half(layout, place, tables, filters, filt, cross, later)
    completed = [completed[0]] + [swap(completed[step], step, parts) for step in range(1, half)]

    ahead = around(first_grads(layout, place, qkv, dout, returned, completed, crossed), -1, parts)
    done = final(layout, place, qkv, dout, split, lanes, most, returned, completed, crossed, None, None, None)
    done = final(layout, place, qkv, dout, split, lanes, last, returned, completed, crossed, ahead, last_edge, done)
    return tuple(done)


def solution(mesh):
    in_specs = (
        P(None, ("chan", "sub"), ("groups", "seq")),
        P(("chan", "sub"), ("groups", "seq")),
        P(("chan", "sub"), "seq"),
        P(None, None, ("chan", "sub")),
        P(("chan", "sub")),
        P("groups"),
    )
    out_specs = (P(("chan", "sub"), ("groups", "seq")), P(None, ("chan", "sub"), ("groups", "seq")))
    return jax.shard_map(local, mesh=mesh, in_specs=in_specs, out_specs=out_specs, check_vma=False)
```

```python
import functools
import math

import jax
import jax.numpy as jnp
import numpy as np
from jax import lax
from jax.experimental import pallas as pl
from jax.experimental.pallas import tpu as pltpu
from jax.sharding import PartitionSpec as P

BF16 = jnp.bfloat16
F32 = jnp.float32
SHARE = 0.5
VMEM_LIMIT = 24 * 1024 * 1024
SCALARS = pl.BlockSpec(memory_space=pltpu.SMEM)
IN_HBM = pl.BlockSpec(memory_space=pltpu.HBM)
HELD = pl.BlockSpec(memory_space=pltpu.VMEM)
ANYWHERE = pl.BlockSpec(memory_space=pl.ANY)


def split_bf16(table):
    high = table.astype(np.float32).astype(BF16)
    low = (table - high.astype(np.float64)).astype(np.float32).astype(BF16)
    return high, low


def block_tables(span):
    freq = np.concatenate([np.arange(0, span, 2), np.arange(1, span, 2)])
    angle = np.pi * (2 * freq[None, :] + 1) * np.arange(span)[:, None] / (2 * span)
    forward = np.concatenate([np.cos(angle), -np.sin(angle)], axis=1)
    inverse = np.concatenate([np.cos(angle), -np.sin(angle)], axis=1).T / span
    return np.concatenate(split_bf16(forward), axis=0), split_bf16(inverse)[0]


def dot(a, b):
    return jnp.dot(a, b, preferred_element_type=F32)


def estimate(time_us):
    return pl.CostEstimate(flops=int(SHARE * time_us * 1e9), bytes_accessed=0, transcendentals=0)


def offsets_row(lengths_ref, first, span, ahead):
    position = lax.broadcasted_iota(jnp.int32, (8, span), 1) + (first + ahead)

    def step(genome, carry):
        end, start = carry
        end = end + lengths_ref[genome]
        return end, jnp.where(position >= end, end, start)

    begin = (jnp.int32(0), jnp.zeros((8, span), jnp.int32))
    _, start = lax.fori_loop(0, lengths_ref.shape[0], step, begin)
    return position, position - start


class Layout:
    def __init__(self, parts, channels, span):
        self.parts, self.channels, self.span = parts, channels, span
        self.half = parts // 2
        self.size = channels // self.half
        self.sub = self.size // 2


def where_am_i(place_ref, layout):
    rank, group = place_ref[0], place_ref[1]
    side = rank // layout.half
    return side, rank % layout.half, jnp.where(side == 0, 1 - group, group)


def channel_block(place_ref, layout, turn, other):
    _, own, main = where_am_i(place_ref, layout)
    return jnp.bitwise_xor(own, turn) * 2 + jnp.bitwise_xor(main, other)


def run(body, layout, place, operands, outs, scratch, cost, in_specs=None, out_specs=None, aliases=None):
    single = not isinstance(outs, list)
    return pl.pallas_call(
        functools.partial(body, layout),
        out_shape=outs,
        in_specs=[SCALARS] + (in_specs or [HELD] * len(operands)),
        out_specs=out_specs or (HELD if single else [HELD] * len(outs)),
        scratch_shapes=scratch,
        input_output_aliases=aliases or {},
        compiler_params=pltpu.CompilerParams(vmem_limit_bytes=VMEM_LIMIT),
        cost_estimate=cost,
    )(place, *operands)


def rows_at(begin, step, count):
    return pl.ds(pl.multiple_of(begin, step), count)


def pack_body(layout, place_ref, feat_hbm, filt_hbm, halo_ref, *rest):
    outs, (tail, turned, sems) = rest[:-3], rest[-3:]
    half, sub = layout.half, layout.sub
    copies = [pltpu.make_async_copy(feat_hbm.at[:, :, pl.ds(layout.span - 128, 128)], tail, sems.at[layout.parts + 1])]
    for step in range(layout.parts + 1):
        turn, other = (step % half, step // half) if step else (0, 0)
        if step == layout.parts:
            turn, other = 0, 1
        begin = channel_block(place_ref, layout, turn, other) * sub
        source = filt_hbm.at[rows_at(begin, sub, sub), :]
        copies.append(pltpu.make_async_copy(source, outs[step], sems.at[step]))
    for copy in copies:
        copy.start()
    turned[...] = jnp.zeros(turned.shape, F32)
    copies[0].wait()
    for which in range(3):
        turned[2 * which : 2 * which + 2, :] = tail[which].astype(F32).T[-2:, :]
    halo_ref[...] = turned[...].astype(BF16)
    for copy in copies[1:]:
        copy.wait()


def pack(layout, place, features, filters):
    parts, sub, span, channels = layout.parts, layout.sub, layout.span, layout.channels
    outs = [jax.ShapeDtypeStruct((16, channels), BF16)] + [jax.ShapeDtypeStruct((sub, span), BF16)] * (parts + 1)
    scratch = [
        pltpu.VMEM((3, channels, 128), BF16),
        pltpu.VMEM((16, channels), F32),
        pltpu.SemaphoreType.DMA((parts + 2,)),
    ]
    found = run(pack_body, layout, place, (features, filters), outs, scratch, estimate(2.0), in_specs=[IN_HBM] * 2)
    return found[0], (found[1], found[1 + parts]), found[2 : 1 + parts]


def three_parts(value):
    top = value.astype(BF16).astype(F32)
    middle = (value - top).astype(BF16).astype(F32)
    return [top, middle, value - top - middle]


def edge_table(table_rows, lanes, entries):
    row = lax.broadcasted_iota(jnp.int32, (table_rows, lanes), 0)
    lane = lax.broadcasted_iota(jnp.int32, (table_rows, lanes), 1)
    table = jnp.zeros((table_rows, lanes), F32)
    for rows, where, keep in entries:
        for own_row in rows:
            table = jnp.where((row == own_row) & (lane == where), keep, table)
    return table.astype(BF16)


def small_body(layout, place_ref, lengths_ref, taps_ref, skip_ref, *rest):
    cols_ref, split_ref, keep_ref, fwd_edge_ref, last_edge_ref, turned, lanes_ref = rest
    span = layout.span
    first = place_ref[0] * span
    _, offset = offsets_row(lengths_ref, first, span, 0)
    keep, keep_back = [], []
    for j in (1, 2):
        keep.append((offset[0:1, :] >= j).astype(F32))
        position, later = offsets_row(lengths_ref, first, span, j)
        inside = (position < layout.parts * span) & (later >= j)
        keep_back.append(inside[0:1, :].astype(F32))
    most = span - 128
    lane = lax.broadcasted_iota(jnp.int32, (1, span), 1)
    keep_ref[...] = jnp.zeros(keep_ref.shape, F32)
    for j in (0, 1):
        keep_ref[j : j + 1, :] = jnp.where(lane > j, keep[j], 0.0)
        keep_ref[2 + j : 3 + j, :] = jnp.where(lane < span - 1 - j, keep_back[j], 0.0)
    for which in range(3):
        begin = which * 256
        two, one = [2 * which], [2 * which + 1]
        fwd_edge_ref[:, begin : begin + 128] = edge_table(16, 128, [(one, 0, keep[0][:, :128])])
        fwd_edge_ref[:, begin + 128 : begin + 256] = edge_table(
            16, 128, [(two, 0, keep[1][:, :128]), (one, 1, keep[1][:, :128])]
        )
        entries = []
        for k, (lane_at, j) in enumerate(((127, 0), (127, 1), (126, 1))):
            entries.append(([3 * which + k + 16 * p for p in range(3)], lane_at, keep_back[j][:, most:]))
        last_edge_ref[:, which * 128 : (which + 1) * 128] = edge_table(48, 128, entries)
    turned[...] = jnp.zeros(turned.shape, F32)
    for which in range(3):
        turned[3 * which : 3 * which + 3, :] = taps_ref[which]
    turned[9:10, :] = skip_ref[...]
    value = turned[...]
    cols_ref[...] = value.T
    split_ref[...] = jnp.concatenate(three_parts(value), axis=0).T.astype(BF16)
    column = lax.broadcasted_iota(jnp.int32, (48, 128), 0) % 16
    for k in range(9):
        lanes_ref[:, k * 128 : (k + 1) * 128] = jnp.where(column == k, 1.0, 0.0).astype(BF16)


def small(layout, place, lengths, taps, skip):
    channels, span = layout.channels, layout.span
    shapes = [
        ((channels, 16), F32),
        ((channels, 48), BF16),
        ((8, span), F32),
        ((16, 768), BF16),
        ((48, 384), BF16),
        ((16, channels), F32),
        ((48, 9 * 128), BF16),
    ]
    return run(
        small_body,
        layout,
        place,
        (lengths, taps, skip.reshape(1, channels)),
        [jax.ShapeDtypeStruct(*s) for s in shapes],
        [],
        estimate(1.2),
        in_specs=[SCALARS, HELD, HELD],
    )


def gate_body(layout, place_ref, feat_hbm, dout_hbm, halo_ref, split_ref, lanes_ref, keep_ref, edge_ref, *rest):
    half, rows, span = layout.half, layout.sub, layout.span
    gated, firsts, cross, seconds = (rest[:4], *(rest[4 + k * half : 4 + (k + 1) * half] for k in range(3)))
    feat_ref, ends_of, spread, ends, sems = rest[4 + 3 * half :]
    side, _, _ = where_am_i(place_ref, layout)
    group = min(32, rows)
    steps = [(turn, other) for other in range(2) for turn in range(half)]
    copies = []
    for k, (turn, other) in enumerate(steps):
        block = rows_at(channel_block(place_ref, layout, turn, other) * rows, rows, rows)
        copies.append(pltpu.make_async_copy(feat_hbm.at[:, block, :], feat_ref.at[k], sems.at[k, 0]))
        copies.append(pltpu.make_async_copy(dout_hbm.at[block, :], gated[2 * other + 1].at[turn], sems.at[k, 1]))
        for copy in copies[-2:]:
            copy.start()
    ends_of[...] = halo_ref[...].astype(F32).T.astype(BF16)
    keep = [keep_ref[j : j + 1, :] for j in range(2)]
    for k, (turn, other) in enumerate(steps):
        block = rows_at(channel_block(place_ref, layout, turn, other) * rows, rows, rows)
        qkv_ref, dout_ref = gated[2 * other : 2 * other + 2]
        spread[...] = dot(split_ref[block, :], lanes_ref[...])
        ends[...] = dot(ends_of[block, :], edge_ref[...])
        for copy in copies[2 * k : 2 * k + 2]:
            copy.wait()

        def tile(index, _, k=k, turn=turn, other=other, qkv_ref=qkv_ref, dout_ref=dout_ref):
            local_rows = rows_at(index * group, group, group)
            filtered = []
            for which in range(3):
                value = feat_ref[k, which, local_rows, :].astype(F32)
                moved = [pltpu.roll(value, j + 1, 1) * keep[j] for j in range(2)]
                taps = [spread[local_rows, (3 * which + j) * 128 : (3 * which + j + 1) * 128] for j in range(3)]
                parts = []
                for lane in range(0, span, 128):
                    back = [moved[j][:, lane : lane + 128] for j in range(2)]
                    if lane == 0:
                        begins = [which * 256 + j * 128 for j in range(2)]
                        back = [back[j] + ends[local_rows, begins[j] : begins[j] + 128] for j in range(2)]
                    total = taps[0] * value[:, lane : lane + 128]
                    parts.append((total + taps[1] * back[0] + taps[2] * back[1]).astype(BF16))
                filtered.append(jnp.concatenate(parts, axis=1))
                qkv_ref[turn, which, local_rows, :] = filtered[-1]
            mixed = filtered[1] * filtered[2]
            grad_in = dout_ref[turn, local_rows, :] * filtered[0]
            first = jnp.where(side == 0, mixed, grad_in)
            second = jnp.where(side == 0, grad_in, mixed)
            pair = seconds[turn] if other else firsts[turn]
            pair[0, local_rows, :] = first
            pair[1, local_rows, :] = second
            if other:
                cross[turn][local_rows, :] = first
            return 0

        lax.fori_loop(0, rows // group, tile, 0, unroll=min(2, rows // group))


def gate(layout, place, features, dout, halo, split, lanes, keep, edge):
    half, rows, span, channels = layout.half, layout.sub, layout.span, layout.channels
    pair = (2, rows, span)
    shapes = [(half, 3, rows, span), (half, rows, span)] * 2 + [pair] * half + [(rows, span)] * half + [pair] * half
    found = run(
        gate_body,
        layout,
        place,
        (features, dout, halo, split, lanes, keep, edge),
        [jax.ShapeDtypeStruct(s, BF16) for s in shapes],
        [
            pltpu.VMEM((2 * half, 3, rows, span), BF16),
            pltpu.VMEM((channels, 16), BF16),
            pltpu.VMEM((rows, 9 * 128), F32),
            pltpu.VMEM((rows, 768), F32),
            pltpu.SemaphoreType.DMA((2 * half, 2)),
        ],
        estimate(5.7),
        in_specs=[IN_HBM] * 2 + [HELD] * 5,
    )
    return found[0:2], found[2:4], found[4 : 4 + half], found[4 + half : 4 + 2 * half], found[4 + 2 * half :]


def loop(count, body, init):
    if count <= 4:
        for k in range(count):
            init = body(k, init)
        return init
    return lax.fori_loop(0, count, body, init)


def add_product(total, f, x):
    return (total[0] + f[0] * x[0] - f[1] * x[1], total[1] + f[0] * x[1] + f[1] * x[0])


def add_conjugate(total, f, x):
    return (total[0] + f[0] * x[0] + f[1] * x[1], total[1] + f[0] * x[1] - f[1] * x[0])


def turned_sum(spectrum, neighbour, sign):
    half = spectrum[0].shape[1] // 2
    parts = []
    for lanes, flip in ((slice(0, half), sign), (slice(half, None), -sign)):
        n_re, n_im = neighbour[0][:, lanes], neighbour[1][:, lanes]
        s_re, s_im = spectrum[0][:, lanes], spectrum[1][:, lanes]
        parts.append((s_re - n_im, s_im + n_re) if flip > 0 else (s_re + n_im, s_im - n_re))
    return tuple(jnp.concatenate([p[k] for p in parts], axis=1) for k in range(2))


def forward(raw, spec, begin, target, rows, table_ref):
    value = raw[pl.ds(pl.multiple_of(begin, 16), rows), :]
    spec[pl.ds(pl.multiple_of(target, 16), rows), :] = dot(jnp.concatenate([value, value], axis=1), table_ref[...])


def spectrum_at(spec, begin, group, span):
    place = pl.ds(pl.multiple_of(begin, group), group)
    return spec[place, :span], spec[place, span:]


def store_spectrum(ready, begin, value, group, span):
    place = pl.ds(pl.multiple_of(begin, group), group)
    ready[place, :span] = value[0].astype(BF16)
    ready[place, span:] = value[1].astype(BF16)


def filter_body(layout, place_ref, forward_ref, filt_ref, *rest):
    parts, sub = layout.parts, layout.sub
    filt_in, (spec, raw) = rest[: parts - 1], rest[parts - 1 :]
    rank = place_ref[0]
    raw[rows_at(rank * sub, sub, sub), :] = filt_ref[...]
    for step in range(1, parts):
        raw[rows_at(jnp.bitwise_xor(rank, step) * sub, sub, sub), :] = filt_in[step - 1][...]
    chunk = math.gcd(parts * sub, 512)

    def transform(index, _):
        forward(raw, spec, index * chunk, index * chunk, chunk, forward_ref)
        return 0

    lax.fori_loop(0, parts * sub // chunk, transform, 0)


def filter_spectra(layout, place, table, own, filt):
    rows, span = layout.parts * layout.sub, layout.span
    return run(
        filter_body,
        layout,
        place,
        (table, own, *filt),
        jax.ShapeDtypeStruct((rows, 2 * span), F32),
        [pltpu.VMEM((rows, span), BF16)],
        estimate(1.5),
    )


def cross_body(layout, place_ref, forward_ref, inverse_ref, known, *rest):
    parts, half, sub, span = layout.parts, layout.half, layout.sub, layout.span
    signal, outs = rest[:half], rest[half : 2 * half]
    spec, raw, ready, back = rest[2 * half :]
    side, own, _ = where_am_i(place_ref, layout)
    for step in range(half):
        raw[rows_at(jnp.bitwise_xor(own, step) * sub, sub, sub), :] = signal[step][0]
    forward(raw, spec, 0, 0, half * sub, forward_ref)
    group = 16
    zero = (jnp.zeros((group, span), F32),) * 2

    def products(index, ahead):
        def filt(k):
            return spectrum_at(known, k * sub + index * group, group, span)

        def sig(k):
            return spectrum_at(spec, k * sub + index * group, group, span)

        before = None
        if ahead:
            for place in range(half - 1, parts):
                total = loop(half, lambda k, t, p=place: add_product(t, filt(p - k), sig(k)), zero)
                if before is not None:
                    value = turned_sum(total, before, 1)
                    store_spectrum(ready, (place - half) * sub + index * group, value, group, span)
                before = total
        else:
            for place in range(half, -1, -1):
                total = loop(half, lambda k, t, p=place: add_conjugate(t, filt(half + k - p), sig(k)), zero)
                if before is not None:
                    value = turned_sum(total, before, -1)
                    store_spectrum(ready, place * sub + index * group, value, group, span)
                before = total
        return 0

    @pl.when(side == 0)
    def _():
        lax.fori_loop(0, sub // group, lambda k, _: products(k, True), 0)

    @pl.when(side == 1)
    def _():
        lax.fori_loop(0, sub // group, lambda k, _: products(k, False), 0)

    back[...] = dot(ready[...], inverse_ref[...])
    for step in range(half):
        outs[step][...] = back[rows_at(jnp.bitwise_xor(own, step) * sub, sub, sub), :].astype(BF16)


def cross_half(layout, place, tables, known, signal):
    half, sub, span = layout.half, layout.sub, layout.span
    rows = half * sub
    found = run(
        cross_body,
        layout,
        place,
        (*tables, known, *signal),
        [jax.ShapeDtypeStruct((sub, span), BF16)] * half + [jax.ShapeDtypeStruct((rows, 2 * span), F32)],
        [
            pltpu.VMEM((rows, span), BF16),
            pltpu.VMEM((rows, 2 * span), BF16),
            pltpu.VMEM((rows, span), F32),
        ],
        estimate(2.0),
    )
    return found[:half], found[half]


def hold_body(layout, place_ref, *refs):
    pass


def hold(layout, place, arrays):
    outs = [jax.ShapeDtypeStruct(a.shape, a.dtype) for a in arrays]
    aliases = {1 + k: k for k in range(len(arrays))}
    return run(hold_body, layout, place, arrays, outs, [], estimate(4.0), aliases=aliases)


def main_body(layout, place_ref, cols_ref, forward_ref, inverse_ref, known, near_spec, *rest):
    parts, half, sub, span = layout.parts, layout.half, layout.sub, layout.span
    firsts, cross, outs = (rest[k * half : (k + 1) * half] for k in range(3))
    raw, spec, ready, back = rest[3 * half :]
    side, own, _ = where_am_i(place_ref, layout)
    block = parts * sub
    for step in range(half):
        place = jnp.bitwise_xor(own, step)
        raw[rows_at((side * half + place) * sub, sub, sub), :] = firsts[step][1]
        raw[rows_at(((1 - side) * half + place) * sub, sub, sub), :] = cross[step][...]
    chunk = math.gcd(block, 512)

    def transform(index, _):
        forward(raw, spec, index * chunk, index * chunk, chunk, forward_ref)
        return 0

    lax.fori_loop(0, block // chunk, transform, 0)
    group = 16
    zero = (jnp.zeros((group, span), F32),) * 2

    def products(index, first_half):
        def filt(k):
            return spectrum_at(known, k * sub + index * group, group, span)

        def near(k):
            return spectrum_at(near_spec, k * sub + index * group, group, span)

        def far(k):
            return spectrum_at(spec, k * sub + index * group, group, span)

        def store(kind, place, value):
            store_spectrum(ready, (kind * half + place) * sub + index * group, value, group, span)

        before = None
        if first_half:
            for place in range(half):
                total = loop(place + 1, lambda k, t, p=place: add_product(t, filt(k), near(p - k)), zero)
                store(0, place, total if before is None else turned_sum(total, before, 1))
                before = total
            before = None
            for place in range(half, -1, -1):
                total = loop(parts - place, lambda k, t, p=place: add_conjugate(t, filt(k), far(p + k)), zero)
                if before is not None:
                    store(1, place, turned_sum(total, before, -1))
                before = total
        else:
            for place in range(half - 1, -1, -1):
                total = loop(half - place, lambda k, t, p=place: add_conjugate(t, filt(k), near(p + k)), zero)
                store(0, place, total if before is None else turned_sum(total, before, -1))
                before = total
            before = None
            for place in range(half - 1, parts):
                total = loop(place + 1, lambda k, t, p=place: add_product(t, filt(k), far(p - k)), zero)
                if before is not None:
                    store(1, place - half, turned_sum(total, before, 1))
                before = total
        return 0

    @pl.when(side == 0)
    def _():
        lax.fori_loop(0, sub // group, lambda k, _: products(k, True), 0)

    @pl.when(side == 1)
    def _():
        lax.fori_loop(0, sub // group, lambda k, _: products(k, False), 0)

    back[...] = dot(ready[...], inverse_ref[...])
    begin = channel_block(place_ref, layout, 0, 0) * sub
    skip = cols_ref[rows_at(begin, sub, sub), 9:10]
    for step in range(half):
        place = jnp.bitwise_xor(own, step)
        for kind in range(2):
            value = back[rows_at((kind * half + place) * sub, sub, sub), :]
            direct = firsts[step][kind].astype(F32)
            outs[step][kind] = (value + skip * direct).astype(BF16)


def main_half(layout, place, cols, tables, known, near, firsts, cross):
    half, sub, span, parts = layout.half, layout.sub, layout.span, layout.parts
    rows = parts * sub
    return run(
        main_body,
        layout,
        place,
        (cols, *tables, known, near, *firsts, *cross),
        [jax.ShapeDtypeStruct((2, sub, span), BF16)] * half,
        [
            pltpu.VMEM((rows, span), BF16),
            pltpu.VMEM((rows, 2 * span), F32),
            pltpu.VMEM((2 * half * sub, 2 * span), BF16),
            pltpu.VMEM((2 * half * sub, span), F32),
        ],
        estimate(3.0),
    )


def other_body(layout, place_ref, cols_ref, forward_ref, inverse_ref, filt_ref, other_ref, *rest):
    parts, half, sub, span = layout.parts, layout.half, layout.sub, layout.span
    seconds, outs = rest[:half], rest[half : 2 * half]
    raw, spec, ready, back = rest[2 * half :]
    side, own, _ = where_am_i(place_ref, layout)
    rank = place_ref[0]
    block, kind_rows = parts * sub, half * sub
    begin = channel_block(place_ref, layout, 0, 1) * sub
    raw[rows_at(rank * sub, sub, sub), :] = filt_ref[...]
    for step in range(1, parts):
        place = rows_at(jnp.bitwise_xor(rank, step) * sub, sub, sub)
        raw[place, :] = other_ref[(step - 1) * sub : step * sub, :]
    for step in range(half):
        place = block + jnp.bitwise_xor(own, step) * sub
        raw[rows_at(place + side * kind_rows, sub, sub), :] = seconds[step][0]
        raw[rows_at(place + (1 - side) * kind_rows, sub, sub), :] = seconds[step][1]

    def transform(kind, _):
        source = jnp.where(kind == 0, 0, block + (kind - 1) * kind_rows)
        forward(raw, spec, source, kind * kind_rows, kind_rows, forward_ref)
        return 0

    lax.fori_loop(0, 3, transform, 0)
    group = 16
    zero = (jnp.zeros((group, span), F32),) * 2

    def products(index, _):
        def read(kind, k):
            return spectrum_at(spec, (kind * half + k) * sub + index * group, group, span)

        def store(kind, k, value):
            store_spectrum(ready, (kind * half + k) * sub + index * group, value, group, span)

        before = None
        for place in range(half):
            total = loop(place + 1, lambda k, t, p=place: add_product(t, read(0, k), read(1, p - k)), zero)
            store(0, place, total if before is None else turned_sum(total, before, 1))
            before = total
        before = None
        for place in range(half - 1, -1, -1):
            total = loop(half - place, lambda k, t, p=place: add_conjugate(t, read(0, k), read(2, p + k)), zero)
            store(1, place, total if before is None else turned_sum(total, before, -1))
            before = total
        return 0

    lax.fori_loop(0, sub // group, products, 0)
    back[...] = dot(ready[...], inverse_ref[...])
    skip = cols_ref[rows_at(begin, sub, sub), 9:10]
    for step in range(half):
        place = jnp.bitwise_xor(own, step) * sub
        for kind in range(2):
            source = jnp.where(side == kind, 0, 1) * kind_rows + place
            value = back[rows_at(source, sub, sub), :]
            direct = seconds[step][kind].astype(F32)
            outs[step][kind] = (value + skip * direct).astype(BF16)


def other_half(layout, place, cols, tables, filters, other, seconds):
    half, sub, span, parts = layout.half, layout.sub, layout.span, layout.parts
    rows = 3 * half * sub
    return run(
        other_body,
        layout,
        place,
        (cols, *tables, filters, other, *seconds),
        [jax.ShapeDtypeStruct((2, sub, span), BF16)] * half,
        [
            pltpu.VMEM(((parts + 2 * half) * sub, span), BF16),
            pltpu.VMEM((rows, 2 * span), F32),
            pltpu.VMEM((2 * half * sub, 2 * span), BF16),
            pltpu.VMEM((2 * half * sub, span), F32),
        ],
        estimate(3.0),
    )


def results(side, found, crossed, here):
    plain, mixed = found[(0, *here)], found[(1, *here)]
    if crossed is not None:
        mixed = (mixed.astype(F32) + crossed[here].astype(F32)).astype(BF16)
    return jnp.where(side == 0, plain, mixed), jnp.where(side == 0, mixed, plain)


def first_body(layout, place_ref, qkv_main, dout_main, qkv_other, dout_other, *refs):
    half, sub = layout.half, layout.sub
    main, rest, crossed = (refs[k * half : (k + 1) * half] for k in range(3))
    out_ref, grads = refs[3 * half :]
    side, _, _ = where_am_i(place_ref, layout)
    for turn in range(half):
        for other in range(2):
            place = rows_at(channel_block(place_ref, layout, turn, other) * sub, sub, sub)
            qkv, dout_ref = (qkv_other, dout_other) if other else (qkv_main, dout_main)
            here = (slice(None), slice(0, 128))
            pair = results(side, (rest if other else main)[turn], crossed[turn] if other else None, here)
            y_out, dmixed = (f.astype(F32) for f in pair)
            grads[0, place, :] = dout_ref[turn, :, 0:128].astype(F32) * y_out
            grads[1, place, :] = dmixed * qkv[turn, 2, :, 0:128].astype(F32)
            grads[2, place, :] = dmixed * qkv[turn, 1, :, 0:128].astype(F32)
    out_ref[...] = jnp.zeros(out_ref.shape, F32)
    for which in range(3):
        out_ref[2 * which : 2 * which + 2, :] = grads[which].T[0:2, :]


def first_grads(layout, place, gated, main, rest, crossed):
    channels = layout.channels
    return run(
        first_body,
        layout,
        place,
        (*gated, *main, *rest, *crossed),
        jax.ShapeDtypeStruct((8, channels), F32),
        [pltpu.VMEM((3, channels, 128), F32)],
        estimate(1.2),
    )


def final_body(other, layout, place_ref, qkv, dout_ref, split_ref, lanes_ref, keep_ref, *refs):
    half, rows, span = layout.half, layout.sub, layout.span
    found, refs = refs[:half], refs[half:]
    crossed, refs = (refs[:half], refs[half + 2 :]) if other else (None, refs)
    out_hbm, dfeat_hbm, partial, out_ref, dfeat_ref, spread, sems = refs
    most = span - 128
    side, _, _ = where_am_i(place_ref, layout)
    group = min(32, rows)
    keep = [keep_ref[2 + j : 3 + j, :] for j in range(2)]
    copies = []
    for turn in range(half):
        base = channel_block(place_ref, layout, turn, other) * rows
        block = rows_at(base, rows, rows)
        spread[...] = dot(split_ref[block, :], lanes_ref[...])

        def tile(index, _, turn=turn):
            local_rows = rows_at(index * group, group, group)
            pair = results(side, found[turn], crossed and crossed[turn], (local_rows, slice(None)))
            out_ref[turn, local_rows, :] = qkv[turn, 0, local_rows, :] * pair[0]
            y_out, dmixed = (f.astype(F32) for f in pair)
            grads = (
                dout_ref[turn, local_rows, :].astype(F32) * y_out,
                dmixed * qkv[turn, 2, local_rows, :].astype(F32),
                dmixed * qkv[turn, 1, local_rows, :].astype(F32),
            )
            for which in range(3):
                ahead = [pltpu.roll(grads[which], span - 1 - j, 1) * keep[j] for j in range(2)]
                taps = [spread[local_rows, (3 * which + j) * 128 : (3 * which + j + 1) * 128] for j in range(3)]
                for lane in range(0, span, 128):
                    total = taps[0] * grads[which][:, lane : lane + 128]
                    total = total + taps[1] * ahead[0][:, lane : lane + 128] + taps[2] * ahead[1][:, lane : lane + 128]
                    if lane == most:
                        partial[turn, which, local_rows, :] = total
                    else:
                        dfeat_ref[turn, which, local_rows, lane : lane + 128] = total.astype(BF16)
            return 0

        lax.fori_loop(0, rows // group, tile, 0, unroll=min(2, rows // group))
        copies.append(pltpu.make_async_copy(out_ref.at[turn], out_hbm.at[block, :], sems.at[turn, 0]))
        copies.append(
            pltpu.make_async_copy(dfeat_ref.at[turn], dfeat_hbm.at[:, block, pl.ds(0, most)], sems.at[turn, 1])
        )
        for copy in copies[-2:]:
            copy.start()
    for copy in copies:
        copy.wait()


def final(other, layout, place, gated, split, lane_sum, keep, found, crossed, earlier):
    half, span, channels, rows = layout.half, layout.span, layout.channels, layout.sub
    operands = [*gated, split, lane_sum, keep, *found]
    in_specs = [HELD] * len(operands)
    aliases = {}
    if other:
        operands += [*crossed, *earlier]
        in_specs += [HELD] * half + [IN_HBM] * 2
        aliases = {len(operands) - 1: 0, len(operands): 1}
    return run(
        functools.partial(final_body, other),
        layout,
        place,
        operands,
        [
            jax.ShapeDtypeStruct((channels, span), BF16),
            jax.ShapeDtypeStruct((3, channels, span), BF16),
            jax.ShapeDtypeStruct((half, 3, rows, 128), F32),
        ],
        [
            pltpu.VMEM((half, rows, span), BF16),
            pltpu.VMEM((half, 3, rows, span - 128), BF16),
            pltpu.VMEM((rows, 9 * 128), F32),
            pltpu.SemaphoreType.DMA((half, 2)),
        ],
        estimate(3.3),
        in_specs=in_specs,
        out_specs=[IN_HBM, IN_HBM, HELD],
        aliases=aliases,
    )


def finish_body(layout, place_ref, ahead_ref, taps_ref, edge_ref, part_main, part_other, dfeat_in, dfeat_hbm, *refs):
    rows_ref, placed, dfeat_ref, sems = refs
    half, rows, span = layout.half, layout.sub, layout.span
    for which in range(3):
        first, second = (ahead_ref[2 * which + k : 2 * which + k + 1, :] for k in range(2))
        one, two = (taps_ref[3 * which + k : 3 * which + k + 1, :] for k in (1, 2))
        for k, value in enumerate((one * first, two * second, two * first)):
            rows_ref[3 * which + k : 3 * which + k + 1, :] = value
    rows_ref[9:16, :] = jnp.zeros((7, layout.channels), F32)
    split = jnp.concatenate(three_parts(rows_ref[...]), axis=0).T.astype(BF16)
    placed[...] = dot(split, edge_ref[...])
    copies = []
    for turn in range(half):
        for other in range(2):
            block = rows_at(channel_block(place_ref, layout, turn, other) * rows, rows, rows)
            partial = part_other if other else part_main
            for which in range(3):
                value = partial[turn, which] + placed[block, which * 128 : (which + 1) * 128]
                dfeat_ref[which, block, :] = value.astype(BF16)
            target = dfeat_hbm.at[:, block, pl.ds(span - 128, 128)]
            copies.append(pltpu.make_async_copy(dfeat_ref.at[:, block, :], target, sems.at[2 * turn + other]))
            copies[-1].start()
    for copy in copies:
        copy.wait()


def finish(layout, place, ahead, taps_rows, edge, partials, dfeat):
    channels = layout.channels
    return run(
        finish_body,
        layout,
        place,
        (ahead, taps_rows, edge, *partials, dfeat),
        jax.ShapeDtypeStruct(dfeat.shape, BF16),
        [
            pltpu.VMEM((16, channels), F32),
            pltpu.VMEM((channels, 384), F32),
            pltpu.VMEM((3, channels, 128), BF16),
            pltpu.SemaphoreType.DMA((layout.parts,)),
        ],
        estimate(1.9),
        in_specs=[HELD] * 5 + [IN_HBM],
        out_specs=IN_HBM,
        aliases={6: 0},
    )


def swap(value, step, parts, axis="seq"):
    return lax.ppermute(value, axis, [(source, source ^ step) for source in range(parts)])


def around(value, steps, parts):
    return lax.ppermute(value, "seq", [(source, (source + steps) % parts) for source in range(parts)])


def local(features, dout, filters, taps, skip, lengths):
    parts = lax.axis_size("seq")
    _, channels, span = features.shape
    layout = Layout(parts, channels, span)
    half = layout.half
    place = jnp.stack([lax.axis_index("seq"), lax.axis_index("groups")]).astype(jnp.int32)
    tables = [jnp.asarray(t) for t in block_tables(span)]

    features, dout, filters = (pltpu.with_memory_space_constraint(a, pltpu.HBM) for a in (features, dout, filters))

    halo, own_filt, filt = pack(layout, place, features, filters)
    halo, filt = lax.optimization_barrier((around(halo, 1, parts), filt))
    filt = [swap(filt[step - 1], step, parts) for step in range(1, parts)]
    other = swap(jnp.concatenate(filt, axis=0), 1, 2, "groups")
    cols, split, keep, first_edge, last_edge, taps_rows, lanes = small(layout, place, lengths, taps, skip)
    gated_main, gated_other, firsts, cross, seconds = gate(
        layout, place, features, dout, halo, split, lanes, keep, first_edge
    )
    firsts = [firsts[0]] + [swap(firsts[step], step, parts) for step in range(1, half)]
    cross = [swap(cross[step], step + half, parts) for step in range(half)]
    seconds = [seconds[0]] + [swap(seconds[step], step, parts) for step in range(1, half)]

    known = filter_spectra(layout, place, tables[0], own_filt[0], filt)
    sent, near = cross_half(layout, place, tables, known, firsts)
    crossed = hold(layout, place, [swap(sent[step], step + half, parts) for step in range(half)])
    main = main_half(layout, place, cols, tables, known, near, firsts, cross)
    main = [main[0]] + [swap(main[step], step, parts) for step in range(1, half)]
    rest = other_half(layout, place, cols, tables, own_filt[1], other, seconds)
    rest = [rest[0]] + [swap(rest[step], step, parts) for step in range(1, half)]

    taken = (split, lanes, keep)
    out, dfeat, part_main = final(0, layout, place, gated_main, *taken, main, None, None)
    first = first_grads(layout, place, (*gated_main, *gated_other), main, rest, crossed)
    ahead = around(first, -1, parts)
    out, dfeat, part_other = final(1, layout, place, gated_other, *taken, rest, crossed, (out, dfeat))
    return out, finish(layout, place, ahead, taps_rows, last_edge, (part_main, part_other), dfeat)


def solution(mesh):
    in_specs = (
        P(None, ("chan", "sub"), ("groups", "seq")),
        P(("chan", "sub"), ("groups", "seq")),
        P(("chan", "sub"), "seq"),
        P(None, None, ("chan", "sub")),
        P(("chan", "sub")),
        P("groups"),
    )
    out_specs = (P(("chan", "sub"), ("groups", "seq")), P(None, ("chan", "sub"), ("groups", "seq")))
    return jax.shard_map(local, mesh=mesh, in_specs=in_specs, out_specs=out_specs, check_vma=False)
```

```python
import functools
import math

import jax
import jax.numpy as jnp
import numpy as np
from jax import lax
from jax.experimental import pallas as pl
from jax.experimental.pallas import tpu as pltpu
from jax.sharding import PartitionSpec as P

BF16 = jnp.bfloat16
F32 = jnp.float32
SHARE = 0.6
VMEM_LIMIT = 24 * 1024 * 1024
SCALARS = pl.BlockSpec(memory_space=pltpu.SMEM)
IN_HBM = pl.BlockSpec(memory_space=pltpu.HBM)
HELD = pl.BlockSpec(memory_space=pltpu.VMEM)
ANYWHERE = pl.BlockSpec(memory_space=pl.ANY)


def split_bf16(table):
    high = table.astype(np.float32).astype(BF16)
    low = (table - high.astype(np.float64)).astype(np.float32).astype(BF16)
    return high, low


def block_tables(span):
    freq = np.concatenate([np.arange(0, span, 2), np.arange(1, span, 2)])
    angle = np.pi * (2 * freq[None, :] + 1) * np.arange(span)[:, None] / (2 * span)
    forward = np.concatenate([np.cos(angle), -np.sin(angle)], axis=1)
    inverse = np.concatenate([np.cos(angle), -np.sin(angle)], axis=1).T / span
    return np.concatenate(split_bf16(forward), axis=0), split_bf16(inverse)[0]


def dot(a, b):
    return jnp.dot(a, b, preferred_element_type=F32)


def estimate(time_us):
    return pl.CostEstimate(flops=int(SHARE * time_us * 1e9), bytes_accessed=0, transcendentals=0)


def offsets_row(lengths_ref, first, span, ahead):
    position = lax.broadcasted_iota(jnp.int32, (8, span), 1) + (first + ahead)

    def step(genome, carry):
        end, start = carry
        end = end + lengths_ref[genome]
        return end, jnp.where(position >= end, end, start)

    begin = (jnp.int32(0), jnp.zeros((8, span), jnp.int32))
    _, start = lax.fori_loop(0, lengths_ref.shape[0], step, begin)
    return position, position - start


class Layout:
    def __init__(self, parts, channels, span):
        self.parts, self.channels, self.span = parts, channels, span
        self.half = parts // 2
        self.size = channels // self.half
        self.sub = self.size // 2


def where_am_i(place_ref, layout):
    rank, group = place_ref[0], place_ref[1]
    side = rank // layout.half
    return side, rank % layout.half, jnp.where(side == 0, 1 - group, group)


def channel_block(place_ref, layout, turn, other):
    _, own, main = where_am_i(place_ref, layout)
    return jnp.bitwise_xor(own, turn) * 2 + jnp.bitwise_xor(main, other)


def run(body, layout, place, operands, outs, scratch, cost, in_specs=None, out_specs=None, aliases=None):
    single = not isinstance(outs, list)
    return pl.pallas_call(
        functools.partial(body, layout),
        out_shape=outs,
        in_specs=[SCALARS] + (in_specs or [HELD] * len(operands)),
        out_specs=out_specs or (HELD if single else [HELD] * len(outs)),
        scratch_shapes=scratch,
        input_output_aliases=aliases or {},
        compiler_params=pltpu.CompilerParams(vmem_limit_bytes=VMEM_LIMIT),
        cost_estimate=cost,
    )(place, *operands)


def rows_at(begin, step, count):
    return pl.ds(pl.multiple_of(begin, step), count)


def pack_body(layout, place_ref, feat_hbm, filt_hbm, halo_ref, *rest):
    outs, (tail, turned, sems) = rest[:-3], rest[-3:]
    half, sub = layout.half, layout.sub
    copies = [pltpu.make_async_copy(feat_hbm.at[:, :, pl.ds(layout.span - 128, 128)], tail, sems.at[layout.parts + 1])]
    for step in range(layout.parts + 1):
        turn, other = (step % half, step // half) if step else (0, 0)
        if step == layout.parts:
            turn, other = 0, 1
        begin = channel_block(place_ref, layout, turn, other) * sub
        source = filt_hbm.at[rows_at(begin, sub, sub), :]
        copies.append(pltpu.make_async_copy(source, outs[step], sems.at[step]))
    for copy in copies:
        copy.start()
    turned[...] = jnp.zeros(turned.shape, F32)
    copies[0].wait()
    for which in range(3):
        turned[2 * which : 2 * which + 2, :] = tail[which].astype(F32).T[-2:, :]
    halo_ref[...] = turned[...].astype(BF16)
    for copy in copies[1:]:
        copy.wait()


def pack(layout, place, features, filters):
    parts, sub, span, channels = layout.parts, layout.sub, layout.span, layout.channels
    outs = [jax.ShapeDtypeStruct((16, channels), BF16)] + [jax.ShapeDtypeStruct((sub, span), BF16)] * (parts + 1)
    scratch = [
        pltpu.VMEM((3, channels, 128), BF16),
        pltpu.VMEM((16, channels), F32),
        pltpu.SemaphoreType.DMA((parts + 2,)),
    ]
    found = run(pack_body, layout, place, (features, filters), outs, scratch, estimate(2.0), in_specs=[IN_HBM] * 2)
    return found[0], (found[1], found[1 + parts]), found[2 : 1 + parts]


def three_parts(value):
    top = value.astype(BF16).astype(F32)
    middle = (value - top).astype(BF16).astype(F32)
    return [top, middle, value - top - middle]


def edge_table(table_rows, lanes, entries):
    row = lax.broadcasted_iota(jnp.int32, (table_rows, lanes), 0)
    lane = lax.broadcasted_iota(jnp.int32, (table_rows, lanes), 1)
    table = jnp.zeros((table_rows, lanes), F32)
    for rows, where, keep in entries:
        for own_row in rows:
            table = jnp.where((row == own_row) & (lane == where), keep, table)
    return table.astype(BF16)


def small_body(layout, place_ref, lengths_ref, taps_ref, skip_ref, *rest):
    cols_ref, split_ref, keep_ref, fwd_edge_ref, last_edge_ref, turned, lanes_ref = rest
    span = layout.span
    first = place_ref[0] * span
    _, offset = offsets_row(lengths_ref, first, span, 0)
    keep, keep_back = [], []
    for j in (1, 2):
        keep.append((offset[0:1, :] >= j).astype(F32))
        position, later = offsets_row(lengths_ref, first, span, j)
        inside = (position < layout.parts * span) & (later >= j)
        keep_back.append(inside[0:1, :].astype(F32))
    most = span - 128
    lane = lax.broadcasted_iota(jnp.int32, (1, span), 1)
    keep_ref[...] = jnp.zeros(keep_ref.shape, F32)
    for j in (0, 1):
        keep_ref[j : j + 1, :] = jnp.where(lane > j, keep[j], 0.0)
        keep_ref[2 + j : 3 + j, :] = jnp.where(lane < span - 1 - j, keep_back[j], 0.0)
    for which in range(3):
        begin = which * 256
        two, one = [2 * which], [2 * which + 1]
        fwd_edge_ref[:, begin : begin + 128] = edge_table(16, 128, [(one, 0, keep[0][:, :128])])
        fwd_edge_ref[:, begin + 128 : begin + 256] = edge_table(
            16, 128, [(two, 0, keep[1][:, :128]), (one, 1, keep[1][:, :128])]
        )
        entries = []
        for k, (lane_at, j) in enumerate(((127, 0), (127, 1), (126, 1))):
            entries.append(([3 * which + k + 16 * p for p in range(3)], lane_at, keep_back[j][:, most:]))
        last_edge_ref[:, which * 128 : (which + 1) * 128] = edge_table(48, 128, entries)
    turned[...] = jnp.zeros(turned.shape, F32)
    for which in range(3):
        turned[3 * which : 3 * which + 3, :] = taps_ref[which]
    turned[9:10, :] = skip_ref[...]
    value = turned[...]
    cols_ref[...] = value.T
    split_ref[...] = jnp.concatenate(three_parts(value), axis=0).T.astype(BF16)
    column = lax.broadcasted_iota(jnp.int32, (48, 128), 0) % 16
    for k in range(9):
        lanes_ref[:, k * 128 : (k + 1) * 128] = jnp.where(column == k, 1.0, 0.0).astype(BF16)


def small(layout, place, lengths, taps, skip):
    channels, span = layout.channels, layout.span
    shapes = [
        ((channels, 16), F32),
        ((channels, 48), BF16),
        ((8, span), F32),
        ((16, 768), BF16),
        ((48, 384), BF16),
        ((16, channels), F32),
        ((48, 9 * 128), BF16),
    ]
    return run(
        small_body,
        layout,
        place,
        (lengths, taps, skip.reshape(1, channels)),
        [jax.ShapeDtypeStruct(*s) for s in shapes],
        [],
        estimate(1.2),
        in_specs=[SCALARS, HELD, HELD],
    )


def gate_body(layout, place_ref, feat_hbm, dout_hbm, halo_ref, split_ref, lanes_ref, keep_ref, edge_ref, *rest):
    half, rows, span = layout.half, layout.sub, layout.span
    gated, firsts, cross, seconds = (rest[:4], *(rest[4 + k * half : 4 + (k + 1) * half] for k in range(3)))
    feat_ref, ends_of, spread, ends, sems = rest[4 + 3 * half :]
    side, _, _ = where_am_i(place_ref, layout)
    group = min(64, rows)
    steps = [(turn, other) for other in range(2) for turn in range(half)]
    copies = []
    for k, (turn, other) in enumerate(steps):
        block = rows_at(channel_block(place_ref, layout, turn, other) * rows, rows, rows)
        copies.append(pltpu.make_async_copy(feat_hbm.at[:, block, :], feat_ref.at[k], sems.at[k, 0]))
        copies.append(pltpu.make_async_copy(dout_hbm.at[block, :], gated[2 * other + 1].at[turn], sems.at[k, 1]))
        for copy in copies[-2:]:
            copy.start()
    ends_of[...] = halo_ref[...].astype(F32).T.astype(BF16)
    keep = [keep_ref[j : j + 1, :] for j in range(2)]
    for k, (turn, other) in enumerate(steps):
        block = rows_at(channel_block(place_ref, layout, turn, other) * rows, rows, rows)
        qkv_ref, dout_ref = gated[2 * other : 2 * other + 2]
        spread[...] = dot(split_ref[block, :], lanes_ref[...])
        ends[...] = dot(ends_of[block, :], edge_ref[...])
        for copy in copies[2 * k : 2 * k + 2]:
            copy.wait()

        def tile(index, _, k=k, turn=turn, other=other, qkv_ref=qkv_ref, dout_ref=dout_ref):
            local_rows = rows_at(index * group, group, group)
            filtered = []
            for which in range(3):
                value = feat_ref[k, which, local_rows, :].astype(F32)
                moved = [pltpu.roll(value, j + 1, 1) * keep[j] for j in range(2)]
                taps = [spread[local_rows, (3 * which + j) * 128 : (3 * which + j + 1) * 128] for j in range(3)]
                parts = []
                for lane in range(0, span, 128):
                    back = [moved[j][:, lane : lane + 128] for j in range(2)]
                    if lane == 0:
                        begins = [which * 256 + j * 128 for j in range(2)]
                        back = [back[j] + ends[local_rows, begins[j] : begins[j] + 128] for j in range(2)]
                    total = taps[0] * value[:, lane : lane + 128]
                    parts.append((total + taps[1] * back[0] + taps[2] * back[1]).astype(BF16))
                filtered.append(jnp.concatenate(parts, axis=1))
                qkv_ref[turn, which, local_rows, :] = filtered[-1]
            mixed = filtered[1] * filtered[2]
            grad_in = dout_ref[turn, local_rows, :] * filtered[0]
            first = jnp.where(side == 0, mixed, grad_in)
            second = jnp.where(side == 0, grad_in, mixed)
            pair = seconds[turn] if other else firsts[turn]
            pair[0, local_rows, :] = first
            pair[1, local_rows, :] = second
            if other:
                cross[turn][local_rows, :] = first
            return 0

        lax.fori_loop(0, rows // group, tile, 0, unroll=rows // group)


def gate(layout, place, features, dout, halo, split, lanes, keep, edge):
    half, rows, span, channels = layout.half, layout.sub, layout.span, layout.channels
    pair = (2, rows, span)
    shapes = [(half, 3, rows, span), (half, rows, span)] * 2 + [pair] * half + [(rows, span)] * half + [pair] * half
    found = run(
        gate_body,
        layout,
        place,
        (features, dout, halo, split, lanes, keep, edge),
        [jax.ShapeDtypeStruct(s, BF16) for s in shapes],
        [
            pltpu.VMEM((2 * half, 3, rows, span), BF16),
            pltpu.VMEM((channels, 16), BF16),
            pltpu.VMEM((rows, 9 * 128), F32),
            pltpu.VMEM((rows, 768), F32),
            pltpu.SemaphoreType.DMA((2 * half, 2)),
        ],
        estimate(12.0),
        in_specs=[IN_HBM] * 2 + [HELD] * 5,
    )
    return found[0:2], found[2:4], found[4 : 4 + half], found[4 + half : 4 + 2 * half], found[4 + 2 * half :]


def loop(count, body, init):
    if count <= 4:
        for k in range(count):
            init = body(k, init)
        return init
    return lax.fori_loop(0, count, body, init)


def add_product(total, f, x):
    return (total[0] + f[0] * x[0] - f[1] * x[1], total[1] + f[0] * x[1] + f[1] * x[0])


def add_conjugate(total, f, x):
    return (total[0] + f[0] * x[0] + f[1] * x[1], total[1] + f[0] * x[1] - f[1] * x[0])


def turned_sum(spectrum, neighbour, sign):
    half = spectrum[0].shape[1] // 2
    parts = []
    for lanes, flip in ((slice(0, half), sign), (slice(half, None), -sign)):
        n_re, n_im = neighbour[0][:, lanes], neighbour[1][:, lanes]
        s_re, s_im = spectrum[0][:, lanes], spectrum[1][:, lanes]
        parts.append((s_re - n_im, s_im + n_re) if flip > 0 else (s_re + n_im, s_im - n_re))
    return tuple(jnp.concatenate([p[k] for p in parts], axis=1) for k in range(2))


def forward(raw, spec, begin, target, rows, table_ref):
    value = raw[pl.ds(pl.multiple_of(begin, 16), rows), :]
    spec[pl.ds(pl.multiple_of(target, 16), rows), :] = dot(jnp.concatenate([value, value], axis=1), table_ref[...])


def spectrum_at(spec, begin, group, span):
    place = pl.ds(pl.multiple_of(begin, group), group)
    return spec[place, :span], spec[place, span:]


def store_spectrum(ready, begin, value, group, span):
    place = pl.ds(pl.multiple_of(begin, group), group)
    ready[place, :span] = value[0].astype(BF16)
    ready[place, span:] = value[1].astype(BF16)


def filter_body(layout, place_ref, forward_ref, filt_ref, *rest):
    parts, sub = layout.parts, layout.sub
    filt_in, (spec, raw) = rest[: parts - 1], rest[parts - 1 :]
    rank = place_ref[0]
    raw[rows_at(rank * sub, sub, sub), :] = filt_ref[...]
    for step in range(1, parts):
        raw[rows_at(jnp.bitwise_xor(rank, step) * sub, sub, sub), :] = filt_in[step - 1][...]
    chunk = math.gcd(parts * sub, 512)

    def transform(index, _):
        forward(raw, spec, index * chunk, index * chunk, chunk, forward_ref)
        return 0

    lax.fori_loop(0, parts * sub // chunk, transform, 0, unroll=True)


def filter_spectra(layout, place, table, own, filt):
    rows, span = layout.parts * layout.sub, layout.span
    return run(
        filter_body,
        layout,
        place,
        (table, own, *filt),
        jax.ShapeDtypeStruct((rows, 2 * span), F32),
        [pltpu.VMEM((rows, span), BF16)],
        estimate(0.3),
    )


def cross_body(layout, place_ref, forward_ref, inverse_ref, known, *rest):
    parts, half, sub, span = layout.parts, layout.half, layout.sub, layout.span
    signal, outs = rest[:half], rest[half : 2 * half]
    spec, raw, ready, back = rest[2 * half :]
    side, own, _ = where_am_i(place_ref, layout)
    for step in range(half):
        raw[rows_at(jnp.bitwise_xor(own, step) * sub, sub, sub), :] = signal[step][0]
    forward(raw, spec, 0, 0, half * sub, forward_ref)
    group = 16
    zero = (jnp.zeros((group, span), F32),) * 2

    def products(index, ahead):
        def filt(k):
            return spectrum_at(known, k * sub + index * group, group, span)

        def sig(k):
            return spectrum_at(spec, k * sub + index * group, group, span)

        before = None
        if ahead:
            for place in range(half - 1, parts):
                total = loop(half, lambda k, t, p=place: add_product(t, filt(p - k), sig(k)), zero)
                if before is not None:
                    value = turned_sum(total, before, 1)
                    store_spectrum(ready, (place - half) * sub + index * group, value, group, span)
                before = total
        else:
            for place in range(half, -1, -1):
                total = loop(half, lambda k, t, p=place: add_conjugate(t, filt(half + k - p), sig(k)), zero)
                if before is not None:
                    value = turned_sum(total, before, -1)
                    store_spectrum(ready, place * sub + index * group, value, group, span)
                before = total
        return 0

    @pl.when(side == 0)
    def _():
        lax.fori_loop(0, sub // group, lambda k, _: products(k, True), 0, unroll=min(4, sub // group))

    @pl.when(side == 1)
    def _():
        lax.fori_loop(0, sub // group, lambda k, _: products(k, False), 0, unroll=min(4, sub // group))

    back[...] = dot(ready[...], inverse_ref[...])
    for step in range(half):
        outs[step][...] = back[rows_at(jnp.bitwise_xor(own, step) * sub, sub, sub), :].astype(BF16)


def cross_half(layout, place, tables, known, signal):
    half, sub, span = layout.half, layout.sub, layout.span
    rows = half * sub
    found = run(
        cross_body,
        layout,
        place,
        (*tables, known, *signal),
        [jax.ShapeDtypeStruct((sub, span), BF16)] * half + [jax.ShapeDtypeStruct((rows, 2 * span), F32)],
        [
            pltpu.VMEM((rows, span), BF16),
            pltpu.VMEM((rows, 2 * span), BF16),
            pltpu.VMEM((rows, span), F32),
        ],
        estimate(0.3),
    )
    return found[:half], found[half]


def hold_body(layout, place_ref, *refs):
    pass


def hold(layout, place, arrays, after):
    outs = [jax.ShapeDtypeStruct(a.shape, a.dtype) for a in arrays]
    aliases = {1 + k: k for k in range(len(arrays))}
    return run(hold_body, layout, place, [*arrays, after], outs, [], estimate(4.0), aliases=aliases)


def main_body(layout, place_ref, cols_ref, forward_ref, inverse_ref, known, near_spec, *rest):
    parts, half, sub, span = layout.parts, layout.half, layout.sub, layout.span
    firsts, cross, outs = (rest[k * half : (k + 1) * half] for k in range(3))
    raw, spec, ready, back = rest[3 * half :]
    side, own, _ = where_am_i(place_ref, layout)
    block = parts * sub
    for step in range(half):
        place = jnp.bitwise_xor(own, step)
        raw[rows_at((side * half + place) * sub, sub, sub), :] = firsts[step][1]
        raw[rows_at(((1 - side) * half + place) * sub, sub, sub), :] = cross[step][...]
    chunk = math.gcd(block, 512)

    def transform(index, _):
        forward(raw, spec, index * chunk, index * chunk, chunk, forward_ref)
        return 0

    lax.fori_loop(0, block // chunk, transform, 0, unroll=True)
    group = 16
    zero = (jnp.zeros((group, span), F32),) * 2

    def products(index, first_half):
        def filt(k):
            return spectrum_at(known, k * sub + index * group, group, span)

        def near(k):
            return spectrum_at(near_spec, k * sub + index * group, group, span)

        def far(k):
            return spectrum_at(spec, k * sub + index * group, group, span)

        def store(kind, place, value):
            store_spectrum(ready, (kind * half + place) * sub + index * group, value, group, span)

        before = None
        if first_half:
            for place in range(half):
                total = loop(place + 1, lambda k, t, p=place: add_product(t, filt(k), near(p - k)), zero)
                store(0, place, total if before is None else turned_sum(total, before, 1))
                before = total
            before = None
            for place in range(half, -1, -1):
                total = loop(parts - place, lambda k, t, p=place: add_conjugate(t, filt(k), far(p + k)), zero)
                if before is not None:
                    store(1, place, turned_sum(total, before, -1))
                before = total
        else:
            for place in range(half - 1, -1, -1):
                total = loop(half - place, lambda k, t, p=place: add_conjugate(t, filt(k), near(p + k)), zero)
                store(0, place, total if before is None else turned_sum(total, before, -1))
                before = total
            before = None
            for place in range(half - 1, parts):
                total = loop(place + 1, lambda k, t, p=place: add_product(t, filt(k), far(p - k)), zero)
                if before is not None:
                    store(1, place - half, turned_sum(total, before, 1))
                before = total
        return 0

    @pl.when(side == 0)
    def _():
        lax.fori_loop(0, sub // group, lambda k, _: products(k, True), 0, unroll=min(4, sub // group))

    @pl.when(side == 1)
    def _():
        lax.fori_loop(0, sub // group, lambda k, _: products(k, False), 0, unroll=min(4, sub // group))

    back[...] = dot(ready[...], inverse_ref[...])
    begin = channel_block(place_ref, layout, 0, 0) * sub
    skip = cols_ref[rows_at(begin, sub, sub), 9:10]
    for step in range(half):
        place = jnp.bitwise_xor(own, step)
        for kind in range(2):
            value = back[rows_at((kind * half + place) * sub, sub, sub), :]
            direct = firsts[step][kind].astype(F32)
            outs[step][kind] = (value + skip * direct).astype(BF16)


def main_half(layout, place, cols, tables, known, near, firsts, cross):
    half, sub, span, parts = layout.half, layout.sub, layout.span, layout.parts
    rows = parts * sub
    return run(
        main_body,
        layout,
        place,
        (cols, *tables, known, near, *firsts, *cross),
        [jax.ShapeDtypeStruct((2, sub, span), BF16)] * half,
        [
            pltpu.VMEM((rows, span), BF16),
            pltpu.VMEM((rows, 2 * span), F32),
            pltpu.VMEM((2 * half * sub, 2 * span), BF16),
            pltpu.VMEM((2 * half * sub, span), F32),
        ],
        estimate(10.0),
    )


def other_body(layout, place_ref, cols_ref, forward_ref, inverse_ref, filt_ref, other_ref, *rest):
    parts, half, sub, span = layout.parts, layout.half, layout.sub, layout.span
    seconds, early, late = (rest[k * half : (k + 1) * half] for k in range(3))
    raw, spec, ready, back = rest[3 * half :]
    side, own, _ = where_am_i(place_ref, layout)
    rank = place_ref[0]
    block, kind_rows = parts * sub, half * sub
    begin = channel_block(place_ref, layout, 0, 1) * sub
    raw[rows_at(rank * sub, sub, sub), :] = filt_ref[...]
    for step in range(1, parts):
        place = rows_at(jnp.bitwise_xor(rank, step) * sub, sub, sub)
        raw[place, :] = other_ref[(step - 1) * sub : step * sub, :]
    for step in range(half):
        place = block + jnp.bitwise_xor(own, step) * sub
        raw[rows_at(place + side * kind_rows, sub, sub), :] = seconds[step][0]
        raw[rows_at(place + (1 - side) * kind_rows, sub, sub), :] = seconds[step][1]

    def transform(kind, _):
        source = jnp.where(kind == 0, 0, block + (kind - 1) * kind_rows)
        forward(raw, spec, source, kind * kind_rows, kind_rows, forward_ref)
        return 0

    lax.fori_loop(0, 3, transform, 0, unroll=True)
    group = 16
    zero = (jnp.zeros((group, span), F32),) * 2

    def products(index, _):
        def read(kind, k):
            return spectrum_at(spec, (kind * half + k) * sub + index * group, group, span)

        def store(kind, k, value):
            store_spectrum(ready, (kind * half + k) * sub + index * group, value, group, span)

        before = None
        for place in range(half):
            total = loop(place + 1, lambda k, t, p=place: add_product(t, read(0, k), read(1, p - k)), zero)
            store(0, place, total if before is None else turned_sum(total, before, 1))
            before = total
        before = None
        for place in range(half - 1, -1, -1):
            total = loop(half - place, lambda k, t, p=place: add_conjugate(t, read(0, k), read(2, p + k)), zero)
            store(1, place, total if before is None else turned_sum(total, before, -1))
            before = total
        return 0

    lax.fori_loop(0, sub // group, products, 0, unroll=min(4, sub // group))
    back[...] = dot(ready[...], inverse_ref[...])
    skip = cols_ref[rows_at(begin, sub, sub), 9:10]
    for step in range(half):
        place = jnp.bitwise_xor(own, step) * sub
        for kind in range(2):
            source = jnp.where(side == kind, 0, 1) * kind_rows + place
            value = back[rows_at(source, sub, sub), :]
            direct = seconds[step][kind].astype(F32)
            found = (value + skip * direct).astype(BF16)
            early[step][kind] = found[:, :128]
            late[step][kind] = found[:, 128:]


def other_half(layout, place, cols, tables, filters, other, seconds):
    half, sub, span, parts = layout.half, layout.sub, layout.span, layout.parts
    rows = 3 * half * sub
    found = run(
        other_body,
        layout,
        place,
        (cols, *tables, filters, other, *seconds),
        [jax.ShapeDtypeStruct((2, sub, w), BF16) for w in (128, span - 128) for _ in range(half)],
        [
            pltpu.VMEM(((parts + 2 * half) * sub, span), BF16),
            pltpu.VMEM((rows, 2 * span), F32),
            pltpu.VMEM((2 * half * sub, 2 * span), BF16),
            pltpu.VMEM((2 * half * sub, span), F32),
        ],
        estimate(8.0),
    )
    return found[:half], found[half:]


def results(side, found, crossed, here):
    if isinstance(found, tuple):
        plain, mixed = (jnp.concatenate([part[(k, here[0])] for part in found], axis=1) for k in range(2))
    else:
        plain, mixed = found[(0, *here)], found[(1, *here)]
    if crossed is not None:
        mixed = (mixed.astype(F32) + crossed[here].astype(F32)).astype(BF16)
    return jnp.where(side == 0, plain, mixed), jnp.where(side == 0, mixed, plain)


def first_body(layout, place_ref, qkv_main, dout_main, qkv_other, dout_other, *refs):
    half, sub = layout.half, layout.sub
    main, rest, crossed = (refs[k * half : (k + 1) * half] for k in range(3))
    out_ref, grads = refs[3 * half :]
    side, _, _ = where_am_i(place_ref, layout)
    for turn in range(half):
        for other in range(2):
            place = rows_at(channel_block(place_ref, layout, turn, other) * sub, sub, sub)
            qkv, dout_ref = (qkv_other, dout_other) if other else (qkv_main, dout_main)
            here = (slice(None), slice(0, 128))
            pair = results(side, (rest if other else main)[turn], crossed[turn] if other else None, here)
            y_out, dmixed = (f.astype(F32) for f in pair)
            grads[0, place, :] = dout_ref[turn, :, 0:128].astype(F32) * y_out
            grads[1, place, :] = dmixed * qkv[turn, 2, :, 0:128].astype(F32)
            grads[2, place, :] = dmixed * qkv[turn, 1, :, 0:128].astype(F32)
    out_ref[...] = jnp.zeros(out_ref.shape, F32)
    for which in range(3):
        out_ref[2 * which : 2 * which + 2, :] = grads[which].T[0:2, :]


def first_grads(layout, place, gated, main, rest, crossed):
    channels = layout.channels
    return run(
        first_body,
        layout,
        place,
        (*gated, *main, *rest, *crossed),
        jax.ShapeDtypeStruct((8, channels), F32),
        [pltpu.VMEM((3, channels, 128), F32)],
        estimate(6.0),
    )


def final_body(other, layout, place_ref, qkv, dout_ref, split_ref, lanes_ref, keep_ref, *refs):
    half, rows, span = layout.half, layout.sub, layout.span
    found, refs = refs[:half], refs[half:]
    if other:
        found, refs = list(zip(found, refs[:half])), refs[half:]
    crossed, refs = (refs[:half], refs[half + 2 :]) if other else (None, refs)
    out_hbm, dfeat_hbm, partial, out_ref, dfeat_ref, spread, sems = refs
    most = span - 128
    side, _, _ = where_am_i(place_ref, layout)
    group = min(64, rows)
    keep = [keep_ref[2 + j : 3 + j, :] for j in range(2)]
    copies = []
    for turn in range(half):
        base = channel_block(place_ref, layout, turn, other) * rows
        block = rows_at(base, rows, rows)
        spread[...] = dot(split_ref[block, :], lanes_ref[...])

        def tile(index, _, turn=turn):
            local_rows = rows_at(index * group, group, group)
            pair = results(side, found[turn], crossed and crossed[turn], (local_rows, slice(None)))
            out_ref[turn, local_rows, :] = qkv[turn, 0, local_rows, :] * pair[0]
            y_out, dmixed = (f.astype(F32) for f in pair)
            grads = (
                dout_ref[turn, local_rows, :].astype(F32) * y_out,
                dmixed * qkv[turn, 2, local_rows, :].astype(F32),
                dmixed * qkv[turn, 1, local_rows, :].astype(F32),
            )
            for which in range(3):
                ahead = [pltpu.roll(grads[which], span - 1 - j, 1) * keep[j] for j in range(2)]
                taps = [spread[local_rows, (3 * which + j) * 128 : (3 * which + j + 1) * 128] for j in range(3)]
                for lane in range(0, span, 128):
                    total = taps[0] * grads[which][:, lane : lane + 128]
                    total = total + taps[1] * ahead[0][:, lane : lane + 128] + taps[2] * ahead[1][:, lane : lane + 128]
                    if lane == most:
                        partial[turn, which, local_rows, :] = total
                    else:
                        dfeat_ref[turn, which, local_rows, lane : lane + 128] = total.astype(BF16)
            return 0

        lax.fori_loop(0, rows // group, tile, 0, unroll=rows // group)
        copies.append(pltpu.make_async_copy(out_ref.at[turn], out_hbm.at[block, :], sems.at[turn, 0]))
        copies.append(
            pltpu.make_async_copy(dfeat_ref.at[turn], dfeat_hbm.at[:, block, pl.ds(0, most)], sems.at[turn, 1])
        )
        for copy in copies[-2:]:
            copy.start()
    for copy in copies:
        copy.wait()


def final(other, layout, place, gated, split, lane_sum, keep, found, crossed, earlier):
    half, span, channels, rows = layout.half, layout.span, layout.channels, layout.sub
    operands = [*gated, split, lane_sum, keep, *found]
    in_specs = [HELD] * len(operands)
    aliases = {}
    if other:
        operands += [*crossed, *earlier]
        in_specs += [HELD] * half + [IN_HBM] * 2
        aliases = {len(operands) - 1: 0, len(operands): 1}
    return run(
        functools.partial(final_body, other),
        layout,
        place,
        operands,
        [
            jax.ShapeDtypeStruct((channels, span), BF16),
            jax.ShapeDtypeStruct((3, channels, span), BF16),
            jax.ShapeDtypeStruct((half, 3, rows, 128), F32),
        ],
        [
            pltpu.VMEM((half, rows, span), BF16),
            pltpu.VMEM((half, 3, rows, span - 128), BF16),
            pltpu.VMEM((rows, 9 * 128), F32),
            pltpu.SemaphoreType.DMA((half, 2)),
        ],
        estimate(3.3),
        in_specs=in_specs,
        out_specs=[IN_HBM, IN_HBM, HELD],
        aliases=aliases,
    )


def finish_body(layout, place_ref, ahead_ref, taps_ref, edge_ref, part_main, part_other, dfeat_in, dfeat_hbm, *refs):
    rows_ref, placed, dfeat_ref, sems = refs
    half, rows, span = layout.half, layout.sub, layout.span
    for which in range(3):
        first, second = (ahead_ref[2 * which + k : 2 * which + k + 1, :] for k in range(2))
        one, two = (taps_ref[3 * which + k : 3 * which + k + 1, :] for k in (1, 2))
        for k, value in enumerate((one * first, two * second, two * first)):
            rows_ref[3 * which + k : 3 * which + k + 1, :] = value
    rows_ref[9:16, :] = jnp.zeros((7, layout.channels), F32)
    split = jnp.concatenate(three_parts(rows_ref[...]), axis=0).T.astype(BF16)
    placed[...] = dot(split, edge_ref[...])
    copies = []
    for turn in range(half):
        for other in range(2):
            block = rows_at(channel_block(place_ref, layout, turn, other) * rows, rows, rows)
            partial = part_other if other else part_main
            for which in range(3):
                value = partial[turn, which] + placed[block, which * 128 : (which + 1) * 128]
                dfeat_ref[which, block, :] = value.astype(BF16)
            target = dfeat_hbm.at[:, block, pl.ds(span - 128, 128)]
            copies.append(pltpu.make_async_copy(dfeat_ref.at[:, block, :], target, sems.at[2 * turn + other]))
            copies[-1].start()
    for copy in copies:
        copy.wait()


def finish(layout, place, ahead, taps_rows, edge, partials, dfeat):
    channels = layout.channels
    return run(
        finish_body,
        layout,
        place,
        (ahead, taps_rows, edge, *partials, dfeat),
        jax.ShapeDtypeStruct(dfeat.shape, BF16),
        [
            pltpu.VMEM((16, channels), F32),
            pltpu.VMEM((channels, 384), F32),
            pltpu.VMEM((3, channels, 128), BF16),
            pltpu.SemaphoreType.DMA((layout.parts,)),
        ],
        estimate(1.9),
        in_specs=[HELD] * 5 + [IN_HBM],
        out_specs=IN_HBM,
        aliases={6: 0},
    )


def swap(value, step, parts, axis="seq"):
    return lax.ppermute(value, axis, [(source, source ^ step) for source in range(parts)])


def around(value, steps, parts):
    return lax.ppermute(value, "seq", [(source, (source + steps) % parts) for source in range(parts)])


def local(features, dout, filters, taps, skip, lengths):
    parts = lax.axis_size("seq")
    _, channels, span = features.shape
    layout = Layout(parts, channels, span)
    half = layout.half
    place = jnp.stack([lax.axis_index("seq"), lax.axis_index("groups")]).astype(jnp.int32)
    tables = [jnp.asarray(t) for t in block_tables(span)]

    features, dout, filters = (pltpu.with_memory_space_constraint(a, pltpu.HBM) for a in (features, dout, filters))

    halo, own_filt, filt = pack(layout, place, features, filters)
    halo = around(halo, 1, parts)
    filt = [swap(filt[step - 1], step, parts) for step in range(1, parts)]
    other = swap(jnp.concatenate(filt, axis=0), 1, 2, "groups")
    cols, split, keep, first_edge, last_edge, taps_rows, lanes = small(layout, place, lengths, taps, skip)
    gated_main, gated_other, firsts, cross, seconds = gate(
        layout, place, features, dout, halo, split, lanes, keep, first_edge
    )
    firsts = [firsts[0]] + [swap(firsts[step], step, parts) for step in range(1, half)]
    cross = [swap(cross[step], step + half, parts) for step in range(half)]
    seconds = [seconds[0]] + [swap(seconds[step], step, parts) for step in range(1, half)]

    known = filter_spectra(layout, place, tables[0], own_filt[0], filt)
    sent, near = cross_half(layout, place, tables, known, firsts)
    crossed = [swap(sent[step], step + half, parts) for step in range(half)]
    main = main_half(layout, place, cols, tables, known, near, firsts, cross)
    main = [main[0]] + [swap(main[step], step, parts) for step in range(1, half)]
    early, late = other_half(layout, place, cols, tables, own_filt[1], other, seconds)
    crossed = hold(layout, place, crossed, early[0])
    early = [early[0]] + [swap(early[step], step, parts) for step in range(1, half)]
    late = [late[0]] + [swap(late[step], step, parts) for step in range(1, half)]

    taken = (split, lanes, keep)
    out, dfeat, part_main = final(0, layout, place, gated_main, *taken, main, None, None)
    first = first_grads(layout, place, (*gated_main, *gated_other), main, early, crossed)
    ahead = around(first, -1, parts)
    out, dfeat, part_other = final(1, layout, place, gated_other, *taken, [*early, *late], crossed, (out, dfeat))
    return out, finish(layout, place, ahead, taps_rows, last_edge, (part_main, part_other), dfeat)


def solution(mesh):
    in_specs = (
        P(None, ("chan", "sub"), ("groups", "seq")),
        P(("chan", "sub"), ("groups", "seq")),
        P(("chan", "sub"), "seq"),
        P(None, None, ("chan", "sub")),
        P(("chan", "sub")),
        P("groups"),
    )
    out_specs = (P(("chan", "sub"), ("groups", "seq")), P(None, ("chan", "sub"), ("groups", "seq")))
    return jax.shard_map(local, mesh=mesh, in_specs=in_specs, out_specs=out_specs, check_vma=False)
```

```python
import functools
import math

import jax
import jax.numpy as jnp
import numpy as np
from jax import lax
from jax.experimental import pallas as pl
from jax.experimental.pallas import tpu as pltpu
from jax.sharding import PartitionSpec as P

BF16 = jnp.bfloat16
F32 = jnp.float32
SHARE = 0.6
VMEM_LIMIT = 24 * 1024 * 1024
IN_HBM = pl.BlockSpec(memory_space=pltpu.HBM)
HELD = pl.BlockSpec(memory_space=pltpu.VMEM)
ANYWHERE = pl.BlockSpec(memory_space=pl.ANY)


def split_bf16(table):
    high = table.astype(np.float32).astype(BF16)
    low = (table - high.astype(np.float64)).astype(np.float32).astype(BF16)
    return high, low


def block_tables(span):
    freq = np.concatenate([np.arange(0, span, 2), np.arange(1, span, 2)])
    angle = np.pi * (2 * freq[None, :] + 1) * np.arange(span)[:, None] / (2 * span)
    forward = np.concatenate([np.cos(angle), -np.sin(angle)], axis=1)
    inverse = np.concatenate([np.cos(angle), -np.sin(angle)], axis=1).T / span
    return np.concatenate(split_bf16(forward), axis=0), split_bf16(inverse)[0]


def dot(a, b):
    return jnp.dot(a, b, preferred_element_type=F32)


def estimate(time_us):
    return pl.CostEstimate(flops=int(SHARE * time_us * 1e9), bytes_accessed=0, transcendentals=0)


def offsets_row(lengths_ref, first, span, ahead):
    position = lax.broadcasted_iota(jnp.int32, (8, span), 1) + (first + ahead)
    end, start = jnp.zeros((1, 1), jnp.int32), jnp.zeros((8, span), jnp.int32)
    for genome in range(lengths_ref.shape[1]):
        end = end + lengths_ref[:, genome : genome + 1]
        start = jnp.where(position >= end, end, start)
    return position, position - start


class Layout:
    def __init__(self, parts, channels, span):
        self.parts, self.channels, self.span = parts, channels, span
        self.half = parts // 2
        self.size = channels // self.half
        self.sub = self.size // 2


def where_am_i(place_ref, layout):
    rank, group = place_ref[0], place_ref[1]
    side = rank // layout.half
    return side, rank % layout.half, jnp.where(side == 0, 1 - group, group)


def channel_block(place_ref, layout, turn, other):
    _, own, main = where_am_i(place_ref, layout)
    return jnp.bitwise_xor(own, turn) * 2 + jnp.bitwise_xor(main, other)


def run(body, layout, operands, outs, scratch, cost, in_specs=None, out_specs=None, aliases=None):
    single = not isinstance(outs, list)

    def kernel(*refs):
        body(layout, (lax.axis_index("seq"), lax.axis_index("groups")), *refs)

    return pl.pallas_call(
        kernel,
        out_shape=outs,
        in_specs=in_specs or [HELD] * len(operands),
        out_specs=out_specs or (HELD if single else [HELD] * len(outs)),
        scratch_shapes=scratch,
        input_output_aliases=aliases or {},
        compiler_params=pltpu.CompilerParams(vmem_limit_bytes=VMEM_LIMIT),
        cost_estimate=cost,
    )(*operands)


def rows_at(begin, step, count):
    return pl.ds(pl.multiple_of(begin, step), count)


def pack_body(layout, place_ref, feat_hbm, filt_hbm, halo_ref, *rest):
    outs, (tail, turned, sems) = rest[:-3], rest[-3:]
    half, sub = layout.half, layout.sub
    copies = [pltpu.make_async_copy(feat_hbm.at[:, :, pl.ds(layout.span - 128, 128)], tail, sems.at[layout.parts + 1])]
    for step in range(layout.parts + 1):
        turn, other = (step % half, step // half) if step else (0, 0)
        if step == layout.parts:
            turn, other = 0, 1
        begin = channel_block(place_ref, layout, turn, other) * sub
        source = filt_hbm.at[rows_at(begin, sub, sub), :]
        copies.append(pltpu.make_async_copy(source, outs[step], sems.at[step]))
    for copy in copies:
        copy.start()
    turned[...] = jnp.zeros(turned.shape, F32)
    copies[0].wait()
    for which in range(3):
        turned[2 * which : 2 * which + 2, :] = tail[which].astype(F32).T[-2:, :]
    halo_ref[...] = turned[...].astype(BF16)
    for copy in copies[1:]:
        copy.wait()


def pack(layout, features, filters):
    parts, sub, span, channels = layout.parts, layout.sub, layout.span, layout.channels
    outs = [jax.ShapeDtypeStruct((16, channels), BF16)] + [jax.ShapeDtypeStruct((sub, span), BF16)] * (parts + 1)
    scratch = [
        pltpu.VMEM((3, channels, 128), BF16),
        pltpu.VMEM((16, channels), F32),
        pltpu.SemaphoreType.DMA((parts + 2,)),
    ]
    found = run(pack_body, layout, (features, filters), outs, scratch, estimate(2.0), in_specs=[IN_HBM] * 2)
    return found[0], (found[1], found[1 + parts]), found[2 : 1 + parts]


def three_parts(value):
    top = value.astype(BF16).astype(F32)
    middle = (value - top).astype(BF16).astype(F32)
    return [top, middle, value - top - middle]


def edge_table(table_rows, lanes, entries):
    row = lax.broadcasted_iota(jnp.int32, (table_rows, lanes), 0)
    lane = lax.broadcasted_iota(jnp.int32, (table_rows, lanes), 1)
    table = jnp.zeros((table_rows, lanes), F32)
    for rows, where, keep in entries:
        for own_row in rows:
            table = jnp.where((row == own_row) & (lane == where), keep, table)
    return table.astype(BF16)


def fill_tables(layout, place_ref, lengths_ref, taps_ref, skip_ref, fwd_edge_ref, *rest):
    cols_ref, split_ref, keep_ref, last_edge_ref, turned, lanes_ref = rest
    span = layout.span
    first = place_ref[0] * span
    _, offset = offsets_row(lengths_ref, first, span, 0)
    keep, keep_back = [], []
    for j in (1, 2):
        keep.append((offset[0:1, :] >= j).astype(F32))
        position, later = offsets_row(lengths_ref, first, span, j)
        inside = (position < layout.parts * span) & (later >= j)
        keep_back.append(inside[0:1, :].astype(F32))
    most = span - 128
    lane = lax.broadcasted_iota(jnp.int32, (1, span), 1)
    keep_ref[...] = jnp.zeros(keep_ref.shape, F32)
    for j in (0, 1):
        keep_ref[j : j + 1, :] = jnp.where(lane > j, keep[j], 0.0)
        keep_ref[2 + j : 3 + j, :] = jnp.where(lane < span - 1 - j, keep_back[j], 0.0)
    for which in range(3):
        begin = which * 256
        two, one = [2 * which], [2 * which + 1]
        fwd_edge_ref[:, begin : begin + 128] = edge_table(16, 128, [(one, 0, keep[0][:, :128])])
        fwd_edge_ref[:, begin + 128 : begin + 256] = edge_table(
            16, 128, [(two, 0, keep[1][:, :128]), (one, 1, keep[1][:, :128])]
        )
        entries = []
        for k, (lane_at, j) in enumerate(((127, 0), (127, 1), (126, 1))):
            entries.append(([3 * which + k + 16 * p for p in range(3)], lane_at, keep_back[j][:, most:]))
        last_edge_ref[:, which * 128 : (which + 1) * 128] = edge_table(48, 128, entries)
    turned[...] = jnp.zeros(turned.shape, F32)
    for which in range(3):
        turned[3 * which : 3 * which + 3, :] = taps_ref[which]
    turned[9:10, :] = skip_ref[...]
    value = turned[...]
    cols_ref[...] = value.T
    split_ref[...] = jnp.concatenate(three_parts(value), axis=0).T.astype(BF16)
    column = lax.broadcasted_iota(jnp.int32, (48, 128), 0) % 16
    for k in range(9):
        lanes_ref[:, k * 128 : (k + 1) * 128] = jnp.where(column == k, 1.0, 0.0).astype(BF16)


def table_shapes(layout):
    channels = layout.channels
    return [
        ((channels, 16), F32),
        ((channels, 48), BF16),
        ((8, layout.span), F32),
        ((48, 384), BF16),
        ((16, channels), F32),
        ((48, 9 * 128), BF16),
    ]


def gate_body(layout, place_ref, feat_hbm, dout_hbm, halo_ref, lengths_ref, taps_ref, skip_ref, *rest):
    half, rows, span = layout.half, layout.sub, layout.span
    gated, firsts, trails, cross, seconds = (rest[:4], *(rest[4 + k * half : 4 + (k + 1) * half] for k in range(4)))
    tables, (feat_ref, ends_of, spread, ends, edge_ref, sems) = rest[4 + 4 * half : 10 + 4 * half], rest[10 + 4 * half :]
    _, split_ref, keep_ref, _, _, lanes_ref = tables
    side, _, _ = where_am_i(place_ref, layout)
    group = min(64, rows)
    steps = [(turn, other) for other in range(2) for turn in range(half)]
    copies = []
    for k, (turn, other) in enumerate(steps):
        block = rows_at(channel_block(place_ref, layout, turn, other) * rows, rows, rows)
        copies.append(pltpu.make_async_copy(feat_hbm.at[:, block, :], feat_ref.at[k], sems.at[k, 0]))
        copies.append(pltpu.make_async_copy(dout_hbm.at[block, :], gated[2 * other + 1].at[turn], sems.at[k, 1]))
        for copy in copies[-2:]:
            copy.start()
    fill_tables(layout, place_ref, lengths_ref, taps_ref, skip_ref, edge_ref, *tables)
    ends_of[...] = halo_ref[...].astype(F32).T.astype(BF16)
    keep = [keep_ref[j : j + 1, :] for j in range(2)]
    for k, (turn, other) in enumerate(steps):
        block = rows_at(channel_block(place_ref, layout, turn, other) * rows, rows, rows)
        qkv_ref, dout_ref = gated[2 * other : 2 * other + 2]
        spread[...] = dot(split_ref[block, :], lanes_ref[...])
        ends[...] = dot(ends_of[block, :], edge_ref[...])
        for copy in copies[2 * k : 2 * k + 2]:
            copy.wait()

        def tile(index, _, k=k, turn=turn, other=other, qkv_ref=qkv_ref, dout_ref=dout_ref):
            local_rows = rows_at(index * group, group, group)
            filtered = []
            for which in range(3):
                value = feat_ref[k, which, local_rows, :].astype(F32)
                moved = [pltpu.roll(value, j + 1, 1) * keep[j] for j in range(2)]
                taps = [spread[local_rows, (3 * which + j) * 128 : (3 * which + j + 1) * 128] for j in range(3)]
                parts = []
                for lane in range(0, span, 128):
                    back = [moved[j][:, lane : lane + 128] for j in range(2)]
                    if lane == 0:
                        begins = [which * 256 + j * 128 for j in range(2)]
                        back = [back[j] + ends[local_rows, begins[j] : begins[j] + 128] for j in range(2)]
                    total = taps[0] * value[:, lane : lane + 128]
                    parts.append((total + taps[1] * back[0] + taps[2] * back[1]).astype(BF16))
                filtered.append(jnp.concatenate(parts, axis=1))
                qkv_ref[turn, which, local_rows, :] = filtered[-1]
            mixed = filtered[1] * filtered[2]
            grad_in = dout_ref[turn, local_rows, :] * filtered[0]
            first = jnp.where(side == 0, mixed, grad_in)
            second = jnp.where(side == 0, grad_in, mixed)
            if other:
                seconds[turn][0, local_rows, :] = first
                seconds[turn][1, local_rows, :] = second
                cross[turn][local_rows, :] = first
            else:
                firsts[turn][local_rows, :] = first
                trails[turn][local_rows, :] = second
            return 0

        lax.fori_loop(0, rows // group, tile, 0, unroll=rows // group)


def gate(layout, features, dout, halo, lengths, taps, skip):
    half, rows, span, channels = layout.half, layout.sub, layout.span, layout.channels
    pair = (2, rows, span)
    shapes = [(half, 3, rows, span), (half, rows, span)] * 2 + [(rows, span)] * (3 * half) + [pair] * half
    found = run(
        gate_body,
        layout,
        (features, dout, halo, lengths.reshape(1, -1), taps, skip.reshape(1, channels)),
        [jax.ShapeDtypeStruct(s, BF16) for s in shapes] + [jax.ShapeDtypeStruct(*s) for s in table_shapes(layout)],
        [
            pltpu.VMEM((2 * half, 3, rows, span), BF16),
            pltpu.VMEM((channels, 16), BF16),
            pltpu.VMEM((rows, 9 * 128), F32),
            pltpu.VMEM((rows, 768), F32),
            pltpu.VMEM((16, 768), BF16),
            pltpu.SemaphoreType.DMA((2 * half, 2)),
        ],
        estimate(12.0),
        in_specs=[IN_HBM] * 2 + [HELD] * 4,
    )
    return found[0:2], found[2:4], *(found[4 + k * half : 4 + (k + 1) * half] for k in range(4)), found[4 + 4 * half :]


def loop(count, body, init):
    if count <= 4:
        for k in range(count):
            init = body(k, init)
        return init
    return lax.fori_loop(0, count, body, init)


def add_product(total, f, x):
    return (total[0] + f[0] * x[0] - f[1] * x[1], total[1] + f[0] * x[1] + f[1] * x[0])


def add_conjugate(total, f, x):
    return (total[0] + f[0] * x[0] + f[1] * x[1], total[1] + f[0] * x[1] - f[1] * x[0])


def turned_sum(spectrum, neighbour, sign):
    half = spectrum[0].shape[1] // 2
    parts = []
    for lanes, flip in ((slice(0, half), sign), (slice(half, None), -sign)):
        n_re, n_im = neighbour[0][:, lanes], neighbour[1][:, lanes]
        s_re, s_im = spectrum[0][:, lanes], spectrum[1][:, lanes]
        parts.append((s_re - n_im, s_im + n_re) if flip > 0 else (s_re + n_im, s_im - n_re))
    return tuple(jnp.concatenate([p[k] for p in parts], axis=1) for k in range(2))


def forward(raw, spec, begin, target, rows, table_ref):
    value = raw[pl.ds(pl.multiple_of(begin, 16), rows), :]
    spec[pl.ds(pl.multiple_of(target, 16), rows), :] = dot(jnp.concatenate([value, value], axis=1), table_ref[...])


def spectrum_at(spec, begin, group, span):
    place = pl.ds(pl.multiple_of(begin, group), group)
    return spec[place, :span], spec[place, span:]


def store_spectrum(ready, begin, value, group, span):
    place = pl.ds(pl.multiple_of(begin, group), group)
    ready[place, :span] = value[0].astype(BF16)
    ready[place, span:] = value[1].astype(BF16)


def cross_body(layout, place_ref, forward_ref, inverse_ref, filt_ref, *rest):
    parts, half, sub, span = layout.parts, layout.half, layout.sub, layout.span
    filt_in, rest = rest[: parts - 1], rest[parts - 1 :]
    signal, outs = rest[:half], rest[half : 2 * half]
    known, spec, filt_raw, raw, ready, back = rest[2 * half :]
    rank = place_ref[0]
    filt_raw[rows_at(rank * sub, sub, sub), :] = filt_ref[...]
    for step in range(1, parts):
        filt_raw[rows_at(jnp.bitwise_xor(rank, step) * sub, sub, sub), :] = filt_in[step - 1][...]
    chunk = math.gcd(parts * sub, 512)

    def transform(index, _):
        forward(filt_raw, known, index * chunk, index * chunk, chunk, forward_ref)
        return 0

    lax.fori_loop(0, parts * sub // chunk, transform, 0, unroll=True)
    side, own, _ = where_am_i(place_ref, layout)
    for step in range(half):
        raw[rows_at(jnp.bitwise_xor(own, step) * sub, sub, sub), :] = signal[step][...]
    forward(raw, spec, 0, 0, half * sub, forward_ref)
    group = 16
    zero = (jnp.zeros((group, span), F32),) * 2

    def products(index, ahead):
        def filt(k):
            return spectrum_at(known, k * sub + index * group, group, span)

        def sig(k):
            return spectrum_at(spec, k * sub + index * group, group, span)

        before = None
        if ahead:
            for place in range(half - 1, parts):
                total = loop(half, lambda k, t, p=place: add_product(t, filt(p - k), sig(k)), zero)
                if before is not None:
                    value = turned_sum(total, before, 1)
                    store_spectrum(ready, (place - half) * sub + index * group, value, group, span)
                before = total
        else:
            for place in range(half, -1, -1):
                total = loop(half, lambda k, t, p=place: add_conjugate(t, filt(half + k - p), sig(k)), zero)
                if before is not None:
                    value = turned_sum(total, before, -1)
                    store_spectrum(ready, place * sub + index * group, value, group, span)
                before = total
        return 0

    @pl.when(side == 0)
    def _():
        lax.fori_loop(0, sub // group, lambda k, _: products(k, True), 0, unroll=min(4, sub // group))

    @pl.when(side == 1)
    def _():
        lax.fori_loop(0, sub // group, lambda k, _: products(k, False), 0, unroll=min(4, sub // group))

    back[...] = dot(ready[...], inverse_ref[...])
    for step in range(half):
        outs[step][...] = back[rows_at(jnp.bitwise_xor(own, step) * sub, sub, sub), :].astype(BF16)


def cross_half(layout, tables, own, filt, signal):
    half, sub, span = layout.half, layout.sub, layout.span
    all_rows = layout.parts * sub
    rows = half * sub
    found = run(
        cross_body,
        layout,
        (*tables, own, *filt, *signal),
        [jax.ShapeDtypeStruct((sub, span), BF16)] * half
        + [jax.ShapeDtypeStruct((r, 2 * span), F32) for r in (all_rows, rows)],
        [
            pltpu.VMEM((all_rows, span), BF16),
            pltpu.VMEM((rows, span), BF16),
            pltpu.VMEM((rows, 2 * span), BF16),
            pltpu.VMEM((rows, span), F32),
        ],
        estimate(0.3),
    )
    return found[:half], found[half], found[half + 1]


def hold_body(layout, place_ref, *refs):
    pass


def hold(layout, arrays, after):
    outs = [jax.ShapeDtypeStruct(a.shape, a.dtype) for a in arrays]
    aliases = {k: k for k in range(len(arrays))}
    return run(hold_body, layout, [*arrays, after], outs, [], estimate(4.0), aliases=aliases)


def main_body(layout, place_ref, cols_ref, forward_ref, inverse_ref, known, near_spec, *rest):
    parts, half, sub, span = layout.parts, layout.half, layout.sub, layout.span
    firsts, trails, cross, outs = (rest[k * half : (k + 1) * half] for k in range(4))
    raw, spec, ready, back = rest[4 * half :]
    side, own, _ = where_am_i(place_ref, layout)
    block = parts * sub
    for step in range(half):
        place = jnp.bitwise_xor(own, step)
        raw[rows_at((side * half + place) * sub, sub, sub), :] = trails[step][...]
        raw[rows_at(((1 - side) * half + place) * sub, sub, sub), :] = cross[step][...]
    chunk = math.gcd(block, 512)

    def transform(index, _):
        forward(raw, spec, index * chunk, index * chunk, chunk, forward_ref)
        return 0

    lax.fori_loop(0, block // chunk, transform, 0, unroll=True)
    group = 16
    zero = (jnp.zeros((group, span), F32),) * 2

    def products(index, first_half):
        def filt(k):
            return spectrum_at(known, k * sub + index * group, group, span)

        def near(k):
            return spectrum_at(near_spec, k * sub + index * group, group, span)

        def far(k):
            return spectrum_at(spec, k * sub + index * group, group, span)

        def store(kind, place, value):
            store_spectrum(ready, (kind * half + place) * sub + index * group, value, group, span)

        before = None
        if first_half:
            for place in range(half):
                total = loop(place + 1, lambda k, t, p=place: add_product(t, filt(k), near(p - k)), zero)
                store(0, place, total if before is None else turned_sum(total, before, 1))
                before = total
            before = None
            for place in range(half, -1, -1):
                total = loop(parts - place, lambda k, t, p=place: add_conjugate(t, filt(k), far(p + k)), zero)
                if before is not None:
                    store(1, place, turned_sum(total, before, -1))
                before = total
        else:
            for place in range(half - 1, -1, -1):
                total = loop(half - place, lambda k, t, p=place: add_conjugate(t, filt(k), near(p + k)), zero)
                store(0, place, total if before is None else turned_sum(total, before, -1))
                before = total
            before = None
            for place in range(half - 1, parts):
                total = loop(place + 1, lambda k, t, p=place: add_product(t, filt(k), far(p - k)), zero)
                if before is not None:
                    store(1, place - half, turned_sum(total, before, 1))
                before = total
        return 0

    @pl.when(side == 0)
    def _():
        lax.fori_loop(0, sub // group, lambda k, _: products(k, True), 0, unroll=min(4, sub // group))

    @pl.when(side == 1)
    def _():
        lax.fori_loop(0, sub // group, lambda k, _: products(k, False), 0, unroll=min(4, sub // group))

    back[...] = dot(ready[...], inverse_ref[...])
    begin = channel_block(place_ref, layout, 0, 0) * sub
    skip = cols_ref[rows_at(begin, sub, sub), 9:10]
    for step in range(half):
        place = jnp.bitwise_xor(own, step)
        for kind in range(2):
            value = back[rows_at((kind * half + place) * sub, sub, sub), :]
            direct = (trails if kind else firsts)[step][...].astype(F32)
            outs[step][kind] = (value + skip * direct).astype(BF16)


def main_half(layout, cols, tables, known, near, firsts, trails, cross):
    half, sub, span, parts = layout.half, layout.sub, layout.span, layout.parts
    rows = parts * sub
    return run(
        main_body,
        layout,
        (cols, *tables, known, near, *firsts, *trails, *cross),
        [jax.ShapeDtypeStruct((2, sub, span), BF16)] * half,
        [
            pltpu.VMEM((rows, span), BF16),
            pltpu.VMEM((rows, 2 * span), F32),
            pltpu.VMEM((2 * half * sub, 2 * span), BF16),
            pltpu.VMEM((2 * half * sub, span), F32),
        ],
        estimate(10.0),
    )


def other_body(layout, place_ref, cols_ref, forward_ref, inverse_ref, filt_ref, other_ref, *rest):
    parts, half, sub, span = layout.parts, layout.half, layout.sub, layout.span
    seconds, early, late = (rest[k * half : (k + 1) * half] for k in range(3))
    raw, spec, ready, back = rest[3 * half :]
    side, own, _ = where_am_i(place_ref, layout)
    rank = place_ref[0]
    block, kind_rows = parts * sub, half * sub
    begin = channel_block(place_ref, layout, 0, 1) * sub
    raw[rows_at(rank * sub, sub, sub), :] = filt_ref[...]
    for step in range(1, parts):
        place = rows_at(jnp.bitwise_xor(rank, step) * sub, sub, sub)
        raw[place, :] = other_ref[(step - 1) * sub : step * sub, :]
    for step in range(half):
        place = block + jnp.bitwise_xor(own, step) * sub
        raw[rows_at(place + side * kind_rows, sub, sub), :] = seconds[step][0]
        raw[rows_at(place + (1 - side) * kind_rows, sub, sub), :] = seconds[step][1]

    def transform(kind, _):
        source = jnp.where(kind == 0, 0, block + (kind - 1) * kind_rows)
        forward(raw, spec, source, kind * kind_rows, kind_rows, forward_ref)
        return 0

    lax.fori_loop(0, 3, transform, 0, unroll=True)
    group = 16
    zero = (jnp.zeros((group, span), F32),) * 2

    def products(index, _):
        def read(kind, k):
            return spectrum_at(spec, (kind * half + k) * sub + index * group, group, span)

        def store(kind, k, value):
            store_spectrum(ready, (kind * half + k) * sub + index * group, value, group, span)

        before = None
        for place in range(half):
            total = loop(place + 1, lambda k, t, p=place: add_product(t, read(0, k), read(1, p - k)), zero)
            store(0, place, total if before is None else turned_sum(total, before, 1))
            before = total
        before = None
        for place in range(half - 1, -1, -1):
            total = loop(half - place, lambda k, t, p=place: add_conjugate(t, read(0, k), read(2, p + k)), zero)
            store(1, place, total if before is None else turned_sum(total, before, -1))
            before = total
        return 0

    lax.fori_loop(0, sub // group, products, 0, unroll=min(4, sub // group))
    back[...] = dot(ready[...], inverse_ref[...])
    skip = cols_ref[rows_at(begin, sub, sub), 9:10]
    for step in range(half):
        place = jnp.bitwise_xor(own, step) * sub
        for kind in range(2):
            source = jnp.where(side == kind, 0, 1) * kind_rows + place
            value = back[rows_at(source, sub, sub), :]
            direct = seconds[step][kind].astype(F32)
            found = (value + skip * direct).astype(BF16)
            early[step][kind] = found[:, :128]
            late[step][kind] = found[:, 128:]


def other_half(layout, cols, tables, filters, other, seconds):
    half, sub, span, parts = layout.half, layout.sub, layout.span, layout.parts
    rows = 3 * half * sub
    found = run(
        other_body,
        layout,
        (cols, *tables, filters, other, *seconds),
        [jax.ShapeDtypeStruct((2, sub, w), BF16) for w in (128, span - 128) for _ in range(half)],
        [
            pltpu.VMEM(((parts + 2 * half) * sub, span), BF16),
            pltpu.VMEM((rows, 2 * span), F32),
            pltpu.VMEM((2 * half * sub, 2 * span), BF16),
            pltpu.VMEM((2 * half * sub, span), F32),
        ],
        estimate(8.0),
    )
    return found[:half], found[half:]


def results(side, found, crossed, here):
    if isinstance(found, tuple):
        plain, mixed = (jnp.concatenate([part[(k, here[0])] for part in found], axis=1) for k in range(2))
    else:
        plain, mixed = found[(0, *here)], found[(1, *here)]
    if crossed is not None:
        mixed = (mixed.astype(F32) + crossed[here].astype(F32)).astype(BF16)
    return jnp.where(side == 0, plain, mixed), jnp.where(side == 0, mixed, plain)


def first_body(layout, place_ref, qkv_main, dout_main, qkv_other, dout_other, *refs):
    half, sub = layout.half, layout.sub
    main, rest, crossed = (refs[k * half : (k + 1) * half] for k in range(3))
    out_ref, grads = refs[3 * half :]
    side, _, _ = where_am_i(place_ref, layout)
    for turn in range(half):
        for other in range(2):
            place = rows_at(channel_block(place_ref, layout, turn, other) * sub, sub, sub)
            qkv, dout_ref = (qkv_other, dout_other) if other else (qkv_main, dout_main)
            here = (slice(None), slice(0, 128))
            pair = results(side, (rest if other else main)[turn], crossed[turn] if other else None, here)
            y_out, dmixed = (f.astype(F32) for f in pair)
            grads[0, place, :] = dout_ref[turn, :, 0:128].astype(F32) * y_out
            grads[1, place, :] = dmixed * qkv[turn, 2, :, 0:128].astype(F32)
            grads[2, place, :] = dmixed * qkv[turn, 1, :, 0:128].astype(F32)
    out_ref[...] = jnp.zeros(out_ref.shape, F32)
    for which in range(3):
        out_ref[2 * which : 2 * which + 2, :] = grads[which].T[0:2, :]


def first_grads(layout, gated, main, rest, crossed):
    channels = layout.channels
    return run(
        first_body,
        layout,
        (*gated, *main, *rest, *crossed),
        jax.ShapeDtypeStruct((8, channels), F32),
        [pltpu.VMEM((3, channels, 128), F32)],
        estimate(6.0),
    )


def final_body(blocks, chained, layout, place_ref, qkv_main, dout_main, qkv_other, dout_other, split_ref, lanes_ref, keep_ref, *refs):
    rows, span = layout.sub, layout.span
    found = []
    for _, other in blocks:
        count = 3 if other else 1
        found.append(refs[:count])
        refs = refs[count:]
    refs = refs[1 + 2 * chained :]
    out_hbm, dfeat_hbm, partial, out_ref, dfeat_ref, spread, sems = refs
    most = span - 128
    side, _, _ = where_am_i(place_ref, layout)
    group = min(64, rows)
    keep = [keep_ref[2 + j : 3 + j, :] for j in range(2)]
    copies = []
    for k, (turn, other) in enumerate(blocks):
        block = rows_at(channel_block(place_ref, layout, turn, other) * rows, rows, rows)
        qkv, dout_ref = (qkv_other, dout_other) if other else (qkv_main, dout_main)
        source, crossed = (found[k][:2], found[k][2]) if other else (found[k][0], None)
        spread[...] = dot(split_ref[block, :], lanes_ref[...])

        def tile(index, _, k=k, turn=turn, qkv=qkv, dout_ref=dout_ref, source=source, crossed=crossed):
            local_rows = rows_at(index * group, group, group)
            pair = results(side, source, crossed, (local_rows, slice(None)))
            out_ref[k, local_rows, :] = qkv[turn, 0, local_rows, :] * pair[0]
            y_out, dmixed = (f.astype(F32) for f in pair)
            grads = (
                dout_ref[turn, local_rows, :].astype(F32) * y_out,
                dmixed * qkv[turn, 2, local_rows, :].astype(F32),
                dmixed * qkv[turn, 1, local_rows, :].astype(F32),
            )
            for which in range(3):
                ahead = [pltpu.roll(grads[which], span - 1 - j, 1) * keep[j] for j in range(2)]
                taps = [spread[local_rows, (3 * which + j) * 128 : (3 * which + j + 1) * 128] for j in range(3)]
                for lane in range(0, span, 128):
                    total = taps[0] * grads[which][:, lane : lane + 128]
                    total = total + taps[1] * ahead[0][:, lane : lane + 128] + taps[2] * ahead[1][:, lane : lane + 128]
                    if lane == most:
                        partial[k, which, local_rows, :] = total
                    else:
                        dfeat_ref[k, which, local_rows, lane : lane + 128] = total.astype(BF16)
            return 0

        lax.fori_loop(0, rows // group, tile, 0, unroll=rows // group)
        copies.append(pltpu.make_async_copy(out_ref.at[k], out_hbm.at[block, :], sems.at[k, 0]))
        copies.append(pltpu.make_async_copy(dfeat_ref.at[k], dfeat_hbm.at[:, block, pl.ds(0, most)], sems.at[k, 1]))
        for copy in copies[-2:]:
            copy.start()
    for copy in copies:
        copy.wait()


def final(blocks, layout, gated, shared, found, after, earlier):
    span, channels, rows, count = layout.span, layout.channels, layout.sub, len(blocks)
    operands = [*gated, *shared]
    for turn, other in blocks:
        main, early, late, crossed = (f[turn] for f in found)
        operands += [early, late, crossed] if other else [main]
    in_specs = [HELD] * len(operands) + [ANYWHERE]
    operands.append(after)
    aliases = {}
    if earlier:
        operands += earlier
        in_specs += [IN_HBM] * 2
        aliases = {len(operands) - 2: 0, len(operands) - 1: 1}
    return run(
        functools.partial(final_body, blocks, bool(earlier)),
        layout,
        operands,
        [
            jax.ShapeDtypeStruct((channels, span), BF16),
            jax.ShapeDtypeStruct((3, channels, span), BF16),
            jax.ShapeDtypeStruct((count, 3, rows, 128), F32),
        ],
        [
            pltpu.VMEM((count, rows, span), BF16),
            pltpu.VMEM((count, 3, rows, span - 128), BF16),
            pltpu.VMEM((rows, 9 * 128), F32),
            pltpu.SemaphoreType.DMA((count, 2)),
        ],
        estimate(1.2 * count),
        in_specs=in_specs,
        out_specs=[IN_HBM, IN_HBM, HELD],
        aliases=aliases,
    )


def finish_body(lists, layout, place_ref, ahead_ref, taps_ref, edge_ref, *refs):
    partials, refs = refs[: len(lists)], refs[len(lists) + 1 :]
    dfeat_hbm, rows_ref, placed, dfeat_ref, sems = refs
    rows, span = layout.sub, layout.span
    for which in range(3):
        first, second = (ahead_ref[2 * which + k : 2 * which + k + 1, :] for k in range(2))
        one, two = (taps_ref[3 * which + k : 3 * which + k + 1, :] for k in (1, 2))
        for k, value in enumerate((one * first, two * second, two * first)):
            rows_ref[3 * which + k : 3 * which + k + 1, :] = value
    rows_ref[9:16, :] = jnp.zeros((7, layout.channels), F32)
    split = jnp.concatenate(three_parts(rows_ref[...]), axis=0).T.astype(BF16)
    placed[...] = dot(split, edge_ref[...])
    copies = []
    for blocks, partial in zip(lists, partials):
        for k, (turn, other) in enumerate(blocks):
            block = rows_at(channel_block(place_ref, layout, turn, other) * rows, rows, rows)
            for which in range(3):
                value = partial[k, which] + placed[block, which * 128 : (which + 1) * 128]
                dfeat_ref[which, block, :] = value.astype(BF16)
            target = dfeat_hbm.at[:, block, pl.ds(span - 128, 128)]
            copies.append(pltpu.make_async_copy(dfeat_ref.at[:, block, :], target, sems.at[len(copies)]))
            copies[-1].start()
    for copy in copies:
        copy.wait()


def finish(lists, layout, ahead, taps_rows, edge, partials, dfeat):
    channels = layout.channels
    return run(
        functools.partial(finish_body, lists),
        layout,
        (ahead, taps_rows, edge, *partials, dfeat),
        jax.ShapeDtypeStruct(dfeat.shape, BF16),
        [
            pltpu.VMEM((16, channels), F32),
            pltpu.VMEM((channels, 384), F32),
            pltpu.VMEM((3, channels, 128), BF16),
            pltpu.SemaphoreType.DMA((layout.parts,)),
        ],
        estimate(1.9),
        in_specs=[HELD] * (3 + len(lists)) + [IN_HBM],
        out_specs=IN_HBM,
        aliases={3 + len(lists): 0},
    )


def swap(value, step, parts, axis="seq"):
    return lax.ppermute(value, axis, [(source, source ^ step) for source in range(parts)])


def around(value, steps, parts):
    return lax.ppermute(value, "seq", [(source, (source + steps) % parts) for source in range(parts)])


def local(features, dout, filters, taps, skip, lengths):
    parts = lax.axis_size("seq")
    _, channels, span = features.shape
    layout = Layout(parts, channels, span)
    half = layout.half
    tables = [jnp.asarray(t) for t in block_tables(span)]

    features, dout, filters = (pltpu.with_memory_space_constraint(a, pltpu.HBM) for a in (features, dout, filters))

    halo, own_filt, filt = pack(layout, features, filters)
    halo = around(halo, 1, parts)
    filt = [swap(filt[step - 1], step, parts) for step in range(1, parts)]
    other = swap(jnp.concatenate(filt, axis=0), 1, 2, "groups")
    gated_main, gated_other, firsts, trails, cross, seconds, shared = gate(
        layout, features, dout, halo, lengths, taps, skip
    )
    cols, split, keep, last_edge, taps_rows, lanes = shared
    firsts = [firsts[0]] + [swap(firsts[step], step, parts) for step in range(1, half)]
    trails = [trails[0]] + [swap(trails[step], step, parts) for step in range(1, half)]
    cross = [swap(cross[step], step + half, parts) for step in range(half)]
    seconds = [seconds[0]] + [swap(seconds[step], step, parts) for step in range(1, half)]

    sent, known, near = cross_half(layout, tables, own_filt[0], filt, firsts)
    crossed = [swap(sent[step], step + half, parts) for step in range(half)]
    main = main_half(layout, cols, tables, known, near, firsts, trails, cross)
    main = [main[0]] + [swap(main[step], step, parts) for step in range(1, half)]
    early, late = other_half(layout, cols, tables, own_filt[1], other, seconds)
    crossed = hold(layout, crossed, early[0])
    early = [early[0]] + [swap(early[step], step, parts) for step in range(1, half)]
    late = [late[0]] + [swap(late[step], step, parts) for step in range(1, half)]

    gated = (*gated_main, *gated_other)
    found = (main, early, late, crossed)
    shared = (split, lanes, keep)
    lists = [[(0, 0), (0, 1)], [(turn, 0) for turn in range(1, half)], [(turn, 1) for turn in range(1, half)]]
    ahead = around(first_grads(layout, gated, main, early, crossed), -1, parts)
    done, partials, after = (), [], crossed[0]
    for blocks in lists:
        *done, partial = final(blocks, layout, gated, shared, found, after, done)
        partials.append(partial)
        after = partial
    return done[0], finish(lists, layout, ahead, taps_rows, last_edge, partials, done[1])


def solution(mesh):
    in_specs = (
        P(None, ("chan", "sub"), ("groups", "seq")),
        P(("chan", "sub"), ("groups", "seq")),
        P(("chan", "sub"), "seq"),
        P(None, None, ("chan", "sub")),
        P(("chan", "sub")),
        P("groups"),
    )
    out_specs = (P(("chan", "sub"), ("groups", "seq")), P(None, ("chan", "sub"), ("groups", "seq")))
    return jax.shard_map(local, mesh=mesh, in_specs=in_specs, out_specs=out_specs, check_vma=False)
```

```python
import functools
import math

import jax
import jax.numpy as jnp
import numpy as np
from jax import lax
from jax.experimental import pallas as pl
from jax.experimental.pallas import tpu as pltpu
from jax.sharding import PartitionSpec as P

BF16 = jnp.bfloat16
F32 = jnp.float32
GATE_MAIN, GATE_OTHER = 6.0, 1.0
SHARE = 0.6
VMEM_LIMIT = 24 * 1024 * 1024
IN_HBM = pl.BlockSpec(memory_space=pltpu.HBM)
HELD = pl.BlockSpec(memory_space=pltpu.VMEM)
ANYWHERE = pl.BlockSpec(memory_space=pl.ANY)


def split_bf16(table):
    high = table.astype(np.float32).astype(BF16)
    low = (table - high.astype(np.float64)).astype(np.float32).astype(BF16)
    return high, low


def block_tables(span):
    freq = np.concatenate([np.arange(0, span, 2), np.arange(1, span, 2)])
    angle = np.pi * (2 * freq[None, :] + 1) * np.arange(span)[:, None] / (2 * span)
    forward = np.concatenate([np.cos(angle), -np.sin(angle)], axis=1)
    inverse = np.concatenate([np.cos(angle), -np.sin(angle)], axis=1).T / span
    return np.concatenate(split_bf16(forward), axis=0), split_bf16(inverse)[0]


def dot(a, b):
    return jnp.dot(a, b, preferred_element_type=F32)


def estimate(time_us):
    return pl.CostEstimate(flops=int(SHARE * time_us * 1e9), bytes_accessed=0, transcendentals=0)


def offsets_row(lengths_ref, first, span, ahead):
    position = lax.broadcasted_iota(jnp.int32, (8, span), 1) + (first + ahead)
    end, start = jnp.zeros((1, 1), jnp.int32), jnp.zeros((8, span), jnp.int32)
    for genome in range(lengths_ref.shape[1]):
        end = end + lengths_ref[:, genome : genome + 1]
        start = jnp.where(position >= end, end, start)
    return position, position - start


class Layout:
    def __init__(self, parts, channels, span):
        self.parts, self.channels, self.span = parts, channels, span
        self.half = parts // 2
        self.size = channels // self.half
        self.sub = self.size // 2


def where_am_i(place_ref, layout):
    rank, group = place_ref[0], place_ref[1]
    side = rank // layout.half
    return side, rank % layout.half, jnp.where(side == 0, 1 - group, group)


def channel_block(place_ref, layout, turn, other):
    _, own, main = where_am_i(place_ref, layout)
    return jnp.bitwise_xor(own, turn) * 2 + jnp.bitwise_xor(main, other)


def run(body, layout, operands, outs, scratch, cost, in_specs=None, out_specs=None, aliases=None):
    single = not isinstance(outs, list)

    def kernel(*refs):
        body(layout, (lax.axis_index("seq"), lax.axis_index("groups")), *refs)

    return pl.pallas_call(
        kernel,
        out_shape=outs,
        in_specs=in_specs or [HELD] * len(operands),
        out_specs=out_specs or (HELD if single else [HELD] * len(outs)),
        scratch_shapes=scratch,
        input_output_aliases=aliases or {},
        compiler_params=pltpu.CompilerParams(vmem_limit_bytes=VMEM_LIMIT),
        cost_estimate=cost,
    )(*operands)


def rows_at(begin, step, count):
    return pl.ds(pl.multiple_of(begin, step), count)


def pack_body(layout, place_ref, feat_hbm, filt_hbm, halo_ref, *rest):
    outs, (tail, turned, sems) = rest[:-3], rest[-3:]
    half, sub = layout.half, layout.sub
    copies = [pltpu.make_async_copy(feat_hbm.at[:, :, pl.ds(layout.span - 128, 128)], tail, sems.at[layout.parts + 1])]
    for step in range(layout.parts + 1):
        turn, other = (step % half, step // half) if step else (0, 0)
        if step == layout.parts:
            turn, other = 0, 1
        begin = channel_block(place_ref, layout, turn, other) * sub
        source = filt_hbm.at[rows_at(begin, sub, sub), :]
        copies.append(pltpu.make_async_copy(source, outs[step], sems.at[step]))
    for copy in copies:
        copy.start()
    turned[...] = jnp.zeros(turned.shape, F32)
    copies[0].wait()
    for which in range(3):
        turned[2 * which : 2 * which + 2, :] = tail[which].astype(F32).T[-2:, :]
    halo_ref[...] = turned[...].astype(BF16)
    for copy in copies[1:]:
        copy.wait()


def pack(layout, features, filters):
    parts, sub, span, channels = layout.parts, layout.sub, layout.span, layout.channels
    outs = [jax.ShapeDtypeStruct((16, channels), BF16)] + [jax.ShapeDtypeStruct((sub, span), BF16)] * (parts + 1)
    scratch = [
        pltpu.VMEM((3, channels, 128), BF16),
        pltpu.VMEM((16, channels), F32),
        pltpu.SemaphoreType.DMA((parts + 2,)),
    ]
    found = run(pack_body, layout, (features, filters), outs, scratch, estimate(2.0), in_specs=[IN_HBM] * 2)
    return found[0], (found[1], found[1 + parts]), found[2 : 1 + parts]


def three_parts(value):
    top = value.astype(BF16).astype(F32)
    middle = (value - top).astype(BF16).astype(F32)
    return [top, middle, value - top - middle]


def edge_table(table_rows, lanes, entries):
    row = lax.broadcasted_iota(jnp.int32, (table_rows, lanes), 0)
    lane = lax.broadcasted_iota(jnp.int32, (table_rows, lanes), 1)
    table = jnp.zeros((table_rows, lanes), F32)
    for rows, where, keep in entries:
        for own_row in rows:
            table = jnp.where((row == own_row) & (lane == where), keep, table)
    return table.astype(BF16)


def fill_tables(layout, place_ref, lengths_ref, taps_ref, skip_ref, fwd_edge_ref, *rest):
    cols_ref, split_ref, keep_ref, last_edge_ref, turned, lanes_ref = rest
    span = layout.span
    first = place_ref[0] * span
    _, offset = offsets_row(lengths_ref, first, span, 0)
    keep, keep_back = [], []
    for j in (1, 2):
        keep.append((offset[0:1, :] >= j).astype(F32))
        position, later = offsets_row(lengths_ref, first, span, j)
        inside = (position < layout.parts * span) & (later >= j)
        keep_back.append(inside[0:1, :].astype(F32))
    most = span - 128
    lane = lax.broadcasted_iota(jnp.int32, (1, span), 1)
    keep_ref[...] = jnp.zeros(keep_ref.shape, F32)
    for j in (0, 1):
        keep_ref[j : j + 1, :] = jnp.where(lane > j, keep[j], 0.0)
        keep_ref[2 + j : 3 + j, :] = jnp.where(lane < span - 1 - j, keep_back[j], 0.0)
    for which in range(3):
        begin = which * 256
        two, one = [2 * which], [2 * which + 1]
        fwd_edge_ref[:, begin : begin + 128] = edge_table(16, 128, [(one, 0, keep[0][:, :128])])
        fwd_edge_ref[:, begin + 128 : begin + 256] = edge_table(
            16, 128, [(two, 0, keep[1][:, :128]), (one, 1, keep[1][:, :128])]
        )
        entries = []
        for k, (lane_at, j) in enumerate(((127, 0), (127, 1), (126, 1))):
            entries.append(([3 * which + k + 16 * p for p in range(3)], lane_at, keep_back[j][:, most:]))
        last_edge_ref[:, which * 128 : (which + 1) * 128] = edge_table(48, 128, entries)
    turned[...] = jnp.zeros(turned.shape, F32)
    for which in range(3):
        turned[3 * which : 3 * which + 3, :] = taps_ref[which]
    turned[9:10, :] = skip_ref[...]
    value = turned[...]
    cols_ref[...] = value.T
    split_ref[...] = jnp.concatenate(three_parts(value), axis=0).T.astype(BF16)
    column = lax.broadcasted_iota(jnp.int32, (48, 128), 0) % 16
    for k in range(9):
        lanes_ref[:, k * 128 : (k + 1) * 128] = jnp.where(column == k, 1.0, 0.0).astype(BF16)


def table_shapes(layout):
    channels = layout.channels
    return [
        ((channels, 16), F32),
        ((channels, 48), BF16),
        ((8, layout.span), F32),
        ((48, 384), BF16),
        ((16, channels), F32),
        ((48, 9 * 128), BF16),
    ]


def gate_body(other, layout, place_ref, feat_hbm, dout_hbm, *rest):
    half, rows, span = layout.half, layout.sub, layout.span
    given, rest = (rest[:5], rest[5:]) if other else (rest[:4], rest[4:])
    qkv_ref, dout_ref, firsts, seconds = rest[0], rest[1], rest[2 : 2 + half], rest[2 + half : 2 + 2 * half]
    rest = rest[2 + 2 * half :]
    feat_ref, spread, ends, sems = rest[-4:]
    side, _, _ = where_am_i(place_ref, layout)
    group = min(64, rows)
    copies = []
    for turn in range(half):
        block = rows_at(channel_block(place_ref, layout, turn, other) * rows, rows, rows)
        copies.append(pltpu.make_async_copy(feat_hbm.at[:, block, :], feat_ref.at[turn], sems.at[turn, 0]))
        copies.append(pltpu.make_async_copy(dout_hbm.at[block, :], dout_ref.at[turn], sems.at[turn, 1]))
        for copy in copies[-2:]:
            copy.start()
    if other:
        split_ref, keep_ref, lanes_ref, edge_ref, ends_of = given
    else:
        halo_ref, lengths_ref, taps_ref, skip_ref = given
        tables, edge_ref, ends_of = rest[:6], rest[6], rest[7]
        _, split_ref, keep_ref, _, _, lanes_ref = tables
        fill_tables(layout, place_ref, lengths_ref, taps_ref, skip_ref, edge_ref, *tables)
        ends_of[...] = halo_ref[...].astype(F32).T.astype(BF16)
    keep = [keep_ref[j : j + 1, :] for j in range(2)]
    for turn in range(half):
        block = rows_at(channel_block(place_ref, layout, turn, other) * rows, rows, rows)
        spread[...] = dot(split_ref[block, :], lanes_ref[...])
        ends[...] = dot(ends_of[block, :], edge_ref[...])
        for copy in copies[2 * turn : 2 * turn + 2]:
            copy.wait()

        def tile(index, _, turn=turn):
            local_rows = rows_at(index * group, group, group)
            filtered = []
            for which in range(3):
                value = feat_ref[turn, which, local_rows, :].astype(F32)
                moved = [pltpu.roll(value, j + 1, 1) * keep[j] for j in range(2)]
                taps = [spread[local_rows, (3 * which + j) * 128 : (3 * which + j + 1) * 128] for j in range(3)]
                parts = []
                for lane in range(0, span, 128):
                    back = [moved[j][:, lane : lane + 128] for j in range(2)]
                    if lane == 0:
                        begins = [which * 256 + j * 128 for j in range(2)]
                        back = [back[j] + ends[local_rows, begins[j] : begins[j] + 128] for j in range(2)]
                    total = taps[0] * value[:, lane : lane + 128]
                    parts.append((total + taps[1] * back[0] + taps[2] * back[1]).astype(BF16))
                filtered.append(jnp.concatenate(parts, axis=1))
                qkv_ref[turn, which, local_rows, :] = filtered[-1]
            mixed = filtered[1] * filtered[2]
            grad_in = dout_ref[turn, local_rows, :] * filtered[0]
            first = jnp.where(side == 0, mixed, grad_in)
            second = jnp.where(side == 0, grad_in, mixed)
            firsts[turn][local_rows, :] = first
            if other:
                seconds[turn][0, local_rows, :] = first
                seconds[turn][1, local_rows, :] = second
            else:
                seconds[turn][local_rows, :] = second
            return 0

        lax.fori_loop(0, rows // group, tile, 0, unroll=rows // group)


def gate(other, layout, features, dout, *given):
    half, rows, span, channels = layout.half, layout.sub, layout.span, layout.channels
    shapes = [(half, 3, rows, span), (half, rows, span)] + [(rows, span)] * half
    shapes += [(2, rows, span) if other else (rows, span)] * half
    outs = [jax.ShapeDtypeStruct(s, BF16) for s in shapes]
    if not other:
        more = table_shapes(layout) + [((16, 768), BF16), ((channels, 16), BF16)]
        outs += [jax.ShapeDtypeStruct(*s) for s in more]
    found = run(
        functools.partial(gate_body, other),
        layout,
        (features, dout, *given),
        outs,
        [
            pltpu.VMEM((half, 3, rows, span), BF16),
            pltpu.VMEM((rows, 9 * 128), F32),
            pltpu.VMEM((rows, 768), F32),
            pltpu.SemaphoreType.DMA((half, 2)),
        ],
        estimate(GATE_OTHER if other else GATE_MAIN),
        in_specs=[IN_HBM] * 2 + [HELD] * len(given),
    )
    return found[0:2], found[2 : 2 + half], found[2 + half : 2 + 2 * half], found[2 + 2 * half :]


def loop(count, body, init):
    if count <= 4:
        for k in range(count):
            init = body(k, init)
        return init
    return lax.fori_loop(0, count, body, init)


def add_product(total, f, x):
    return (total[0] + f[0] * x[0] - f[1] * x[1], total[1] + f[0] * x[1] + f[1] * x[0])


def add_conjugate(total, f, x):
    return (total[0] + f[0] * x[0] + f[1] * x[1], total[1] + f[0] * x[1] - f[1] * x[0])


def turned_sum(spectrum, neighbour, sign):
    half = spectrum[0].shape[1] // 2
    parts = []
    for lanes, flip in ((slice(0, half), sign), (slice(half, None), -sign)):
        n_re, n_im = neighbour[0][:, lanes], neighbour[1][:, lanes]
        s_re, s_im = spectrum[0][:, lanes], spectrum[1][:, lanes]
        parts.append((s_re - n_im, s_im + n_re) if flip > 0 else (s_re + n_im, s_im - n_re))
    return tuple(jnp.concatenate([p[k] for p in parts], axis=1) for k in range(2))


def forward(raw, spec, begin, target, rows, table_ref):
    value = raw[pl.ds(pl.multiple_of(begin, 16), rows), :]
    spec[pl.ds(pl.multiple_of(target, 16), rows), :] = dot(jnp.concatenate([value, value], axis=1), table_ref[...])


def spectrum_at(spec, begin, group, span):
    place = pl.ds(pl.multiple_of(begin, group), group)
    return spec[place, :span], spec[place, span:]


def store_spectrum(ready, begin, value, group, span):
    place = pl.ds(pl.multiple_of(begin, group), group)
    ready[place, :span] = value[0].astype(BF16)
    ready[place, span:] = value[1].astype(BF16)


def cross_body(layout, place_ref, forward_ref, inverse_ref, filt_ref, *rest):
    parts, half, sub, span = layout.parts, layout.half, layout.sub, layout.span
    filt_in, rest = rest[: parts - 1], rest[parts - 1 :]
    signal, outs = rest[:half], rest[half : 2 * half]
    known, spec, filt_raw, raw, ready, back = rest[2 * half :]
    rank = place_ref[0]
    filt_raw[rows_at(rank * sub, sub, sub), :] = filt_ref[...]
    for step in range(1, parts):
        filt_raw[rows_at(jnp.bitwise_xor(rank, step) * sub, sub, sub), :] = filt_in[step - 1][...]
    chunk = math.gcd(parts * sub, 512)

    def transform(index, _):
        forward(filt_raw, known, index * chunk, index * chunk, chunk, forward_ref)
        return 0

    lax.fori_loop(0, parts * sub // chunk, transform, 0, unroll=True)
    side, own, _ = where_am_i(place_ref, layout)
    for step in range(half):
        raw[rows_at(jnp.bitwise_xor(own, step) * sub, sub, sub), :] = signal[step][...]
    forward(raw, spec, 0, 0, half * sub, forward_ref)
    group = 16
    zero = (jnp.zeros((group, span), F32),) * 2

    def products(index, ahead):
        def filt(k):
            return spectrum_at(known, k * sub + index * group, group, span)

        def sig(k):
            return spectrum_at(spec, k * sub + index * group, group, span)

        before = None
        if ahead:
            for place in range(half - 1, parts):
                total = loop(half, lambda k, t, p=place: add_product(t, filt(p - k), sig(k)), zero)
                if before is not None:
                    value = turned_sum(total, before, 1)
                    store_spectrum(ready, (place - half) * sub + index * group, value, group, span)
                before = total
        else:
            for place in range(half, -1, -1):
                total = loop(half, lambda k, t, p=place: add_conjugate(t, filt(half + k - p), sig(k)), zero)
                if before is not None:
                    value = turned_sum(total, before, -1)
                    store_spectrum(ready, place * sub + index * group, value, group, span)
                before = total
        return 0

    @pl.when(side == 0)
    def _():
        lax.fori_loop(0, sub // group, lambda k, _: products(k, True), 0, unroll=min(4, sub // group))

    @pl.when(side == 1)
    def _():
        lax.fori_loop(0, sub // group, lambda k, _: products(k, False), 0, unroll=min(4, sub // group))

    back[...] = dot(ready[...], inverse_ref[...])
    for step in range(half):
        outs[step][...] = back[rows_at(jnp.bitwise_xor(own, step) * sub, sub, sub), :].astype(BF16)


def cross_half(layout, tables, own, filt, signal):
    half, sub, span = layout.half, layout.sub, layout.span
    all_rows = layout.parts * sub
    rows = half * sub
    found = run(
        cross_body,
        layout,
        (*tables, own, *filt, *signal),
        [jax.ShapeDtypeStruct((sub, span), BF16)] * half
        + [jax.ShapeDtypeStruct((r, 2 * span), F32) for r in (all_rows, rows)],
        [
            pltpu.VMEM((all_rows, span), BF16),
            pltpu.VMEM((rows, span), BF16),
            pltpu.VMEM((rows, 2 * span), BF16),
            pltpu.VMEM((rows, span), F32),
        ],
        estimate(0.3),
    )
    return found[:half], found[half], found[half + 1]


def hold_body(layout, place_ref, *refs):
    count = (len(refs) - 1) // 2
    for source, target in zip(refs[:count], refs[count + 1 :]):
        target[...] = source[...]


def hold(layout, arrays, after):
    outs = [jax.ShapeDtypeStruct(a.shape, a.dtype) for a in arrays]
    return run(hold_body, layout, [*arrays, after], outs, [], estimate(4.0), in_specs=[HELD] * len(arrays) + [ANYWHERE])


def main_body(layout, place_ref, cols_ref, forward_ref, inverse_ref, known, near_spec, *rest):
    parts, half, sub, span = layout.parts, layout.half, layout.sub, layout.span
    firsts, trails, cross, outs = (rest[k * half : (k + 1) * half] for k in range(4))
    raw, spec, ready, back = rest[4 * half :]
    side, own, _ = where_am_i(place_ref, layout)
    block = parts * sub
    for step in range(half):
        place = jnp.bitwise_xor(own, step)
        raw[rows_at((side * half + place) * sub, sub, sub), :] = trails[step][...]
        raw[rows_at(((1 - side) * half + place) * sub, sub, sub), :] = cross[step][...]
    chunk = math.gcd(block, 512)

    def transform(index, _):
        forward(raw, spec, index * chunk, index * chunk, chunk, forward_ref)
        return 0

    lax.fori_loop(0, block // chunk, transform, 0, unroll=True)
    group = 16
    zero = (jnp.zeros((group, span), F32),) * 2

    def products(index, first_half):
        def filt(k):
            return spectrum_at(known, k * sub + index * group, group, span)

        def near(k):
            return spectrum_at(near_spec, k * sub + index * group, group, span)

        def far(k):
            return spectrum_at(spec, k * sub + index * group, group, span)

        def store(kind, place, value):
            store_spectrum(ready, (kind * half + place) * sub + index * group, value, group, span)

        before = None
        if first_half:
            for place in range(half):
                total = loop(place + 1, lambda k, t, p=place: add_product(t, filt(k), near(p - k)), zero)
                store(0, place, total if before is None else turned_sum(total, before, 1))
                before = total
            before = None
            for place in range(half, -1, -1):
                total = loop(parts - place, lambda k, t, p=place: add_conjugate(t, filt(k), far(p + k)), zero)
                if before is not None:
                    store(1, place, turned_sum(total, before, -1))
                before = total
        else:
            for place in range(half - 1, -1, -1):
                total = loop(half - place, lambda k, t, p=place: add_conjugate(t, filt(k), near(p + k)), zero)
                store(0, place, total if before is None else turned_sum(total, before, -1))
                before = total
            before = None
            for place in range(half - 1, parts):
                total = loop(place + 1, lambda k, t, p=place: add_product(t, filt(k), far(p - k)), zero)
                if before is not None:
                    store(1, place - half, turned_sum(total, before, 1))
                before = total
        return 0

    @pl.when(side == 0)
    def _():
        lax.fori_loop(0, sub // group, lambda k, _: products(k, True), 0, unroll=min(4, sub // group))

    @pl.when(side == 1)
    def _():
        lax.fori_loop(0, sub // group, lambda k, _: products(k, False), 0, unroll=min(4, sub // group))

    back[...] = dot(ready[...], inverse_ref[...])
    begin = channel_block(place_ref, layout, 0, 0) * sub
    skip = cols_ref[rows_at(begin, sub, sub), 9:10]
    for step in range(half):
        place = jnp.bitwise_xor(own, step)
        for kind in range(2):
            value = back[rows_at((kind * half + place) * sub, sub, sub), :]
            direct = (trails if kind else firsts)[step][...].astype(F32)
            outs[step][kind] = (value + skip * direct).astype(BF16)


def main_half(layout, cols, tables, known, near, firsts, trails, cross):
    half, sub, span, parts = layout.half, layout.sub, layout.span, layout.parts
    rows = parts * sub
    return run(
        main_body,
        layout,
        (cols, *tables, known, near, *firsts, *trails, *cross),
        [jax.ShapeDtypeStruct((2, sub, span), BF16)] * half,
        [
            pltpu.VMEM((rows, span), BF16),
            pltpu.VMEM((rows, 2 * span), F32),
            pltpu.VMEM((2 * half * sub, 2 * span), BF16),
            pltpu.VMEM((2 * half * sub, span), F32),
        ],
        estimate(10.0),
    )


def other_body(layout, place_ref, cols_ref, forward_ref, inverse_ref, filt_ref, other_ref, *rest):
    parts, half, sub, span = layout.parts, layout.half, layout.sub, layout.span
    seconds, early, late = (rest[k * half : (k + 1) * half] for k in range(3))
    raw, spec, ready, back = rest[3 * half :]
    side, own, _ = where_am_i(place_ref, layout)
    rank = place_ref[0]
    block, kind_rows = parts * sub, half * sub
    begin = channel_block(place_ref, layout, 0, 1) * sub
    raw[rows_at(rank * sub, sub, sub), :] = filt_ref[...]
    for step in range(1, parts):
        place = rows_at(jnp.bitwise_xor(rank, step) * sub, sub, sub)
        raw[place, :] = other_ref[(step - 1) * sub : step * sub, :]
    for step in range(half):
        place = block + jnp.bitwise_xor(own, step) * sub
        raw[rows_at(place + side * kind_rows, sub, sub), :] = seconds[step][0]
        raw[rows_at(place + (1 - side) * kind_rows, sub, sub), :] = seconds[step][1]

    def transform(kind, _):
        source = jnp.where(kind == 0, 0, block + (kind - 1) * kind_rows)
        forward(raw, spec, source, kind * kind_rows, kind_rows, forward_ref)
        return 0

    lax.fori_loop(0, 3, transform, 0, unroll=True)
    group = 16
    zero = (jnp.zeros((group, span), F32),) * 2

    def products(index, _):
        def read(kind, k):
            return spectrum_at(spec, (kind * half + k) * sub + index * group, group, span)

        def store(kind, k, value):
            store_spectrum(ready, (kind * half + k) * sub + index * group, value, group, span)

        before = None
        for place in range(half):
            total = loop(place + 1, lambda k, t, p=place: add_product(t, read(0, k), read(1, p - k)), zero)
            store(0, place, total if before is None else turned_sum(total, before, 1))
            before = total
        before = None
        for place in range(half - 1, -1, -1):
            total = loop(half - place, lambda k, t, p=place: add_conjugate(t, read(0, k), read(2, p + k)), zero)
            store(1, place, total if before is None else turned_sum(total, before, -1))
            before = total
        return 0

    lax.fori_loop(0, sub // group, products, 0, unroll=min(4, sub // group))
    back[...] = dot(ready[...], inverse_ref[...])
    skip = cols_ref[rows_at(begin, sub, sub), 9:10]
    for step in range(half):
        place = jnp.bitwise_xor(own, step) * sub
        for kind in range(2):
            source = jnp.where(side == kind, 0, 1) * kind_rows + place
            value = back[rows_at(source, sub, sub), :]
            direct = seconds[step][kind].astype(F32)
            found = (value + skip * direct).astype(BF16)
            early[step][kind] = found[:, :128]
            late[step][kind] = found[:, 128:]


def other_half(layout, cols, tables, filters, other, seconds):
    half, sub, span, parts = layout.half, layout.sub, layout.span, layout.parts
    rows = 3 * half * sub
    found = run(
        other_body,
        layout,
        (cols, *tables, filters, other, *seconds),
        [jax.ShapeDtypeStruct((2, sub, w), BF16) for w in (128, span - 128) for _ in range(half)],
        [
            pltpu.VMEM(((parts + 2 * half) * sub, span), BF16),
            pltpu.VMEM((rows, 2 * span), F32),
            pltpu.VMEM((2 * half * sub, 2 * span), BF16),
            pltpu.VMEM((2 * half * sub, span), F32),
        ],
        estimate(8.0),
    )
    return found[:half], found[half:]


def results(side, found, crossed, here):
    if isinstance(found, tuple):
        plain, mixed = (jnp.concatenate([part[(k, here[0])] for part in found], axis=1) for k in range(2))
    else:
        plain, mixed = found[(0, *here)], found[(1, *here)]
    if crossed is not None:
        mixed = (mixed.astype(F32) + crossed[here].astype(F32)).astype(BF16)
    return jnp.where(side == 0, plain, mixed), jnp.where(side == 0, mixed, plain)


def first_body(layout, place_ref, qkv_main, dout_main, qkv_other, dout_other, *refs):
    half, sub = layout.half, layout.sub
    main, rest, crossed = (refs[k * half : (k + 1) * half] for k in range(3))
    out_ref, grads = refs[3 * half :]
    side, _, _ = where_am_i(place_ref, layout)
    for turn in range(half):
        for other in range(2):
            place = rows_at(channel_block(place_ref, layout, turn, other) * sub, sub, sub)
            qkv, dout_ref = (qkv_other, dout_other) if other else (qkv_main, dout_main)
            here = (slice(None), slice(0, 128))
            pair = results(side, (rest if other else main)[turn], crossed[turn] if other else None, here)
            y_out, dmixed = (f.astype(F32) for f in pair)
            grads[0, place, :] = dout_ref[turn, :, 0:128].astype(F32) * y_out
            grads[1, place, :] = dmixed * qkv[turn, 2, :, 0:128].astype(F32)
            grads[2, place, :] = dmixed * qkv[turn, 1, :, 0:128].astype(F32)
    out_ref[...] = jnp.zeros(out_ref.shape, F32)
    for which in range(3):
        out_ref[2 * which : 2 * which + 2, :] = grads[which].T[0:2, :]


def first_grads(layout, gated, main, rest, crossed):
    channels = layout.channels
    return run(
        first_body,
        layout,
        (*gated, *main, *rest, *crossed),
        jax.ShapeDtypeStruct((8, channels), F32),
        [pltpu.VMEM((3, channels, 128), F32)],
        estimate(6.0),
    )


def final_body(blocks, chained, layout, place_ref, qkv_main, dout_main, qkv_other, dout_other, split_ref, lanes_ref, keep_ref, *refs):
    rows, span = layout.sub, layout.span
    found = []
    for _, other in blocks:
        count = 3 if other else 1
        found.append(refs[:count])
        refs = refs[count:]
    refs = refs[1 + 2 * chained :]
    out_hbm, dfeat_hbm, partial, out_ref, dfeat_ref, spread, sems = refs
    most = span - 128
    side, _, _ = where_am_i(place_ref, layout)
    group = min(64, rows)
    keep = [keep_ref[2 + j : 3 + j, :] for j in range(2)]
    copies = []
    for k, (turn, other) in enumerate(blocks):
        block = rows_at(channel_block(place_ref, layout, turn, other) * rows, rows, rows)
        qkv, dout_ref = (qkv_other, dout_other) if other else (qkv_main, dout_main)
        source, crossed = (found[k][:2], found[k][2]) if other else (found[k][0], None)
        spread[...] = dot(split_ref[block, :], lanes_ref[...])

        def tile(index, _, k=k, turn=turn, qkv=qkv, dout_ref=dout_ref, source=source, crossed=crossed):
            local_rows = rows_at(index * group, group, group)
            pair = results(side, source, crossed, (local_rows, slice(None)))
            out_ref[k, local_rows, :] = qkv[turn, 0, local_rows, :] * pair[0]
            y_out, dmixed = (f.astype(F32) for f in pair)
            grads = (
                dout_ref[turn, local_rows, :].astype(F32) * y_out,
                dmixed * qkv[turn, 2, local_rows, :].astype(F32),
                dmixed * qkv[turn, 1, local_rows, :].astype(F32),
            )
            for which in range(3):
                ahead = [pltpu.roll(grads[which], span - 1 - j, 1) * keep[j] for j in range(2)]
                taps = [spread[local_rows, (3 * which + j) * 128 : (3 * which + j + 1) * 128] for j in range(3)]
                for lane in range(0, span, 128):
                    total = taps[0] * grads[which][:, lane : lane + 128]
                    total = total + taps[1] * ahead[0][:, lane : lane + 128] + taps[2] * ahead[1][:, lane : lane + 128]
                    if lane == most:
                        partial[k, which, local_rows, :] = total
                    else:
                        dfeat_ref[k, which, local_rows, lane : lane + 128] = total.astype(BF16)
            return 0

        lax.fori_loop(0, rows // group, tile, 0, unroll=rows // group)
        copies.append(pltpu.make_async_copy(out_ref.at[k], out_hbm.at[block, :], sems.at[k, 0]))
        copies.append(pltpu.make_async_copy(dfeat_ref.at[k], dfeat_hbm.at[:, block, pl.ds(0, most)], sems.at[k, 1]))
        for copy in copies[-2:]:
            copy.start()
    for copy in copies:
        copy.wait()


def final(blocks, layout, gated, shared, found, after, earlier):
    span, channels, rows, count = layout.span, layout.channels, layout.sub, len(blocks)
    operands = [*gated, *shared]
    for turn, other in blocks:
        main, early, late, crossed = (f[turn] for f in found)
        operands += [early, late, crossed] if other else [main]
    in_specs = [HELD] * len(operands) + [ANYWHERE]
    operands.append(after)
    aliases = {}
    if earlier:
        operands += earlier
        in_specs += [IN_HBM] * 2
        aliases = {len(operands) - 2: 0, len(operands) - 1: 1}
    return run(
        functools.partial(final_body, blocks, bool(earlier)),
        layout,
        operands,
        [
            jax.ShapeDtypeStruct((channels, span), BF16),
            jax.ShapeDtypeStruct((3, channels, span), BF16),
            jax.ShapeDtypeStruct((count, 3, rows, 128), F32),
        ],
        [
            pltpu.VMEM((count, rows, span), BF16),
            pltpu.VMEM((count, 3, rows, span - 128), BF16),
            pltpu.VMEM((rows, 9 * 128), F32),
            pltpu.SemaphoreType.DMA((count, 2)),
        ],
        estimate(1.2 * count),
        in_specs=in_specs,
        out_specs=[IN_HBM, IN_HBM, HELD],
        aliases=aliases,
    )


def finish_body(lists, layout, place_ref, ahead_ref, taps_ref, edge_ref, *refs):
    partials, refs = refs[: len(lists)], refs[len(lists) + 1 :]
    dfeat_hbm, rows_ref, placed, dfeat_ref, sems = refs
    rows, span = layout.sub, layout.span
    for which in range(3):
        first, second = (ahead_ref[2 * which + k : 2 * which + k + 1, :] for k in range(2))
        one, two = (taps_ref[3 * which + k : 3 * which + k + 1, :] for k in (1, 2))
        for k, value in enumerate((one * first, two * second, two * first)):
            rows_ref[3 * which + k : 3 * which + k + 1, :] = value
    rows_ref[9:16, :] = jnp.zeros((7, layout.channels), F32)
    split = jnp.concatenate(three_parts(rows_ref[...]), axis=0).T.astype(BF16)
    placed[...] = dot(split, edge_ref[...])
    copies = []
    for blocks, partial in zip(lists, partials):
        for k, (turn, other) in enumerate(blocks):
            block = rows_at(channel_block(place_ref, layout, turn, other) * rows, rows, rows)
            for which in range(3):
                value = partial[k, which] + placed[block, which * 128 : (which + 1) * 128]
                dfeat_ref[which, block, :] = value.astype(BF16)
            target = dfeat_hbm.at[:, block, pl.ds(span - 128, 128)]
            copies.append(pltpu.make_async_copy(dfeat_ref.at[:, block, :], target, sems.at[len(copies)]))
            copies[-1].start()
    for copy in copies:
        copy.wait()


def finish(lists, layout, ahead, taps_rows, edge, partials, dfeat):
    channels = layout.channels
    return run(
        functools.partial(finish_body, lists),
        layout,
        (ahead, taps_rows, edge, *partials, dfeat),
        jax.ShapeDtypeStruct(dfeat.shape, BF16),
        [
            pltpu.VMEM((16, channels), F32),
            pltpu.VMEM((channels, 384), F32),
            pltpu.VMEM((3, channels, 128), BF16),
            pltpu.SemaphoreType.DMA((layout.parts,)),
        ],
        estimate(1.9),
        in_specs=[HELD] * (3 + len(lists)) + [IN_HBM],
        out_specs=IN_HBM,
        aliases={3 + len(lists): 0},
    )


def swap(value, step, parts, axis="seq"):
    return lax.ppermute(value, axis, [(source, source ^ step) for source in range(parts)])


def around(value, steps, parts):
    return lax.ppermute(value, "seq", [(source, (source + steps) % parts) for source in range(parts)])


def local(features, dout, filters, taps, skip, lengths):
    parts = lax.axis_size("seq")
    _, channels, span = features.shape
    layout = Layout(parts, channels, span)
    half = layout.half
    tables = [jnp.asarray(t) for t in block_tables(span)]

    features, dout, filters = (pltpu.with_memory_space_constraint(a, pltpu.HBM) for a in (features, dout, filters))

    halo, own_filt, filt = pack(layout, features, filters)
    halo = around(halo, 1, parts)
    filt = [swap(filt[step - 1], step, parts) for step in range(1, parts)]
    other = swap(jnp.concatenate(filt, axis=0), 1, 2, "groups")
    first_given = (halo, lengths.reshape(1, -1), taps, skip.reshape(1, channels))
    gated_main, firsts, trails, shared = gate(0, layout, features, dout, *first_given)
    cols, split, keep, last_edge, taps_rows, lanes, first_edge, ends_of = shared
    gated_other, cross, seconds, _ = gate(1, layout, features, dout, split, keep, lanes, first_edge, ends_of)
    firsts = [firsts[0]] + [swap(firsts[step], step, parts) for step in range(1, half)]
    trails = [trails[0]] + [swap(trails[step], step, parts) for step in range(1, half)]
    cross = [swap(cross[step], step + half, parts) for step in range(half)]
    seconds = [seconds[0]] + [swap(seconds[step], step, parts) for step in range(1, half)]

    sent, known, near = cross_half(layout, tables, own_filt[0], filt, firsts)
    crossed = [swap(sent[step], step + half, parts) for step in range(half)]
    main = main_half(layout, cols, tables, known, near, firsts, trails, cross)
    main = [main[0]] + [swap(main[step], step, parts) for step in range(1, half)]
    early, late = other_half(layout, cols, tables, own_filt[1], other, seconds)
    crossed = hold(layout, crossed, early[0])
    early = [early[0]] + [swap(early[step], step, parts) for step in range(1, half)]
    late = [late[0]] + [swap(late[step], step, parts) for step in range(1, half)]

    gated = (*gated_main, *gated_other)
    found = (main, early, late, crossed)
    shared = (split, lanes, keep)
    lists = [[(0, 0), (0, 1)], [(turn, 0) for turn in range(1, half)], [(turn, 1) for turn in range(1, half)]]
    ahead = around(first_grads(layout, gated, main, early, crossed), -1, parts)
    done, partials, after = (), [], crossed[0]
    for blocks in lists:
        *done, partial = final(blocks, layout, gated, shared, found, after, done)
        partials.append(partial)
        after = partial
    return done[0], finish(lists, layout, ahead, taps_rows, last_edge, partials, done[1])


def solution(mesh):
    in_specs = (
        P(None, ("chan", "sub"), ("groups", "seq")),
        P(("chan", "sub"), ("groups", "seq")),
        P(("chan", "sub"), "seq"),
        P(None, None, ("chan", "sub")),
        P(("chan", "sub")),
        P("groups"),
    )
    out_specs = (P(("chan", "sub"), ("groups", "seq")), P(None, ("chan", "sub"), ("groups", "seq")))
    return jax.shard_map(local, mesh=mesh, in_specs=in_specs, out_specs=out_specs, check_vma=False)
```

```python
import functools
import math

import jax
import jax.numpy as jnp
import numpy as np
from jax import lax
from jax.experimental import pallas as pl
from jax.experimental.pallas import tpu as pltpu
from jax.sharding import PartitionSpec as P

BF16 = jnp.bfloat16
F32 = jnp.float32
GATE_MAIN, GATE_OTHER = 6.0, 1.0
SHARE = 0.6
VMEM_LIMIT = 24 * 1024 * 1024
IN_HBM = pl.BlockSpec(memory_space=pltpu.HBM)
HELD = pl.BlockSpec(memory_space=pltpu.VMEM)
ANYWHERE = pl.BlockSpec(memory_space=pl.ANY)


def split_bf16(table):
    high = table.astype(np.float32).astype(BF16)
    low = (table - high.astype(np.float64)).astype(np.float32).astype(BF16)
    return high, low


def block_tables(span):
    freq = np.concatenate([np.arange(0, span, 2), np.arange(1, span, 2)])
    angle = np.pi * (2 * freq[None, :] + 1) * np.arange(span)[:, None] / (2 * span)
    forward = np.concatenate([np.cos(angle), -np.sin(angle)], axis=1)
    inverse = np.concatenate([np.cos(angle), -np.sin(angle)], axis=1).T / span
    return np.concatenate(split_bf16(forward), axis=0), split_bf16(inverse)[0]


def dot(a, b):
    return jnp.dot(a, b, preferred_element_type=F32)


def estimate(time_us):
    return pl.CostEstimate(flops=int(SHARE * time_us * 1e9), bytes_accessed=0, transcendentals=0)


def offsets_row(lengths_ref, first, span, ahead):
    position = lax.broadcasted_iota(jnp.int32, (8, span), 1) + (first + ahead)
    end, start = jnp.zeros((1, 1), jnp.int32), jnp.zeros((8, span), jnp.int32)
    for genome in range(lengths_ref.shape[1]):
        end = end + lengths_ref[:, genome : genome + 1]
        start = jnp.where(position >= end, end, start)
    return position, position - start


class Layout:
    def __init__(self, parts, channels, span):
        self.parts, self.channels, self.span = parts, channels, span
        self.half = parts // 2
        self.size = channels // self.half
        self.sub = self.size // 2


def where_am_i(place_ref, layout):
    rank, group = place_ref[0], place_ref[1]
    side = rank // layout.half
    return side, rank % layout.half, jnp.where(side == 0, 1 - group, group)


def channel_block(place_ref, layout, turn, other):
    _, own, main = where_am_i(place_ref, layout)
    return jnp.bitwise_xor(own, turn) * 2 + jnp.bitwise_xor(main, other)


def run(body, layout, operands, outs, scratch, cost, in_specs=None, out_specs=None, aliases=None):
    single = not isinstance(outs, list)

    def kernel(*refs):
        body(layout, (lax.axis_index("seq"), lax.axis_index("groups")), *refs)

    return pl.pallas_call(
        kernel,
        out_shape=outs,
        in_specs=in_specs or [HELD] * len(operands),
        out_specs=out_specs or (HELD if single else [HELD] * len(outs)),
        scratch_shapes=scratch,
        input_output_aliases=aliases or {},
        compiler_params=pltpu.CompilerParams(vmem_limit_bytes=VMEM_LIMIT),
        cost_estimate=cost,
    )(*operands)


def rows_at(begin, step, count):
    return pl.ds(pl.multiple_of(begin, step), count)


def pack_body(layout, place_ref, feat_hbm, filt_hbm, halo_ref, *rest):
    outs, (tail, turned, sems) = rest[:-3], rest[-3:]
    half, sub = layout.half, layout.sub
    copies = [pltpu.make_async_copy(feat_hbm.at[:, :, pl.ds(layout.span - 128, 128)], tail, sems.at[layout.parts + 1])]
    for step in range(layout.parts + 1):
        turn, other = (step % half, step // half) if step else (0, 0)
        if step == layout.parts:
            turn, other = 0, 1
        begin = channel_block(place_ref, layout, turn, other) * sub
        source = filt_hbm.at[rows_at(begin, sub, sub), :]
        copies.append(pltpu.make_async_copy(source, outs[step], sems.at[step]))
    for copy in copies:
        copy.start()
    turned[...] = jnp.zeros(turned.shape, F32)
    copies[0].wait()
    for which in range(3):
        turned[2 * which : 2 * which + 2, :] = tail[which].astype(F32).T[-2:, :]
    halo_ref[...] = turned[...].astype(BF16)
    for copy in copies[1:]:
        copy.wait()


def pack(layout, features, filters):
    parts, sub, span, channels = layout.parts, layout.sub, layout.span, layout.channels
    outs = [jax.ShapeDtypeStruct((16, channels), BF16)] + [jax.ShapeDtypeStruct((sub, span), BF16)] * (parts + 1)
    scratch = [
        pltpu.VMEM((3, channels, 128), BF16),
        pltpu.VMEM((16, channels), F32),
        pltpu.SemaphoreType.DMA((parts + 2,)),
    ]
    found = run(pack_body, layout, (features, filters), outs, scratch, estimate(2.0), in_specs=[IN_HBM] * 2)
    return found[0], (found[1], found[1 + parts]), found[2 : 1 + parts]


def three_parts(value):
    top = value.astype(BF16).astype(F32)
    middle = (value - top).astype(BF16).astype(F32)
    return [top, middle, value - top - middle]


def edge_table(table_rows, lanes, entries):
    row = lax.broadcasted_iota(jnp.int32, (table_rows, lanes), 0)
    lane = lax.broadcasted_iota(jnp.int32, (table_rows, lanes), 1)
    table = jnp.zeros((table_rows, lanes), F32)
    for rows, where, keep in entries:
        for own_row in rows:
            table = jnp.where((row == own_row) & (lane == where), keep, table)
    return table.astype(BF16)


def fill_tables(layout, place_ref, lengths_ref, taps_ref, skip_ref, fwd_edge_ref, *rest):
    cols_ref, split_ref, keep_ref, last_edge_ref, turned, lanes_ref = rest
    span = layout.span
    first = place_ref[0] * span
    _, offset = offsets_row(lengths_ref, first, span, 0)
    keep, keep_back = [], []
    for j in (1, 2):
        keep.append((offset[0:1, :] >= j).astype(F32))
        position, later = offsets_row(lengths_ref, first, span, j)
        inside = (position < layout.parts * span) & (later >= j)
        keep_back.append(inside[0:1, :].astype(F32))
    most = span - 128
    lane = lax.broadcasted_iota(jnp.int32, (1, span), 1)
    keep_ref[...] = jnp.zeros(keep_ref.shape, F32)
    for j in (0, 1):
        keep_ref[j : j + 1, :] = jnp.where(lane > j, keep[j], 0.0)
        keep_ref[2 + j : 3 + j, :] = jnp.where(lane < span - 1 - j, keep_back[j], 0.0)
    for which in range(3):
        begin = which * 256
        two, one = [2 * which], [2 * which + 1]
        fwd_edge_ref[:, begin : begin + 128] = edge_table(16, 128, [(one, 0, keep[0][:, :128])])
        fwd_edge_ref[:, begin + 128 : begin + 256] = edge_table(
            16, 128, [(two, 0, keep[1][:, :128]), (one, 1, keep[1][:, :128])]
        )
        entries = []
        for k, (lane_at, j) in enumerate(((127, 0), (127, 1), (126, 1))):
            entries.append(([3 * which + k + 16 * p for p in range(3)], lane_at, keep_back[j][:, most:]))
        last_edge_ref[:, which * 128 : (which + 1) * 128] = edge_table(48, 128, entries)
    turned[...] = jnp.zeros(turned.shape, F32)
    for which in range(3):
        turned[3 * which : 3 * which + 3, :] = taps_ref[which]
    turned[9:10, :] = skip_ref[...]
    value = turned[...]
    cols_ref[...] = value.T
    split_ref[...] = jnp.concatenate(three_parts(value), axis=0).T.astype(BF16)
    column = lax.broadcasted_iota(jnp.int32, (48, 128), 0) % 16
    for k in range(9):
        lanes_ref[:, k * 128 : (k + 1) * 128] = jnp.where(column == k, 1.0, 0.0).astype(BF16)


def table_shapes(layout):
    channels = layout.channels
    return [
        ((channels, 16), F32),
        ((channels, 48), BF16),
        ((8, layout.span), F32),
        ((48, 384), BF16),
        ((16, channels), F32),
        ((48, 9 * 128), BF16),
    ]


def gate_body(other, layout, place_ref, feat_hbm, dout_hbm, *rest):
    half, rows, span = layout.half, layout.sub, layout.span
    given, rest = (rest[:5], rest[5:]) if other else (rest[:4], rest[4:])
    qkv_ref, dout_ref, firsts, seconds = rest[0], rest[1], rest[2 : 2 + half], rest[2 + half : 2 + 2 * half]
    rest = rest[2 + 2 * half :]
    feat_ref, spread, ends, sems = rest[-4:]
    side, _, _ = where_am_i(place_ref, layout)
    group = min(64, rows)
    copies = []
    for turn in range(half):
        block = rows_at(channel_block(place_ref, layout, turn, other) * rows, rows, rows)
        copies.append(pltpu.make_async_copy(feat_hbm.at[:, block, :], feat_ref.at[turn], sems.at[turn, 0]))
        copies.append(pltpu.make_async_copy(dout_hbm.at[block, :], dout_ref.at[turn], sems.at[turn, 1]))
        for copy in copies[-2:]:
            copy.start()
    if other:
        split_ref, keep_ref, lanes_ref, edge_ref, ends_of = given
    else:
        halo_ref, lengths_ref, taps_ref, skip_ref = given
        tables, edge_ref, ends_of = rest[:6], rest[6], rest[7]
        _, split_ref, keep_ref, _, _, lanes_ref = tables
        fill_tables(layout, place_ref, lengths_ref, taps_ref, skip_ref, edge_ref, *tables)
        ends_of[...] = halo_ref[...].astype(F32).T.astype(BF16)
    keep = [keep_ref[j : j + 1, :] for j in range(2)]
    for turn in range(half):
        block = rows_at(channel_block(place_ref, layout, turn, other) * rows, rows, rows)
        spread[...] = dot(split_ref[block, :], lanes_ref[...])
        ends[...] = dot(ends_of[block, :], edge_ref[...])
        for copy in copies[2 * turn : 2 * turn + 2]:
            copy.wait()

        def tile(index, _, turn=turn):
            local_rows = rows_at(index * group, group, group)
            filtered = []
            for which in range(3):
                value = feat_ref[turn, which, local_rows, :].astype(F32)
                moved = [pltpu.roll(value, j + 1, 1) * keep[j] for j in range(2)]
                taps = [spread[local_rows, (3 * which + j) * 128 : (3 * which + j + 1) * 128] for j in range(3)]
                parts = []
                for lane in range(0, span, 128):
                    back = [moved[j][:, lane : lane + 128] for j in range(2)]
                    if lane == 0:
                        begins = [which * 256 + j * 128 for j in range(2)]
                        back = [back[j] + ends[local_rows, begins[j] : begins[j] + 128] for j in range(2)]
                    total = taps[0] * value[:, lane : lane + 128]
                    parts.append((total + taps[1] * back[0] + taps[2] * back[1]).astype(BF16))
                filtered.append(jnp.concatenate(parts, axis=1))
                qkv_ref[turn, which, local_rows, :] = filtered[-1]
            mixed = filtered[1] * filtered[2]
            grad_in = dout_ref[turn, local_rows, :] * filtered[0]
            first = jnp.where(side == 0, mixed, grad_in)
            second = jnp.where(side == 0, grad_in, mixed)
            firsts[turn][local_rows, :] = first
            if other:
                seconds[turn][0, local_rows, :] = first
                seconds[turn][1, local_rows, :] = second
            else:
                seconds[turn][local_rows, :] = second
            return 0

        lax.fori_loop(0, rows // group, tile, 0, unroll=rows // group)


def gate(other, layout, features, dout, *given):
    half, rows, span, channels = layout.half, layout.sub, layout.span, layout.channels
    shapes = [(half, 3, rows, span), (half, rows, span)] + [(rows, span)] * half
    shapes += [(2, rows, span) if other else (rows, span)] * half
    outs = [jax.ShapeDtypeStruct(s, BF16) for s in shapes]
    if not other:
        more = table_shapes(layout) + [((16, 768), BF16), ((channels, 16), BF16)]
        outs += [jax.ShapeDtypeStruct(*s) for s in more]
    found = run(
        functools.partial(gate_body, other),
        layout,
        (features, dout, *given),
        outs,
        [
            pltpu.VMEM((half, 3, rows, span), BF16),
            pltpu.VMEM((rows, 9 * 128), F32),
            pltpu.VMEM((rows, 768), F32),
            pltpu.SemaphoreType.DMA((half, 2)),
        ],
        estimate(GATE_OTHER if other else GATE_MAIN),
        in_specs=[IN_HBM] * 2 + [HELD] * len(given),
    )
    return found[0:2], found[2 : 2 + half], found[2 + half : 2 + 2 * half], found[2 + 2 * half :]


def loop(count, body, init):
    if count <= 4:
        for k in range(count):
            init = body(k, init)
        return init
    return lax.fori_loop(0, count, body, init)


def add_product(total, f, x):
    return (total[0] + f[0] * x[0] - f[1] * x[1], total[1] + f[0] * x[1] + f[1] * x[0])


def add_conjugate(total, f, x):
    return (total[0] + f[0] * x[0] + f[1] * x[1], total[1] + f[0] * x[1] - f[1] * x[0])


def turned_sum(spectrum, neighbour, sign):
    half = spectrum[0].shape[1] // 2
    parts = []
    for lanes, flip in ((slice(0, half), sign), (slice(half, None), -sign)):
        n_re, n_im = neighbour[0][:, lanes], neighbour[1][:, lanes]
        s_re, s_im = spectrum[0][:, lanes], spectrum[1][:, lanes]
        parts.append((s_re - n_im, s_im + n_re) if flip > 0 else (s_re + n_im, s_im - n_re))
    return tuple(jnp.concatenate([p[k] for p in parts], axis=1) for k in range(2))


def forward(raw, spec, begin, target, rows, table_ref):
    value = raw[pl.ds(pl.multiple_of(begin, 16), rows), :]
    spec[pl.ds(pl.multiple_of(target, 16), rows), :] = dot(jnp.concatenate([value, value], axis=1), table_ref[...])


def spectrum_at(spec, begin, group, span):
    place = pl.ds(pl.multiple_of(begin, group), group)
    return spec[place, :span], spec[place, span:]


def store_spectrum(ready, begin, value, group, span):
    place = pl.ds(pl.multiple_of(begin, group), group)
    ready[place, :span] = value[0].astype(BF16)
    ready[place, span:] = value[1].astype(BF16)


def cross_body(layout, place_ref, forward_ref, inverse_ref, filt_ref, *rest):
    parts, half, sub, span = layout.parts, layout.half, layout.sub, layout.span
    filt_in, rest = rest[: parts - 1], rest[parts - 1 :]
    signal, outs = rest[:half], rest[half : 2 * half]
    known, spec, filt_raw, raw, ready, back = rest[2 * half :]
    rank = place_ref[0]
    filt_raw[rows_at(rank * sub, sub, sub), :] = filt_ref[...]
    for step in range(1, parts):
        filt_raw[rows_at(jnp.bitwise_xor(rank, step) * sub, sub, sub), :] = filt_in[step - 1][...]
    chunk = math.gcd(parts * sub, 512)

    def transform(index, _):
        forward(filt_raw, known, index * chunk, index * chunk, chunk, forward_ref)
        return 0

    lax.fori_loop(0, parts * sub // chunk, transform, 0, unroll=True)
    side, own, _ = where_am_i(place_ref, layout)
    for step in range(half):
        raw[rows_at(jnp.bitwise_xor(own, step) * sub, sub, sub), :] = signal[step][...]
    forward(raw, spec, 0, 0, half * sub, forward_ref)
    group = 16
    zero = (jnp.zeros((group, span), F32),) * 2

    def products(index, ahead):
        def filt(k):
            return spectrum_at(known, k * sub + index * group, group, span)

        def sig(k):
            return spectrum_at(spec, k * sub + index * group, group, span)

        before = None
        if ahead:
            for place in range(half - 1, parts):
                total = loop(half, lambda k, t, p=place: add_product(t, filt(p - k), sig(k)), zero)
                if before is not None:
                    value = turned_sum(total, before, 1)
                    store_spectrum(ready, (place - half) * sub + index * group, value, group, span)
                before = total
        else:
            for place in range(half, -1, -1):
                total = loop(half, lambda k, t, p=place: add_conjugate(t, filt(half + k - p), sig(k)), zero)
                if before is not None:
                    value = turned_sum(total, before, -1)
                    store_spectrum(ready, place * sub + index * group, value, group, span)
                before = total
        return 0

    @pl.when(side == 0)
    def _():
        lax.fori_loop(0, sub // group, lambda k, _: products(k, True), 0, unroll=min(4, sub // group))

    @pl.when(side == 1)
    def _():
        lax.fori_loop(0, sub // group, lambda k, _: products(k, False), 0, unroll=min(4, sub // group))

    back[...] = dot(ready[...], inverse_ref[...])
    for step in range(half):
        outs[step][...] = back[rows_at(jnp.bitwise_xor(own, step) * sub, sub, sub), :].astype(BF16)


def cross_half(layout, tables, own, filt, signal):
    half, sub, span = layout.half, layout.sub, layout.span
    all_rows = layout.parts * sub
    rows = half * sub
    found = run(
        cross_body,
        layout,
        (*tables, own, *filt, *signal),
        [jax.ShapeDtypeStruct((sub, span), BF16)] * half
        + [jax.ShapeDtypeStruct((r, 2 * span), F32) for r in (all_rows, rows)],
        [
            pltpu.VMEM((all_rows, span), BF16),
            pltpu.VMEM((rows, span), BF16),
            pltpu.VMEM((rows, 2 * span), BF16),
            pltpu.VMEM((rows, span), F32),
        ],
        estimate(0.3),
    )
    return found[:half], found[half], found[half + 1]


def hold_body(layout, place_ref, *refs):
    count = (len(refs) - 1) // 2
    for source, target in zip(refs[:count], refs[count + 1 :]):
        target[...] = source[...]


def hold(layout, arrays, after):
    outs = [jax.ShapeDtypeStruct(a.shape, a.dtype) for a in arrays]
    return run(hold_body, layout, [*arrays, after], outs, [], estimate(4.0), in_specs=[HELD] * len(arrays) + [ANYWHERE])


def main_body(layout, place_ref, cols_ref, forward_ref, inverse_ref, known, near_spec, *rest):
    parts, half, sub, span = layout.parts, layout.half, layout.sub, layout.span
    firsts, trails, cross, outs = (rest[k * half : (k + 1) * half] for k in range(4))
    raw, spec, ready, back = rest[4 * half :]
    side, own, _ = where_am_i(place_ref, layout)
    block = parts * sub
    for step in range(half):
        place = jnp.bitwise_xor(own, step)
        raw[rows_at((side * half + place) * sub, sub, sub), :] = trails[step][...]
        raw[rows_at(((1 - side) * half + place) * sub, sub, sub), :] = cross[step][...]
    chunk = math.gcd(block, 512)

    def transform(index, _):
        forward(raw, spec, index * chunk, index * chunk, chunk, forward_ref)
        return 0

    lax.fori_loop(0, block // chunk, transform, 0, unroll=True)
    group = 16
    zero = (jnp.zeros((group, span), F32),) * 2

    def products(index, first_half):
        def filt(k):
            return spectrum_at(known, k * sub + index * group, group, span)

        def near(k):
            return spectrum_at(near_spec, k * sub + index * group, group, span)

        def far(k):
            return spectrum_at(spec, k * sub + index * group, group, span)

        def store(kind, place, value):
            store_spectrum(ready, (kind * half + place) * sub + index * group, value, group, span)

        before = None
        if first_half:
            for place in range(half):
                total = loop(place + 1, lambda k, t, p=place: add_product(t, filt(k), near(p - k)), zero)
                store(0, place, total if before is None else turned_sum(total, before, 1))
                before = total
            before = None
            for place in range(half, -1, -1):
                total = loop(parts - place, lambda k, t, p=place: add_conjugate(t, filt(k), far(p + k)), zero)
                if before is not None:
                    store(1, place, turned_sum(total, before, -1))
                before = total
        else:
            for place in range(half - 1, -1, -1):
                total = loop(half - place, lambda k, t, p=place: add_conjugate(t, filt(k), near(p + k)), zero)
                store(0, place, total if before is None else turned_sum(total, before, -1))
                before = total
            before = None
            for place in range(half - 1, parts):
                total = loop(place + 1, lambda k, t, p=place: add_product(t, filt(k), far(p - k)), zero)
                if before is not None:
                    store(1, place - half, turned_sum(total, before, 1))
                before = total
        return 0

    @pl.when(side == 0)
    def _():
        lax.fori_loop(0, sub // group, lambda k, _: products(k, True), 0, unroll=min(4, sub // group))

    @pl.when(side == 1)
    def _():
        lax.fori_loop(0, sub // group, lambda k, _: products(k, False), 0, unroll=min(4, sub // group))

    back[...] = dot(ready[...], inverse_ref[...])
    begin = channel_block(place_ref, layout, 0, 0) * sub
    skip = cols_ref[rows_at(begin, sub, sub), 9:10]
    for step in range(half):
        place = jnp.bitwise_xor(own, step)
        for kind in range(2):
            value = back[rows_at((kind * half + place) * sub, sub, sub), :]
            direct = (trails if kind else firsts)[step][...].astype(F32)
            outs[step][kind] = (value + skip * direct).astype(BF16)


def main_half(layout, cols, tables, known, near, firsts, trails, cross):
    half, sub, span, parts = layout.half, layout.sub, layout.span, layout.parts
    rows = parts * sub
    return run(
        main_body,
        layout,
        (cols, *tables, known, near, *firsts, *trails, *cross),
        [jax.ShapeDtypeStruct((2, sub, span), BF16)] * half,
        [
            pltpu.VMEM((rows, span), BF16),
            pltpu.VMEM((rows, 2 * span), F32),
            pltpu.VMEM((2 * half * sub, 2 * span), BF16),
            pltpu.VMEM((2 * half * sub, span), F32),
        ],
        estimate(10.0),
    )


def pick_first(value):
    row = lax.broadcasted_iota(jnp.int32, (16, 128), 0)
    lane = lax.broadcasted_iota(jnp.int32, (16, 128), 1)
    table = jnp.where((row == lane) & (row < 2), 1.0, 0.0).astype(BF16)
    dims = (((1,), (1,)), ((), ()))
    return lax.dot_general(table, value, dims, preferred_element_type=F32).astype(BF16)


def other_body(layout, place_ref, cols_ref, forward_ref, inverse_ref, filt_ref, other_ref, *rest):
    parts, half, sub, span = layout.parts, layout.half, layout.sub, layout.span
    seconds, leads, outs = (rest[k * half : (k + 1) * half] for k in range(3))
    raw, spec, ready, back = rest[3 * half :]
    side, own, _ = where_am_i(place_ref, layout)
    rank = place_ref[0]
    block, kind_rows = parts * sub, half * sub
    begin = channel_block(place_ref, layout, 0, 1) * sub
    raw[rows_at(rank * sub, sub, sub), :] = filt_ref[...]
    for step in range(1, parts):
        place = rows_at(jnp.bitwise_xor(rank, step) * sub, sub, sub)
        raw[place, :] = other_ref[(step - 1) * sub : step * sub, :]
    for step in range(half):
        place = block + jnp.bitwise_xor(own, step) * sub
        raw[rows_at(place + side * kind_rows, sub, sub), :] = seconds[step][0]
        raw[rows_at(place + (1 - side) * kind_rows, sub, sub), :] = seconds[step][1]

    def transform(kind, _):
        source = jnp.where(kind == 0, 0, block + (kind - 1) * kind_rows)
        forward(raw, spec, source, kind * kind_rows, kind_rows, forward_ref)
        return 0

    lax.fori_loop(0, 3, transform, 0, unroll=True)
    group = 16
    zero = (jnp.zeros((group, span), F32),) * 2

    def products(index, _):
        def read(kind, k):
            return spectrum_at(spec, (kind * half + k) * sub + index * group, group, span)

        def store(kind, k, value):
            store_spectrum(ready, (kind * half + k) * sub + index * group, value, group, span)

        before = None
        for place in range(half):
            total = loop(place + 1, lambda k, t, p=place: add_product(t, read(0, k), read(1, p - k)), zero)
            store(0, place, total if before is None else turned_sum(total, before, 1))
            before = total
        before = None
        for place in range(half - 1, -1, -1):
            total = loop(half - place, lambda k, t, p=place: add_conjugate(t, read(0, k), read(2, p + k)), zero)
            store(1, place, total if before is None else turned_sum(total, before, -1))
            before = total
        return 0

    lax.fori_loop(0, sub // group, products, 0, unroll=min(4, sub // group))
    back[...] = dot(ready[...], inverse_ref[...])
    skip = cols_ref[rows_at(begin, sub, sub), 9:10]
    for step in range(half):
        place = jnp.bitwise_xor(own, step) * sub
        for kind in range(2):
            source = jnp.where(side == kind, 0, 1) * kind_rows + place
            value = back[rows_at(source, sub, sub), :]
            direct = seconds[step][kind].astype(F32)
            found = (value + skip * direct).astype(BF16)
            outs[step][kind] = found
            leads[step][kind] = pick_first(found[:, :128])


def other_half(layout, cols, tables, filters, other, seconds):
    half, sub, span, parts = layout.half, layout.sub, layout.span, layout.parts
    rows = 3 * half * sub
    found = run(
        other_body,
        layout,
        (cols, *tables, filters, other, *seconds),
        [jax.ShapeDtypeStruct((2, 16, sub), BF16)] * half + [jax.ShapeDtypeStruct((2, sub, span), BF16)] * half,
        [
            pltpu.VMEM(((parts + 2 * half) * sub, span), BF16),
            pltpu.VMEM((rows, 2 * span), F32),
            pltpu.VMEM((2 * half * sub, 2 * span), BF16),
            pltpu.VMEM((2 * half * sub, span), F32),
        ],
        estimate(8.0),
    )
    return found[:half], found[half:]


def results(side, plain, mixed, crossed):
    if crossed is not None:
        mixed = (mixed.astype(F32) + crossed.astype(F32)).astype(BF16)
    return jnp.where(side == 0, plain, mixed), jnp.where(side == 0, mixed, plain)


def first_body(layout, place_ref, qkv_main, dout_main, qkv_other, dout_other, *refs):
    half, sub = layout.half, layout.sub
    main, rest, crossed = (refs[k * half : (k + 1) * half] for k in range(3))
    out_ref, grads = refs[3 * half :]
    side, _, _ = where_am_i(place_ref, layout)
    for turn in range(half):
        for other in range(2):
            place = rows_at(channel_block(place_ref, layout, turn, other) * sub, sub, sub)
            qkv, dout_ref = (qkv_other, dout_other) if other else (qkv_main, dout_main)
            source = (rest if other else main)[turn]
            if other and turn:
                fill = jnp.zeros((112, sub), F32)
                pair = [jnp.concatenate([source[k].astype(F32), fill], axis=0).T.astype(BF16) for k in range(2)]
            else:
                pair = [source[k, :, 0:128] for k in range(2)]
            pair = results(side, *pair, crossed[turn][:, 0:128] if other else None)
            y_out, dmixed = (f.astype(F32) for f in pair)
            grads[0, place, :] = dout_ref[turn, :, 0:128].astype(F32) * y_out
            grads[1, place, :] = dmixed * qkv[turn, 2, :, 0:128].astype(F32)
            grads[2, place, :] = dmixed * qkv[turn, 1, :, 0:128].astype(F32)
    out_ref[...] = jnp.zeros(out_ref.shape, F32)
    for which in range(3):
        out_ref[2 * which : 2 * which + 2, :] = grads[which].T[0:2, :]


def first_grads(layout, gated, main, rest, crossed):
    channels = layout.channels
    return run(
        first_body,
        layout,
        (*gated, *main, *rest, *crossed),
        jax.ShapeDtypeStruct((8, channels), F32),
        [pltpu.VMEM((3, channels, 128), F32)],
        estimate(6.0),
    )


def final_body(blocks, chained, layout, place_ref, qkv_main, dout_main, qkv_other, dout_other, split_ref, lanes_ref, keep_ref, *refs):
    rows, span = layout.sub, layout.span
    found = []
    for _, other in blocks:
        count = 2 if other else 1
        found.append(refs[:count])
        refs = refs[count:]
    refs = refs[1 + 2 * chained :]
    out_hbm, dfeat_hbm, partial, out_ref, dfeat_ref, spread, sems = refs
    most = span - 128
    side, _, _ = where_am_i(place_ref, layout)
    group = min(64, rows)
    keep = [keep_ref[2 + j : 3 + j, :] for j in range(2)]
    copies = []
    for k, (turn, other) in enumerate(blocks):
        block = rows_at(channel_block(place_ref, layout, turn, other) * rows, rows, rows)
        qkv, dout_ref = (qkv_other, dout_other) if other else (qkv_main, dout_main)
        source, crossed = found[k] if other else (found[k][0], None)
        spread[...] = dot(split_ref[block, :], lanes_ref[...])

        def tile(index, _, k=k, turn=turn, qkv=qkv, dout_ref=dout_ref, source=source, crossed=crossed):
            local_rows = rows_at(index * group, group, group)
            pair = [source[kind, local_rows, :] for kind in range(2)]
            pair = results(side, *pair, None if crossed is None else crossed[local_rows, :])
            out_ref[k, local_rows, :] = qkv[turn, 0, local_rows, :] * pair[0]
            y_out, dmixed = (f.astype(F32) for f in pair)
            grads = (
                dout_ref[turn, local_rows, :].astype(F32) * y_out,
                dmixed * qkv[turn, 2, local_rows, :].astype(F32),
                dmixed * qkv[turn, 1, local_rows, :].astype(F32),
            )
            for which in range(3):
                ahead = [pltpu.roll(grads[which], span - 1 - j, 1) * keep[j] for j in range(2)]
                taps = [spread[local_rows, (3 * which + j) * 128 : (3 * which + j + 1) * 128] for j in range(3)]
                for lane in range(0, span, 128):
                    total = taps[0] * grads[which][:, lane : lane + 128]
                    total = total + taps[1] * ahead[0][:, lane : lane + 128] + taps[2] * ahead[1][:, lane : lane + 128]
                    if lane == most:
                        partial[k, which, local_rows, :] = total
                    else:
                        dfeat_ref[k, which, local_rows, lane : lane + 128] = total.astype(BF16)
            return 0

        lax.fori_loop(0, rows // group, tile, 0, unroll=rows // group)
        copies.append(pltpu.make_async_copy(out_ref.at[k], out_hbm.at[block, :], sems.at[k, 0]))
        copies.append(pltpu.make_async_copy(dfeat_ref.at[k], dfeat_hbm.at[:, block, pl.ds(0, most)], sems.at[k, 1]))
        for copy in copies[-2:]:
            copy.start()
    for copy in copies:
        copy.wait()


def final(blocks, layout, gated, shared, found, after, earlier):
    span, channels, rows, count = layout.span, layout.channels, layout.sub, len(blocks)
    operands = [*gated, *shared]
    for turn, other in blocks:
        main, rest, crossed = (f[turn] for f in found)
        operands += [rest, crossed] if other else [main]
    in_specs = [HELD] * len(operands) + [ANYWHERE]
    operands.append(after)
    aliases = {}
    if earlier:
        operands += earlier
        in_specs += [IN_HBM] * 2
        aliases = {len(operands) - 2: 0, len(operands) - 1: 1}
    return run(
        functools.partial(final_body, blocks, bool(earlier)),
        layout,
        operands,
        [
            jax.ShapeDtypeStruct((channels, span), BF16),
            jax.ShapeDtypeStruct((3, channels, span), BF16),
            jax.ShapeDtypeStruct((count, 3, rows, 128), F32),
        ],
        [
            pltpu.VMEM((count, rows, span), BF16),
            pltpu.VMEM((count, 3, rows, span - 128), BF16),
            pltpu.VMEM((rows, 9 * 128), F32),
            pltpu.SemaphoreType.DMA((count, 2)),
        ],
        estimate(1.2 * count),
        in_specs=in_specs,
        out_specs=[IN_HBM, IN_HBM, HELD],
        aliases=aliases,
    )


def finish_body(lists, layout, place_ref, ahead_ref, taps_ref, edge_ref, *refs):
    partials, refs = refs[: len(lists)], refs[len(lists) + 1 :]
    dfeat_hbm, rows_ref, placed, dfeat_ref, sems = refs
    rows, span = layout.sub, layout.span
    for which in range(3):
        first, second = (ahead_ref[2 * which + k : 2 * which + k + 1, :] for k in range(2))
        one, two = (taps_ref[3 * which + k : 3 * which + k + 1, :] for k in (1, 2))
        for k, value in enumerate((one * first, two * second, two * first)):
            rows_ref[3 * which + k : 3 * which + k + 1, :] = value
    rows_ref[9:16, :] = jnp.zeros((7, layout.channels), F32)
    split = jnp.concatenate(three_parts(rows_ref[...]), axis=0).T.astype(BF16)
    placed[...] = dot(split, edge_ref[...])
    copies = []
    for blocks, partial in zip(lists, partials):
        for k, (turn, other) in enumerate(blocks):
            block = rows_at(channel_block(place_ref, layout, turn, other) * rows, rows, rows)
            for which in range(3):
                value = partial[k, which] + placed[block, which * 128 : (which + 1) * 128]
                dfeat_ref[which, block, :] = value.astype(BF16)
            target = dfeat_hbm.at[:, block, pl.ds(span - 128, 128)]
            copies.append(pltpu.make_async_copy(dfeat_ref.at[:, block, :], target, sems.at[len(copies)]))
            copies[-1].start()
    for copy in copies:
        copy.wait()


def finish(lists, layout, ahead, taps_rows, edge, partials, dfeat):
    channels = layout.channels
    return run(
        functools.partial(finish_body, lists),
        layout,
        (ahead, taps_rows, edge, *partials, dfeat),
        jax.ShapeDtypeStruct(dfeat.shape, BF16),
        [
            pltpu.VMEM((16, channels), F32),
            pltpu.VMEM((channels, 384), F32),
            pltpu.VMEM((3, channels, 128), BF16),
            pltpu.SemaphoreType.DMA((layout.parts,)),
        ],
        estimate(1.9),
        in_specs=[HELD] * (3 + len(lists)) + [IN_HBM],
        out_specs=IN_HBM,
        aliases={3 + len(lists): 0},
    )


def swap(value, step, parts, axis="seq"):
    return lax.ppermute(value, axis, [(source, source ^ step) for source in range(parts)])


def around(value, steps, parts):
    return lax.ppermute(value, "seq", [(source, (source + steps) % parts) for source in range(parts)])


def local(features, dout, filters, taps, skip, lengths):
    parts = lax.axis_size("seq")
    _, channels, span = features.shape
    layout = Layout(parts, channels, span)
    half = layout.half
    tables = [jnp.asarray(t) for t in block_tables(span)]

    features, dout, filters = (pltpu.with_memory_space_constraint(a, pltpu.HBM) for a in (features, dout, filters))

    halo, own_filt, filt = pack(layout, features, filters)
    halo = around(halo, 1, parts)
    filt = [swap(filt[step - 1], step, parts) for step in range(1, parts)]
    other = swap(jnp.concatenate(filt, axis=0), 1, 2, "groups")
    first_given = (halo, lengths.reshape(1, -1), taps, skip.reshape(1, channels))
    gated_main, firsts, trails, shared = gate(0, layout, features, dout, *first_given)
    cols, split, keep, last_edge, taps_rows, lanes, first_edge, ends_of = shared
    gated_other, cross, seconds, _ = gate(1, layout, features, dout, split, keep, lanes, first_edge, ends_of)
    firsts = [firsts[0]] + [swap(firsts[step], step, parts) for step in range(1, half)]
    trails = [trails[0]] + [swap(trails[step], step, parts) for step in range(1, half)]
    cross = [swap(cross[step], step + half, parts) for step in range(half)]
    seconds = [seconds[0]] + [swap(seconds[step], step, parts) for step in range(1, half)]

    sent, known, near = cross_half(layout, tables, own_filt[0], filt, firsts)
    crossed = [swap(sent[step], step + half, parts) for step in range(half)]
    main = main_half(layout, cols, tables, known, near, firsts, trails, cross)
    main = [main[0]] + [swap(main[step], step, parts) for step in range(1, half)]
    leads, rest = other_half(layout, cols, tables, own_filt[1], other, seconds)
    crossed = hold(layout, crossed, leads[0])
    leads = [swap(leads[step], step, parts) for step in range(1, half)]
    rest = [rest[0]] + [swap(rest[step], step, parts) for step in range(1, half)]

    gated = (*gated_main, *gated_other)
    found = (main, rest, crossed)
    shared = (split, lanes, keep)
    lists = [[(0, 0), (0, 1)], [(turn, 0) for turn in range(1, half)], [(turn, 1) for turn in range(1, half)]]
    ahead = around(first_grads(layout, gated, main, [rest[0], *leads], crossed), -1, parts)
    done, partials, after = (), [], crossed[0]
    for blocks in lists:
        *done, partial = final(blocks, layout, gated, shared, found, after, done)
        partials.append(partial)
        after = partial
    return done[0], finish(lists, layout, ahead, taps_rows, last_edge, partials, done[1])


def solution(mesh):
    in_specs = (
        P(None, ("chan", "sub"), ("groups", "seq")),
        P(("chan", "sub"), ("groups", "seq")),
        P(("chan", "sub"), "seq"),
        P(None, None, ("chan", "sub")),
        P(("chan", "sub")),
        P("groups"),
    )
    out_specs = (P(("chan", "sub"), ("groups", "seq")), P(None, ("chan", "sub"), ("groups", "seq")))
    return jax.shard_map(local, mesh=mesh, in_specs=in_specs, out_specs=out_specs, check_vma=False)
```

```python
import functools
import math

import jax
import jax.numpy as jnp
import numpy as np
from jax import lax
from jax.experimental import pallas as pl
from jax.experimental.pallas import tpu as pltpu
from jax.sharding import PartitionSpec as P

BF16 = jnp.bfloat16
F32 = jnp.float32
GATE_MAIN, GATE_OTHER = 6.0, 6.0
SHARE = 0.6
VMEM_LIMIT = 24 * 1024 * 1024
IN_HBM = pl.BlockSpec(memory_space=pltpu.HBM)
HELD = pl.BlockSpec(memory_space=pltpu.VMEM)
ANYWHERE = pl.BlockSpec(memory_space=pl.ANY)


def split_bf16(table):
    high = table.astype(np.float32).astype(BF16)
    low = (table - high.astype(np.float64)).astype(np.float32).astype(BF16)
    return high, low


def block_tables(span):
    freq = np.concatenate([np.arange(0, span, 2), np.arange(1, span, 2)])
    angle = np.pi * (2 * freq[None, :] + 1) * np.arange(span)[:, None] / (2 * span)
    forward = np.concatenate([np.cos(angle), -np.sin(angle)], axis=1)
    inverse = np.concatenate([np.cos(angle), -np.sin(angle)], axis=1).T / span
    return np.concatenate(split_bf16(forward), axis=0), split_bf16(inverse)[0]


def dot(a, b):
    return jnp.dot(a, b, preferred_element_type=F32)


def estimate(time_us):
    return pl.CostEstimate(flops=int(SHARE * time_us * 1e9), bytes_accessed=0, transcendentals=0)


def offsets_row(lengths_ref, first, span, ahead):
    position = lax.broadcasted_iota(jnp.int32, (8, span), 1) + (first + ahead)
    end, start = jnp.zeros((1, 1), jnp.int32), jnp.zeros((8, span), jnp.int32)
    for genome in range(lengths_ref.shape[1]):
        end = end + lengths_ref[:, genome : genome + 1]
        start = jnp.where(position >= end, end, start)
    return position, position - start


class Layout:
    def __init__(self, parts, channels, span):
        self.parts, self.channels, self.span = parts, channels, span
        self.half = parts // 2
        self.size = channels // self.half
        self.sub = self.size // 2


def where_am_i(place_ref, layout):
    rank, group = place_ref[0], place_ref[1]
    side = rank // layout.half
    return side, rank % layout.half, jnp.where(side == 0, 1 - group, group)


def channel_block(place_ref, layout, turn, other):
    _, own, main = where_am_i(place_ref, layout)
    return jnp.bitwise_xor(own, turn) * 2 + jnp.bitwise_xor(main, other)


def run(body, layout, operands, outs, scratch, cost, in_specs=None, out_specs=None, aliases=None):
    single = not isinstance(outs, list)

    def kernel(*refs):
        body(layout, (lax.axis_index("seq"), lax.axis_index("groups")), *refs)

    return pl.pallas_call(
        kernel,
        out_shape=outs,
        in_specs=in_specs or [HELD] * len(operands),
        out_specs=out_specs or (HELD if single else [HELD] * len(outs)),
        scratch_shapes=scratch,
        input_output_aliases=aliases or {},
        compiler_params=pltpu.CompilerParams(vmem_limit_bytes=VMEM_LIMIT),
        cost_estimate=cost,
    )(*operands)


def rows_at(begin, step, count):
    return pl.ds(pl.multiple_of(begin, step), count)


def pack_body(layout, place_ref, feat_hbm, filt_hbm, halo_ref, *rest):
    outs, (tail, turned, sems) = rest[:-3], rest[-3:]
    half, sub = layout.half, layout.sub
    copies = [pltpu.make_async_copy(feat_hbm.at[:, :, pl.ds(layout.span - 128, 128)], tail, sems.at[layout.parts + 1])]
    for step in range(layout.parts + 1):
        turn, other = (step % half, step // half) if step else (0, 0)
        if step == layout.parts:
            turn, other = 0, 1
        begin = channel_block(place_ref, layout, turn, other) * sub
        source = filt_hbm.at[rows_at(begin, sub, sub), :]
        copies.append(pltpu.make_async_copy(source, outs[step], sems.at[step]))
    for copy in copies:
        copy.start()
    turned[...] = jnp.zeros(turned.shape, F32)
    copies[0].wait()
    for which in range(3):
        turned[2 * which : 2 * which + 2, :] = tail[which].astype(F32).T[-2:, :]
    halo_ref[...] = turned[...].astype(BF16)
    for copy in copies[1:]:
        copy.wait()


def pack(layout, features, filters):
    parts, sub, span, channels = layout.parts, layout.sub, layout.span, layout.channels
    outs = [jax.ShapeDtypeStruct((16, channels), BF16)] + [jax.ShapeDtypeStruct((sub, span), BF16)] * (parts + 1)
    scratch = [
        pltpu.VMEM((3, channels, 128), BF16),
        pltpu.VMEM((16, channels), F32),
        pltpu.SemaphoreType.DMA((parts + 2,)),
    ]
    found = run(pack_body, layout, (features, filters), outs, scratch, estimate(2.0), in_specs=[IN_HBM] * 2)
    return found[0], (found[1], found[1 + parts]), found[2 : 1 + parts]


def three_parts(value):
    top = value.astype(BF16).astype(F32)
    middle = (value - top).astype(BF16).astype(F32)
    return [top, middle, value - top - middle]


def edge_table(table_rows, lanes, entries):
    row = lax.broadcasted_iota(jnp.int32, (table_rows, lanes), 0)
    lane = lax.broadcasted_iota(jnp.int32, (table_rows, lanes), 1)
    table = jnp.zeros((table_rows, lanes), F32)
    for rows, where, keep in entries:
        for own_row in rows:
            table = jnp.where((row == own_row) & (lane == where), keep, table)
    return table.astype(BF16)


def fill_tables(layout, place_ref, lengths_ref, taps_ref, skip_ref, fwd_edge_ref, *rest):
    cols_ref, split_ref, keep_ref, last_edge_ref, turned, lanes_ref = rest
    span = layout.span
    first = place_ref[0] * span
    _, offset = offsets_row(lengths_ref, first, span, 0)
    keep, keep_back = [], []
    for j in (1, 2):
        keep.append((offset[0:1, :] >= j).astype(F32))
        position, later = offsets_row(lengths_ref, first, span, j)
        inside = (position < layout.parts * span) & (later >= j)
        keep_back.append(inside[0:1, :].astype(F32))
    most = span - 128
    lane = lax.broadcasted_iota(jnp.int32, (1, span), 1)
    keep_ref[...] = jnp.zeros(keep_ref.shape, F32)
    for j in (0, 1):
        keep_ref[j : j + 1, :] = jnp.where(lane > j, keep[j], 0.0)
        keep_ref[2 + j : 3 + j, :] = jnp.where(lane < span - 1 - j, keep_back[j], 0.0)
    for which in range(3):
        begin = which * 256
        two, one = [2 * which], [2 * which + 1]
        fwd_edge_ref[:, begin : begin + 128] = edge_table(16, 128, [(one, 0, keep[0][:, :128])])
        fwd_edge_ref[:, begin + 128 : begin + 256] = edge_table(
            16, 128, [(two, 0, keep[1][:, :128]), (one, 1, keep[1][:, :128])]
        )
        entries = []
        for k, (lane_at, j) in enumerate(((127, 0), (127, 1), (126, 1))):
            entries.append(([3 * which + k + 16 * p for p in range(3)], lane_at, keep_back[j][:, most:]))
        last_edge_ref[:, which * 128 : (which + 1) * 128] = edge_table(48, 128, entries)
    turned[...] = jnp.zeros(turned.shape, F32)
    for which in range(3):
        turned[3 * which : 3 * which + 3, :] = taps_ref[which]
    turned[9:10, :] = skip_ref[...]
    value = turned[...]
    cols_ref[...] = value.T
    split_ref[...] = jnp.concatenate(three_parts(value), axis=0).T.astype(BF16)
    column = lax.broadcasted_iota(jnp.int32, (48, 128), 0) % 16
    for k in range(9):
        lanes_ref[:, k * 128 : (k + 1) * 128] = jnp.where(column == k, 1.0, 0.0).astype(BF16)


def table_shapes(layout):
    channels = layout.channels
    return [
        ((channels, 16), F32),
        ((channels, 48), BF16),
        ((8, layout.span), F32),
        ((48, 384), BF16),
        ((16, channels), F32),
        ((48, 9 * 128), BF16),
    ]


def gate_body(other, layout, place_ref, feat_hbm, dout_hbm, *rest):
    half, rows, span = layout.half, layout.sub, layout.span
    given, rest = (rest[:5], rest[5:]) if other else (rest[:4], rest[4:])
    qkv_ref, dout_ref, pairs, rest = rest[0], rest[1], rest[2 : 2 + half], rest[2 + half :]
    if other:
        cross, rest = rest[:half], rest[half:]
    feat_ref, spread, ends, sems = rest[-4:]
    side, _, _ = where_am_i(place_ref, layout)
    group = min(64, rows)
    copies = []
    for turn in range(half):
        block = rows_at(channel_block(place_ref, layout, turn, other) * rows, rows, rows)
        copies.append(pltpu.make_async_copy(feat_hbm.at[:, block, :], feat_ref.at[turn], sems.at[turn, 0]))
        copies.append(pltpu.make_async_copy(dout_hbm.at[block, :], dout_ref.at[turn], sems.at[turn, 1]))
        for copy in copies[-2:]:
            copy.start()
    if other:
        split_ref, keep_ref, lanes_ref, edge_ref, ends_of = given
    else:
        halo_ref, lengths_ref, taps_ref, skip_ref = given
        tables, edge_ref, ends_of = rest[:6], rest[6], rest[7]
        _, split_ref, keep_ref, _, _, lanes_ref = tables
        fill_tables(layout, place_ref, lengths_ref, taps_ref, skip_ref, edge_ref, *tables)
        ends_of[...] = halo_ref[...].astype(F32).T.astype(BF16)
    keep = [keep_ref[j : j + 1, :] for j in range(2)]
    for turn in range(half):
        block = rows_at(channel_block(place_ref, layout, turn, other) * rows, rows, rows)
        spread[...] = dot(split_ref[block, :], lanes_ref[...])
        ends[...] = dot(ends_of[block, :], edge_ref[...])
        for copy in copies[2 * turn : 2 * turn + 2]:
            copy.wait()

        def tile(index, _, turn=turn):
            local_rows = rows_at(index * group, group, group)
            filtered = []
            for which in range(3):
                value = feat_ref[turn, which, local_rows, :].astype(F32)
                moved = [pltpu.roll(value, j + 1, 1) * keep[j] for j in range(2)]
                taps = [spread[local_rows, (3 * which + j) * 128 : (3 * which + j + 1) * 128] for j in range(3)]
                parts = []
                for lane in range(0, span, 128):
                    back = [moved[j][:, lane : lane + 128] for j in range(2)]
                    if lane == 0:
                        begins = [which * 256 + j * 128 for j in range(2)]
                        back = [back[j] + ends[local_rows, begins[j] : begins[j] + 128] for j in range(2)]
                    total = taps[0] * value[:, lane : lane + 128]
                    parts.append((total + taps[1] * back[0] + taps[2] * back[1]).astype(BF16))
                filtered.append(jnp.concatenate(parts, axis=1))
                qkv_ref[turn, which, local_rows, :] = filtered[-1]
            mixed = filtered[1] * filtered[2]
            grad_in = dout_ref[turn, local_rows, :] * filtered[0]
            first = jnp.where(side == 0, mixed, grad_in)
            second = jnp.where(side == 0, grad_in, mixed)
            pairs[turn][0, local_rows, :] = first
            pairs[turn][1, local_rows, :] = second
            if other:
                cross[turn][local_rows, :] = first
            return 0

        lax.fori_loop(0, rows // group, tile, 0, unroll=rows // group)


def gate(other, layout, features, dout, *given):
    half, rows, span, channels = layout.half, layout.sub, layout.span, layout.channels
    shapes = [(half, 3, rows, span), (half, rows, span)] + [(2, rows, span)] * half
    shapes += [(rows, span)] * half if other else []
    outs = [jax.ShapeDtypeStruct(s, BF16) for s in shapes]
    if not other:
        more = table_shapes(layout) + [((16, 768), BF16), ((channels, 16), BF16)]
        outs += [jax.ShapeDtypeStruct(*s) for s in more]
    found = run(
        functools.partial(gate_body, other),
        layout,
        (features, dout, *given),
        outs,
        [
            pltpu.VMEM((half, 3, rows, span), BF16),
            pltpu.VMEM((rows, 9 * 128), F32),
            pltpu.VMEM((rows, 768), F32),
            pltpu.SemaphoreType.DMA((half, 2)),
        ],
        estimate(GATE_OTHER if other else GATE_MAIN),
        in_specs=[IN_HBM] * 2 + [HELD] * len(given),
    )
    return found[0:2], found[2 : 2 + half], found[2 + half :]


def loop(count, body, init):
    if count <= 4:
        for k in range(count):
            init = body(k, init)
        return init
    return lax.fori_loop(0, count, body, init)


def add_product(total, f, x):
    return (total[0] + f[0] * x[0] - f[1] * x[1], total[1] + f[0] * x[1] + f[1] * x[0])


def add_conjugate(total, f, x):
    return (total[0] + f[0] * x[0] + f[1] * x[1], total[1] + f[0] * x[1] - f[1] * x[0])


def turned_sum(spectrum, neighbour, sign):
    half = spectrum[0].shape[1] // 2
    parts = []
    for lanes, flip in ((slice(0, half), sign), (slice(half, None), -sign)):
        n_re, n_im = neighbour[0][:, lanes], neighbour[1][:, lanes]
        s_re, s_im = spectrum[0][:, lanes], spectrum[1][:, lanes]
        parts.append((s_re - n_im, s_im + n_re) if flip > 0 else (s_re + n_im, s_im - n_re))
    return tuple(jnp.concatenate([p[k] for p in parts], axis=1) for k in range(2))


def forward(raw, spec, begin, target, rows, table_ref):
    value = raw[pl.ds(pl.multiple_of(begin, 16), rows), :]
    spec[pl.ds(pl.multiple_of(target, 16), rows), :] = dot(jnp.concatenate([value, value], axis=1), table_ref[...])


def spectrum_at(spec, begin, group, span):
    place = pl.ds(pl.multiple_of(begin, group), group)
    return spec[place, :span], spec[place, span:]


def store_spectrum(ready, begin, value, group, span):
    place = pl.ds(pl.multiple_of(begin, group), group)
    ready[place, :span] = value[0].astype(BF16)
    ready[place, span:] = value[1].astype(BF16)


def cross_body(layout, place_ref, forward_ref, inverse_ref, filt_ref, *rest):
    parts, half, sub, span = layout.parts, layout.half, layout.sub, layout.span
    filt_in, rest = rest[: parts - 1], rest[parts - 1 :]
    signal, outs = rest[:half], rest[half : 2 * half]
    known, spec, filt_raw, raw, ready, back = rest[2 * half :]
    rank = place_ref[0]
    filt_raw[rows_at(rank * sub, sub, sub), :] = filt_ref[...]
    for step in range(1, parts):
        filt_raw[rows_at(jnp.bitwise_xor(rank, step) * sub, sub, sub), :] = filt_in[step - 1][...]
    chunk = math.gcd(parts * sub, 512)

    def transform(index, _):
        forward(filt_raw, known, index * chunk, index * chunk, chunk, forward_ref)
        return 0

    lax.fori_loop(0, parts * sub // chunk, transform, 0, unroll=True)
    side, own, _ = where_am_i(place_ref, layout)
    for step in range(half):
        raw[rows_at(jnp.bitwise_xor(own, step) * sub, sub, sub), :] = signal[step][0]
    forward(raw, spec, 0, 0, half * sub, forward_ref)
    group = 16
    zero = (jnp.zeros((group, span), F32),) * 2

    def products(index, ahead):
        def filt(k):
            return spectrum_at(known, k * sub + index * group, group, span)

        def sig(k):
            return spectrum_at(spec, k * sub + index * group, group, span)

        before = None
        if ahead:
            for place in range(half - 1, parts):
                total = loop(half, lambda k, t, p=place: add_product(t, filt(p - k), sig(k)), zero)
                if before is not None:
                    value = turned_sum(total, before, 1)
                    store_spectrum(ready, (place - half) * sub + index * group, value, group, span)
                before = total
        else:
            for place in range(half, -1, -1):
                total = loop(half, lambda k, t, p=place: add_conjugate(t, filt(half + k - p), sig(k)), zero)
                if before is not None:
                    value = turned_sum(total, before, -1)
                    store_spectrum(ready, place * sub + index * group, value, group, span)
                before = total
        return 0

    @pl.when(side == 0)
    def _():
        lax.fori_loop(0, sub // group, lambda k, _: products(k, True), 0, unroll=min(4, sub // group))

    @pl.when(side == 1)
    def _():
        lax.fori_loop(0, sub // group, lambda k, _: products(k, False), 0, unroll=min(4, sub // group))

    back[...] = dot(ready[...], inverse_ref[...])
    for step in range(half):
        outs[step][...] = back[rows_at(jnp.bitwise_xor(own, step) * sub, sub, sub), :].astype(BF16)


def cross_half(layout, tables, own, filt, signal):
    half, sub, span = layout.half, layout.sub, layout.span
    all_rows = layout.parts * sub
    rows = half * sub
    found = run(
        cross_body,
        layout,
        (*tables, own, *filt, *signal),
        [jax.ShapeDtypeStruct((sub, span), BF16)] * half
        + [jax.ShapeDtypeStruct((r, 2 * span), F32) for r in (all_rows, rows)],
        [
            pltpu.VMEM((all_rows, span), BF16),
            pltpu.VMEM((rows, span), BF16),
            pltpu.VMEM((rows, 2 * span), BF16),
            pltpu.VMEM((rows, span), F32),
        ],
        estimate(0.3),
    )
    return found[:half], found[half], found[half + 1]


def hold_body(layout, place_ref, *refs):
    count = (len(refs) - 1) // 2
    for source, target in zip(refs[:count], refs[count + 1 :]):
        target[...] = source[...]


def hold(layout, arrays, after):
    outs = [jax.ShapeDtypeStruct(a.shape, a.dtype) for a in arrays]
    return run(hold_body, layout, [*arrays, after], outs, [], estimate(4.0), in_specs=[HELD] * len(arrays) + [ANYWHERE])


def main_body(layout, place_ref, cols_ref, forward_ref, inverse_ref, known, near_spec, *rest):
    parts, half, sub, span = layout.parts, layout.half, layout.sub, layout.span
    firsts, cross, outs = (rest[k * half : (k + 1) * half] for k in range(3))
    raw, spec, ready, back = rest[3 * half :]
    side, own, _ = where_am_i(place_ref, layout)
    block = parts * sub
    for step in range(half):
        place = jnp.bitwise_xor(own, step)
        raw[rows_at((side * half + place) * sub, sub, sub), :] = firsts[step][1]
        raw[rows_at(((1 - side) * half + place) * sub, sub, sub), :] = cross[step][...]
    chunk = math.gcd(block, 512)

    def transform(index, _):
        forward(raw, spec, index * chunk, index * chunk, chunk, forward_ref)
        return 0

    lax.fori_loop(0, block // chunk, transform, 0, unroll=True)
    group = 16
    zero = (jnp.zeros((group, span), F32),) * 2

    def products(index, first_half):
        def filt(k):
            return spectrum_at(known, k * sub + index * group, group, span)

        def near(k):
            return spectrum_at(near_spec, k * sub + index * group, group, span)

        def far(k):
            return spectrum_at(spec, k * sub + index * group, group, span)

        def store(kind, place, value):
            store_spectrum(ready, (kind * half + place) * sub + index * group, value, group, span)

        before = None
        if first_half:
            for place in range(half):
                total = loop(place + 1, lambda k, t, p=place: add_product(t, filt(k), near(p - k)), zero)
                store(0, place, total if before is None else turned_sum(total, before, 1))
                before = total
            before = None
            for place in range(half, -1, -1):
                total = loop(parts - place, lambda k, t, p=place: add_conjugate(t, filt(k), far(p + k)), zero)
                if before is not None:
                    store(1, place, turned_sum(total, before, -1))
                before = total
        else:
            for place in range(half - 1, -1, -1):
                total = loop(half - place, lambda k, t, p=place: add_conjugate(t, filt(k), near(p + k)), zero)
                store(0, place, total if before is None else turned_sum(total, before, -1))
                before = total
            before = None
            for place in range(half - 1, parts):
                total = loop(place + 1, lambda k, t, p=place: add_product(t, filt(k), far(p - k)), zero)
                if before is not None:
                    store(1, place - half, turned_sum(total, before, 1))
                before = total
        return 0

    @pl.when(side == 0)
    def _():
        lax.fori_loop(0, sub // group, lambda k, _: products(k, True), 0, unroll=min(4, sub // group))

    @pl.when(side == 1)
    def _():
        lax.fori_loop(0, sub // group, lambda k, _: products(k, False), 0, unroll=min(4, sub // group))

    back[...] = dot(ready[...], inverse_ref[...])
    begin = channel_block(place_ref, layout, 0, 0) * sub
    skip = cols_ref[rows_at(begin, sub, sub), 9:10]
    for step in range(half):
        place = jnp.bitwise_xor(own, step)
        for kind in range(2):
            value = back[rows_at((kind * half + place) * sub, sub, sub), :]
            direct = firsts[step][kind].astype(F32)
            outs[step][kind] = (value + skip * direct).astype(BF16)


def main_half(layout, cols, tables, known, near, firsts, cross):
    half, sub, span, parts = layout.half, layout.sub, layout.span, layout.parts
    rows = parts * sub
    return run(
        main_body,
        layout,
        (cols, *tables, known, near, *firsts, *cross),
        [jax.ShapeDtypeStruct((2, sub, span), BF16)] * half,
        [
            pltpu.VMEM((rows, span), BF16),
            pltpu.VMEM((rows, 2 * span), F32),
            pltpu.VMEM((2 * half * sub, 2 * span), BF16),
            pltpu.VMEM((2 * half * sub, span), F32),
        ],
        estimate(10.0),
    )


def pick_first(value):
    row = lax.broadcasted_iota(jnp.int32, (16, 128), 0)
    lane = lax.broadcasted_iota(jnp.int32, (16, 128), 1)
    table = jnp.where((row == lane) & (row < 2), 1.0, 0.0).astype(BF16)
    dims = (((1,), (1,)), ((), ()))
    return lax.dot_general(table, value, dims, preferred_element_type=F32).astype(BF16)


def other_body(layout, place_ref, cols_ref, forward_ref, inverse_ref, filt_ref, other_ref, *rest):
    parts, half, sub, span = layout.parts, layout.half, layout.sub, layout.span
    seconds, leads, outs = (rest[k * half : (k + 1) * half] for k in range(3))
    raw, spec, ready, back = rest[3 * half :]
    side, own, _ = where_am_i(place_ref, layout)
    rank = place_ref[0]
    block, kind_rows = parts * sub, half * sub
    begin = channel_block(place_ref, layout, 0, 1) * sub
    raw[rows_at(rank * sub, sub, sub), :] = filt_ref[...]
    for step in range(1, parts):
        place = rows_at(jnp.bitwise_xor(rank, step) * sub, sub, sub)
        raw[place, :] = other_ref[(step - 1) * sub : step * sub, :]
    for step in range(half):
        place = block + jnp.bitwise_xor(own, step) * sub
        raw[rows_at(place + side * kind_rows, sub, sub), :] = seconds[step][0]
        raw[rows_at(place + (1 - side) * kind_rows, sub, sub), :] = seconds[step][1]

    def transform(kind, _):
        source = jnp.where(kind == 0, 0, block + (kind - 1) * kind_rows)
        forward(raw, spec, source, kind * kind_rows, kind_rows, forward_ref)
        return 0

    lax.fori_loop(0, 3, transform, 0, unroll=True)
    group = 16
    zero = (jnp.zeros((group, span), F32),) * 2

    def products(index, _):
        def read(kind, k):
            return spectrum_at(spec, (kind * half + k) * sub + index * group, group, span)

        def store(kind, k, value):
            store_spectrum(ready, (kind * half + k) * sub + index * group, value, group, span)

        before = None
        for place in range(half):
            total = loop(place + 1, lambda k, t, p=place: add_product(t, read(0, k), read(1, p - k)), zero)
            store(0, place, total if before is None else turned_sum(total, before, 1))
            before = total
        before = None
        for place in range(half - 1, -1, -1):
            total = loop(half - place, lambda k, t, p=place: add_conjugate(t, read(0, k), read(2, p + k)), zero)
            store(1, place, total if before is None else turned_sum(total, before, -1))
            before = total
        return 0

    lax.fori_loop(0, sub // group, products, 0, unroll=min(4, sub // group))
    back[...] = dot(ready[...], inverse_ref[...])
    skip = cols_ref[rows_at(begin, sub, sub), 9:10]
    for step in range(half):
        place = jnp.bitwise_xor(own, step) * sub
        for kind in range(2):
            source = jnp.where(side == kind, 0, 1) * kind_rows + place
            value = back[rows_at(source, sub, sub), :]
            direct = seconds[step][kind].astype(F32)
            found = (value + skip * direct).astype(BF16)
            outs[step][kind] = found
            leads[step][kind] = pick_first(found[:, :128])


def other_half(layout, cols, tables, filters, other, seconds):
    half, sub, span, parts = layout.half, layout.sub, layout.span, layout.parts
    rows = 3 * half * sub
    found = run(
        other_body,
        layout,
        (cols, *tables, filters, other, *seconds),
        [jax.ShapeDtypeStruct((2, 16, sub), BF16)] * half + [jax.ShapeDtypeStruct((2, sub, span), BF16)] * half,
        [
            pltpu.VMEM(((parts + 2 * half) * sub, span), BF16),
            pltpu.VMEM((rows, 2 * span), F32),
            pltpu.VMEM((2 * half * sub, 2 * span), BF16),
            pltpu.VMEM((2 * half * sub, span), F32),
        ],
        estimate(8.0),
    )
    return found[:half], found[half:]


def results(side, plain, mixed, crossed):
    if crossed is not None:
        mixed = (mixed.astype(F32) + crossed.astype(F32)).astype(BF16)
    return jnp.where(side == 0, plain, mixed), jnp.where(side == 0, mixed, plain)


def first_body(layout, place_ref, qkv_main, dout_main, qkv_other, dout_other, *refs):
    half, sub = layout.half, layout.sub
    main, rest, crossed = (refs[k * half : (k + 1) * half] for k in range(3))
    out_ref, grads = refs[3 * half :]
    side, _, _ = where_am_i(place_ref, layout)
    for turn in range(half):
        for other in range(2):
            place = rows_at(channel_block(place_ref, layout, turn, other) * sub, sub, sub)
            qkv, dout_ref = (qkv_other, dout_other) if other else (qkv_main, dout_main)
            source = (rest if other else main)[turn]
            if other and turn:
                fill = jnp.zeros((112, sub), F32)
                pair = [jnp.concatenate([source[k].astype(F32), fill], axis=0).T.astype(BF16) for k in range(2)]
            else:
                pair = [source[k, :, 0:128] for k in range(2)]
            pair = results(side, *pair, crossed[turn][:, 0:128] if other else None)
            y_out, dmixed = (f.astype(F32) for f in pair)
            grads[0, place, :] = dout_ref[turn, :, 0:128].astype(F32) * y_out
            grads[1, place, :] = dmixed * qkv[turn, 2, :, 0:128].astype(F32)
            grads[2, place, :] = dmixed * qkv[turn, 1, :, 0:128].astype(F32)
    out_ref[...] = jnp.zeros(out_ref.shape, F32)
    for which in range(3):
        out_ref[2 * which : 2 * which + 2, :] = grads[which].T[0:2, :]


def first_grads(layout, gated, main, rest, crossed):
    channels = layout.channels
    return run(
        first_body,
        layout,
        (*gated, *main, *rest, *crossed),
        jax.ShapeDtypeStruct((8, channels), F32),
        [pltpu.VMEM((3, channels, 128), F32)],
        estimate(6.0),
    )


def final_body(blocks, chained, layout, place_ref, qkv_main, dout_main, qkv_other, dout_other, split_ref, lanes_ref, keep_ref, *refs):
    rows, span = layout.sub, layout.span
    found = []
    for _, other in blocks:
        count = 2 if other else 1
        found.append(refs[:count])
        refs = refs[count:]
    refs = refs[1 + 2 * chained :]
    out_hbm, dfeat_hbm, partial, out_ref, dfeat_ref, spread, sems = refs
    most = span - 128
    side, _, _ = where_am_i(place_ref, layout)
    group = min(64, rows)
    keep = [keep_ref[2 + j : 3 + j, :] for j in range(2)]
    copies = []
    for k, (turn, other) in enumerate(blocks):
        block = rows_at(channel_block(place_ref, layout, turn, other) * rows, rows, rows)
        qkv, dout_ref = (qkv_other, dout_other) if other else (qkv_main, dout_main)
        source, crossed = found[k] if other else (found[k][0], None)
        spread[...] = dot(split_ref[block, :], lanes_ref[...])

        def tile(index, _, k=k, turn=turn, qkv=qkv, dout_ref=dout_ref, source=source, crossed=crossed):
            local_rows = rows_at(index * group, group, group)
            pair = [source[kind, local_rows, :] for kind in range(2)]
            pair = results(side, *pair, None if crossed is None else crossed[local_rows, :])
            out_ref[k, local_rows, :] = qkv[turn, 0, local_rows, :] * pair[0]
            y_out, dmixed = (f.astype(F32) for f in pair)
            grads = (
                dout_ref[turn, local_rows, :].astype(F32) * y_out,
                dmixed * qkv[turn, 2, local_rows, :].astype(F32),
                dmixed * qkv[turn, 1, local_rows, :].astype(F32),
            )
            for which in range(3):
                ahead = [pltpu.roll(grads[which], span - 1 - j, 1) * keep[j] for j in range(2)]
                taps = [spread[local_rows, (3 * which + j) * 128 : (3 * which + j + 1) * 128] for j in range(3)]
                for lane in range(0, span, 128):
                    total = taps[0] * grads[which][:, lane : lane + 128]
                    total = total + taps[1] * ahead[0][:, lane : lane + 128] + taps[2] * ahead[1][:, lane : lane + 128]
                    if lane == most:
                        partial[k, which, local_rows, :] = total
                    else:
                        dfeat_ref[k, which, local_rows, lane : lane + 128] = total.astype(BF16)
            return 0

        lax.fori_loop(0, rows // group, tile, 0, unroll=rows // group)
        copies.append(pltpu.make_async_copy(out_ref.at[k], out_hbm.at[block, :], sems.at[k, 0]))
        copies.append(pltpu.make_async_copy(dfeat_ref.at[k], dfeat_hbm.at[:, block, pl.ds(0, most)], sems.at[k, 1]))
        for copy in copies[-2:]:
            copy.start()
    for copy in copies:
        copy.wait()


def final(blocks, layout, gated, shared, found, after, earlier):
    span, channels, rows, count = layout.span, layout.channels, layout.sub, len(blocks)
    operands = [*gated, *shared]
    for turn, other in blocks:
        main, rest, crossed = (f[turn] for f in found)
        operands += [rest, crossed] if other else [main]
    in_specs = [HELD] * len(operands) + [ANYWHERE]
    operands.append(after)
    aliases = {}
    if earlier:
        operands += earlier
        in_specs += [IN_HBM] * 2
        aliases = {len(operands) - 2: 0, len(operands) - 1: 1}
    return run(
        functools.partial(final_body, blocks, bool(earlier)),
        layout,
        operands,
        [
            jax.ShapeDtypeStruct((channels, span), BF16),
            jax.ShapeDtypeStruct((3, channels, span), BF16),
            jax.ShapeDtypeStruct((count, 3, rows, 128), F32),
        ],
        [
            pltpu.VMEM((count, rows, span), BF16),
            pltpu.VMEM((count, 3, rows, span - 128), BF16),
            pltpu.VMEM((rows, 9 * 128), F32),
            pltpu.SemaphoreType.DMA((count, 2)),
        ],
        estimate(1.2 * count),
        in_specs=in_specs,
        out_specs=[IN_HBM, IN_HBM, HELD],
        aliases=aliases,
    )


def finish_body(lists, layout, place_ref, ahead_ref, taps_ref, edge_ref, *refs):
    partials, refs = refs[: len(lists)], refs[len(lists) + 1 :]
    dfeat_hbm, rows_ref, placed, dfeat_ref, sems = refs
    rows, span = layout.sub, layout.span
    for which in range(3):
        first, second = (ahead_ref[2 * which + k : 2 * which + k + 1, :] for k in range(2))
        one, two = (taps_ref[3 * which + k : 3 * which + k + 1, :] for k in (1, 2))
        for k, value in enumerate((one * first, two * second, two * first)):
            rows_ref[3 * which + k : 3 * which + k + 1, :] = value
    rows_ref[9:16, :] = jnp.zeros((7, layout.channels), F32)
    split = jnp.concatenate(three_parts(rows_ref[...]), axis=0).T.astype(BF16)
    placed[...] = dot(split, edge_ref[...])
    copies = []
    for blocks, partial in zip(lists, partials):
        for k, (turn, other) in enumerate(blocks):
            block = rows_at(channel_block(place_ref, layout, turn, other) * rows, rows, rows)
            for which in range(3):
                value = partial[k, which] + placed[block, which * 128 : (which + 1) * 128]
                dfeat_ref[which, block, :] = value.astype(BF16)
            target = dfeat_hbm.at[:, block, pl.ds(span - 128, 128)]
            copies.append(pltpu.make_async_copy(dfeat_ref.at[:, block, :], target, sems.at[len(copies)]))
            copies[-1].start()
    for copy in copies:
        copy.wait()


def finish(lists, layout, ahead, taps_rows, edge, partials, dfeat):
    channels = layout.channels
    return run(
        functools.partial(finish_body, lists),
        layout,
        (ahead, taps_rows, edge, *partials, dfeat),
        jax.ShapeDtypeStruct(dfeat.shape, BF16),
        [
            pltpu.VMEM((16, channels), F32),
            pltpu.VMEM((channels, 384), F32),
            pltpu.VMEM((3, channels, 128), BF16),
            pltpu.SemaphoreType.DMA((layout.parts,)),
        ],
        estimate(1.9),
        in_specs=[HELD] * (3 + len(lists)) + [IN_HBM],
        out_specs=IN_HBM,
        aliases={3 + len(lists): 0},
    )


def swap(value, step, parts, axis="seq"):
    return lax.ppermute(value, axis, [(source, source ^ step) for source in range(parts)])


def around(value, steps, parts):
    return lax.ppermute(value, "seq", [(source, (source + steps) % parts) for source in range(parts)])


def local(features, dout, filters, taps, skip, lengths):
    parts = lax.axis_size("seq")
    _, channels, span = features.shape
    layout = Layout(parts, channels, span)
    half = layout.half
    tables = [jnp.asarray(t) for t in block_tables(span)]

    features, dout, filters = (pltpu.with_memory_space_constraint(a, pltpu.HBM) for a in (features, dout, filters))

    halo, own_filt, filt = pack(layout, features, filters)
    halo = around(halo, 1, parts)
    filt = [swap(filt[step - 1], step, parts) for step in range(1, parts)]
    other = swap(jnp.concatenate(filt, axis=0), 1, 2, "groups")
    first_given = (halo, lengths.reshape(1, -1), taps, skip.reshape(1, channels))
    gated_main, firsts, shared = gate(0, layout, features, dout, *first_given)
    cols, split, keep, last_edge, taps_rows, lanes, first_edge, ends_of = shared
    gated_other, seconds, cross = gate(1, layout, features, dout, split, keep, lanes, first_edge, ends_of)
    firsts = [firsts[0]] + [swap(firsts[step], step, parts) for step in range(1, half)]
    cross = [swap(cross[step], step + half, parts) for step in range(half)]
    seconds = [seconds[0]] + [swap(seconds[step], step, parts) for step in range(1, half)]

    sent, known, near = cross_half(layout, tables, own_filt[0], filt, firsts)
    crossed = [swap(sent[step], step + half, parts) for step in range(half)]
    main = main_half(layout, cols, tables, known, near, firsts, cross)
    main = [main[0]] + [swap(main[step], step, parts) for step in range(1, half)]
    leads, rest = other_half(layout, cols, tables, own_filt[1], other, seconds)
    crossed = hold(layout, crossed, leads[0])
    leads = [swap(leads[step], step, parts) for step in range(1, half)]
    rest = [rest[0]] + [swap(rest[step], step, parts) for step in range(1, half)]

    gated = (*gated_main, *gated_other)
    found = (main, rest, crossed)
    shared = (split, lanes, keep)
    lists = [[(0, 0), (0, 1)], [(turn, 0) for turn in range(1, half)], [(turn, 1) for turn in range(1, half)]]
    ahead = around(first_grads(layout, gated, main, [rest[0], *leads], crossed), -1, parts)
    done, partials, after = (), [], crossed[0]
    for blocks in lists:
        *done, partial = final(blocks, layout, gated, shared, found, after, done)
        partials.append(partial)
        after = partial
    return done[0], finish(lists, layout, ahead, taps_rows, last_edge, partials, done[1])


def solution(mesh):
    in_specs = (
        P(None, ("chan", "sub"), ("groups", "seq")),
        P(("chan", "sub"), ("groups", "seq")),
        P(("chan", "sub"), "seq"),
        P(None, None, ("chan", "sub")),
        P(("chan", "sub")),
        P("groups"),
    )
    out_specs = (P(("chan", "sub"), ("groups", "seq")), P(None, ("chan", "sub"), ("groups", "seq")))
    return jax.shard_map(local, mesh=mesh, in_specs=in_specs, out_specs=out_specs, check_vma=False)
```

```python
import functools
import math

import jax
import jax.numpy as jnp
import numpy as np
from jax import lax
from jax.experimental import pallas as pl
from jax.experimental.pallas import tpu as pltpu
from jax.sharding import PartitionSpec as P

BF16 = jnp.bfloat16
F32 = jnp.float32
GATE_MAIN, GATE_OTHER = 6.0, 6.0
SHARE = 0.6
VMEM_LIMIT = 24 * 1024 * 1024
IN_HBM = pl.BlockSpec(memory_space=pltpu.HBM)
HELD = pl.BlockSpec(memory_space=pltpu.VMEM)
ANYWHERE = pl.BlockSpec(memory_space=pl.ANY)


def split_bf16(table):
    high = table.astype(np.float32).astype(BF16)
    low = (table - high.astype(np.float64)).astype(np.float32).astype(BF16)
    return high, low


def block_tables(span):
    freq = np.concatenate([np.arange(0, span, 2), np.arange(1, span, 2)])
    angle = np.pi * (2 * freq[None, :] + 1) * np.arange(span)[:, None] / (2 * span)
    forward = np.concatenate([np.cos(angle), -np.sin(angle)], axis=1)
    inverse = np.concatenate([np.cos(angle), -np.sin(angle)], axis=1).T / span
    return np.concatenate(split_bf16(forward), axis=0), split_bf16(inverse)[0]


def dot(a, b):
    return jnp.dot(a, b, preferred_element_type=F32)


def estimate(time_us):
    return pl.CostEstimate(flops=int(SHARE * time_us * 1e9), bytes_accessed=0, transcendentals=0)


def offsets_row(lengths_ref, first, span, ahead):
    position = lax.broadcasted_iota(jnp.int32, (8, span), 1) + (first + ahead)
    end, start = jnp.zeros((1, 1), jnp.int32), jnp.zeros((8, span), jnp.int32)
    for genome in range(lengths_ref.shape[1]):
        end = end + lengths_ref[:, genome : genome + 1]
        start = jnp.where(position >= end, end, start)
    return position, position - start


class Layout:
    def __init__(self, parts, channels, span):
        self.parts, self.channels, self.span = parts, channels, span
        self.half = parts // 2
        self.size = channels // self.half
        self.sub = self.size // 2


def where_am_i(place_ref, layout):
    rank, group = place_ref[0], place_ref[1]
    side = rank // layout.half
    return side, rank % layout.half, jnp.where(side == 0, 1 - group, group)


def channel_block(place_ref, layout, turn, other):
    _, own, main = where_am_i(place_ref, layout)
    return jnp.bitwise_xor(own, turn) * 2 + jnp.bitwise_xor(main, other)


def run(body, layout, operands, outs, scratch, cost, in_specs=None, out_specs=None, aliases=None):
    single = not isinstance(outs, list)

    def kernel(*refs):
        body(layout, (lax.axis_index("seq"), lax.axis_index("groups")), *refs)

    return pl.pallas_call(
        kernel,
        out_shape=outs,
        in_specs=in_specs or [HELD] * len(operands),
        out_specs=out_specs or (HELD if single else [HELD] * len(outs)),
        scratch_shapes=scratch,
        input_output_aliases=aliases or {},
        compiler_params=pltpu.CompilerParams(vmem_limit_bytes=VMEM_LIMIT),
        cost_estimate=cost,
    )(*operands)


def rows_at(begin, step, count):
    return pl.ds(pl.multiple_of(begin, step), count)


def pack_body(layout, place_ref, feat_hbm, filt_hbm, halo_ref, *rest):
    outs, (tail, turned, sems) = rest[:-3], rest[-3:]
    half, sub = layout.half, layout.sub
    copies = [pltpu.make_async_copy(feat_hbm.at[:, :, pl.ds(layout.span - 128, 128)], tail, sems.at[layout.parts + 1])]
    for step in range(layout.parts + 1):
        turn, other = (step % half, step // half) if step else (0, 0)
        if step == layout.parts:
            turn, other = 0, 1
        begin = channel_block(place_ref, layout, turn, other) * sub
        source = filt_hbm.at[rows_at(begin, sub, sub), :]
        copies.append(pltpu.make_async_copy(source, outs[step], sems.at[step]))
    for copy in copies:
        copy.start()
    turned[...] = jnp.zeros(turned.shape, F32)
    copies[0].wait()
    for which in range(3):
        turned[2 * which : 2 * which + 2, :] = tail[which].astype(F32).T[-2:, :]
    halo_ref[...] = turned[...].astype(BF16)
    for copy in copies[1:]:
        copy.wait()


def pack(layout, features, filters):
    parts, sub, span, channels = layout.parts, layout.sub, layout.span, layout.channels
    outs = [jax.ShapeDtypeStruct((16, channels), BF16)] + [jax.ShapeDtypeStruct((sub, span), BF16)] * (parts + 1)
    scratch = [
        pltpu.VMEM((3, channels, 128), BF16),
        pltpu.VMEM((16, channels), F32),
        pltpu.SemaphoreType.DMA((parts + 2,)),
    ]
    found = run(pack_body, layout, (features, filters), outs, scratch, estimate(2.0), in_specs=[IN_HBM] * 2)
    return found[0], (found[1], found[1 + parts]), found[2 : 1 + parts]


def three_parts(value):
    top = value.astype(BF16).astype(F32)
    middle = (value - top).astype(BF16).astype(F32)
    return [top, middle, value - top - middle]


def edge_table(table_rows, lanes, entries):
    row = lax.broadcasted_iota(jnp.int32, (table_rows, lanes), 0)
    lane = lax.broadcasted_iota(jnp.int32, (table_rows, lanes), 1)
    table = jnp.zeros((table_rows, lanes), F32)
    for rows, where, keep in entries:
        for own_row in rows:
            table = jnp.where((row == own_row) & (lane == where), keep, table)
    return table.astype(BF16)


def fill_tables(layout, place_ref, lengths_ref, taps_ref, skip_ref, fwd_edge_ref, *rest):
    cols_ref, split_ref, keep_ref, last_edge_ref, turned, lanes_ref = rest
    span = layout.span
    first = place_ref[0] * span
    _, offset = offsets_row(lengths_ref, first, span, 0)
    keep, keep_back = [], []
    for j in (1, 2):
        keep.append((offset[0:1, :] >= j).astype(F32))
        position, later = offsets_row(lengths_ref, first, span, j)
        inside = (position < layout.parts * span) & (later >= j)
        keep_back.append(inside[0:1, :].astype(F32))
    most = span - 128
    lane = lax.broadcasted_iota(jnp.int32, (1, span), 1)
    keep_ref[...] = jnp.zeros(keep_ref.shape, F32)
    for j in (0, 1):
        keep_ref[j : j + 1, :] = jnp.where(lane > j, keep[j], 0.0)
        keep_ref[2 + j : 3 + j, :] = jnp.where(lane < span - 1 - j, keep_back[j], 0.0)
    for which in range(3):
        begin = which * 256
        two, one = [2 * which], [2 * which + 1]
        fwd_edge_ref[:, begin : begin + 128] = edge_table(16, 128, [(one, 0, keep[0][:, :128])])
        fwd_edge_ref[:, begin + 128 : begin + 256] = edge_table(
            16, 128, [(two, 0, keep[1][:, :128]), (one, 1, keep[1][:, :128])]
        )
        entries = []
        for k, (lane_at, j) in enumerate(((127, 0), (127, 1), (126, 1))):
            entries.append(([3 * which + k + 16 * p for p in range(3)], lane_at, keep_back[j][:, most:]))
        last_edge_ref[:, which * 128 : (which + 1) * 128] = edge_table(48, 128, entries)
    turned[...] = jnp.zeros(turned.shape, F32)
    for which in range(3):
        turned[3 * which : 3 * which + 3, :] = taps_ref[which]
    turned[9:10, :] = skip_ref[...]
    value = turned[...]
    cols_ref[...] = value.T
    split_ref[...] = jnp.concatenate(three_parts(value), axis=0).T.astype(BF16)
    column = lax.broadcasted_iota(jnp.int32, (48, 128), 0) % 16
    for k in range(9):
        lanes_ref[:, k * 128 : (k + 1) * 128] = jnp.where(column == k, 1.0, 0.0).astype(BF16)


def table_shapes(layout):
    channels = layout.channels
    return [
        ((channels, 16), F32),
        ((channels, 48), BF16),
        ((8, layout.span), F32),
        ((48, 384), BF16),
        ((16, channels), F32),
        ((48, 9 * 128), BF16),
    ]


def gate_body(other, layout, place_ref, feat_hbm, dout_hbm, *rest):
    half, rows, span = layout.half, layout.sub, layout.span
    given, rest = (rest[:5], rest[5:]) if other else (rest[:4], rest[4:])
    qkv_ref, dout_ref, pairs, rest = rest[0], rest[1], rest[2 : 2 + half], rest[2 + half :]
    if other:
        cross, rest = rest[:half], rest[half:]
    feat_ref, spread, ends, sems = rest[-4:]
    side, _, _ = where_am_i(place_ref, layout)
    group = min(64, rows)
    copies = []
    for turn in range(half):
        block = rows_at(channel_block(place_ref, layout, turn, other) * rows, rows, rows)
        copies.append(pltpu.make_async_copy(feat_hbm.at[:, block, :], feat_ref.at[turn], sems.at[turn, 0]))
        copies.append(pltpu.make_async_copy(dout_hbm.at[block, :], dout_ref.at[turn], sems.at[turn, 1]))
        for copy in copies[-2:]:
            copy.start()
    if other:
        split_ref, keep_ref, lanes_ref, edge_ref, ends_of = given
    else:
        halo_ref, lengths_ref, taps_ref, skip_ref = given
        tables, edge_ref, ends_of = rest[:6], rest[6], rest[7]
        _, split_ref, keep_ref, _, _, lanes_ref = tables
        fill_tables(layout, place_ref, lengths_ref, taps_ref, skip_ref, edge_ref, *tables)
        ends_of[...] = halo_ref[...].astype(F32).T.astype(BF16)
    keep = [keep_ref[j : j + 1, :] for j in range(2)]
    for turn in range(half):
        block = rows_at(channel_block(place_ref, layout, turn, other) * rows, rows, rows)
        spread[...] = dot(split_ref[block, :], lanes_ref[...])
        ends[...] = dot(ends_of[block, :], edge_ref[...])
        for copy in copies[2 * turn : 2 * turn + 2]:
            copy.wait()

        def tile(index, _, turn=turn):
            local_rows = rows_at(index * group, group, group)
            filtered = []
            for which in range(3):
                value = feat_ref[turn, which, local_rows, :].astype(F32)
                moved = [pltpu.roll(value, j + 1, 1) * keep[j] for j in range(2)]
                taps = [spread[local_rows, (3 * which + j) * 128 : (3 * which + j + 1) * 128] for j in range(3)]
                parts = []
                for lane in range(0, span, 128):
                    back = [moved[j][:, lane : lane + 128] for j in range(2)]
                    if lane == 0:
                        begins = [which * 256 + j * 128 for j in range(2)]
                        back = [back[j] + ends[local_rows, begins[j] : begins[j] + 128] for j in range(2)]
                    total = taps[0] * value[:, lane : lane + 128]
                    parts.append((total + taps[1] * back[0] + taps[2] * back[1]).astype(BF16))
                filtered.append(jnp.concatenate(parts, axis=1))
                qkv_ref[turn, which, local_rows, :] = filtered[-1]
            mixed = filtered[1] * filtered[2]
            grad_in = dout_ref[turn, local_rows, :] * filtered[0]
            first = jnp.where(side == 0, mixed, grad_in)
            second = jnp.where(side == 0, grad_in, mixed)
            pairs[turn][0, local_rows, :] = first
            pairs[turn][1, local_rows, :] = second
            if other:
                cross[turn][local_rows, :] = first
            return 0

        lax.fori_loop(0, rows // group, tile, 0, unroll=rows // group)


def gate(other, layout, features, dout, *given):
    half, rows, span, channels = layout.half, layout.sub, layout.span, layout.channels
    shapes = [(half, 3, rows, span), (half, rows, span)] + [(2, rows, span)] * half
    shapes += [(rows, span)] * half if other else []
    outs = [jax.ShapeDtypeStruct(s, BF16) for s in shapes]
    if not other:
        more = table_shapes(layout) + [((16, 768), BF16), ((channels, 16), BF16)]
        outs += [jax.ShapeDtypeStruct(*s) for s in more]
    found = run(
        functools.partial(gate_body, other),
        layout,
        (features, dout, *given),
        outs,
        [
            pltpu.VMEM((half, 3, rows, span), BF16),
            pltpu.VMEM((rows, 9 * 128), F32),
            pltpu.VMEM((rows, 768), F32),
            pltpu.SemaphoreType.DMA((half, 2)),
        ],
        estimate(GATE_OTHER if other else GATE_MAIN),
        in_specs=[IN_HBM] * 2 + [HELD] * len(given),
    )
    return found[0:2], found[2 : 2 + half], found[2 + half :]


def loop(count, body, init):
    if count <= 4:
        for k in range(count):
            init = body(k, init)
        return init
    return lax.fori_loop(0, count, body, init)


def add_product(total, f, x):
    return (total[0] + f[0] * x[0] - f[1] * x[1], total[1] + f[0] * x[1] + f[1] * x[0])


def add_conjugate(total, f, x):
    return (total[0] + f[0] * x[0] + f[1] * x[1], total[1] + f[0] * x[1] - f[1] * x[0])


def turned_sum(spectrum, neighbour, sign):
    half = spectrum[0].shape[1] // 2
    parts = []
    for lanes, flip in ((slice(0, half), sign), (slice(half, None), -sign)):
        n_re, n_im = neighbour[0][:, lanes], neighbour[1][:, lanes]
        s_re, s_im = spectrum[0][:, lanes], spectrum[1][:, lanes]
        parts.append((s_re - n_im, s_im + n_re) if flip > 0 else (s_re + n_im, s_im - n_re))
    return tuple(jnp.concatenate([p[k] for p in parts], axis=1) for k in range(2))


def forward(raw, spec, begin, target, rows, table_ref):
    value = raw[pl.ds(pl.multiple_of(begin, 16), rows), :]
    spec[pl.ds(pl.multiple_of(target, 16), rows), :] = dot(jnp.concatenate([value, value], axis=1), table_ref[...])


def spectrum_at(spec, begin, group, span):
    place = pl.ds(pl.multiple_of(begin, group), group)
    return spec[place, :span], spec[place, span:]


def store_spectrum(ready, begin, value, group, span):
    place = pl.ds(pl.multiple_of(begin, group), group)
    ready[place, :span] = value[0].astype(BF16)
    ready[place, span:] = value[1].astype(BF16)


def cross_body(layout, place_ref, forward_ref, inverse_ref, filt_ref, *rest):
    parts, half, sub, span = layout.parts, layout.half, layout.sub, layout.span
    filt_in, rest = rest[: parts - 1], rest[parts - 1 :]
    signal, outs = rest[:half], rest[half : 2 * half]
    known, spec, filt_raw, raw, ready, back = rest[2 * half :]
    rank = place_ref[0]
    filt_raw[rows_at(rank * sub, sub, sub), :] = filt_ref[...]
    for step in range(1, parts):
        filt_raw[rows_at(jnp.bitwise_xor(rank, step) * sub, sub, sub), :] = filt_in[step - 1][...]
    chunk = math.gcd(parts * sub, 512)

    def transform(index, _):
        forward(filt_raw, known, index * chunk, index * chunk, chunk, forward_ref)
        return 0

    lax.fori_loop(0, parts * sub // chunk, transform, 0, unroll=True)
    side, own, _ = where_am_i(place_ref, layout)
    for step in range(half):
        raw[rows_at(jnp.bitwise_xor(own, step) * sub, sub, sub), :] = signal[step][0]
    forward(raw, spec, 0, 0, half * sub, forward_ref)
    group = 16
    zero = (jnp.zeros((group, span), F32),) * 2

    def products(index, ahead):
        def filt(k):
            return spectrum_at(known, k * sub + index * group, group, span)

        def sig(k):
            return spectrum_at(spec, k * sub + index * group, group, span)

        before = None
        if ahead:
            for place in range(half - 1, parts):
                total = loop(half, lambda k, t, p=place: add_product(t, filt(p - k), sig(k)), zero)
                if before is not None:
                    value = turned_sum(total, before, 1)
                    store_spectrum(ready, (place - half) * sub + index * group, value, group, span)
                before = total
        else:
            for place in range(half, -1, -1):
                total = loop(half, lambda k, t, p=place: add_conjugate(t, filt(half + k - p), sig(k)), zero)
                if before is not None:
                    value = turned_sum(total, before, -1)
                    store_spectrum(ready, place * sub + index * group, value, group, span)
                before = total
        return 0

    @pl.when(side == 0)
    def _():
        lax.fori_loop(0, sub // group, lambda k, _: products(k, True), 0, unroll=min(4, sub // group))

    @pl.when(side == 1)
    def _():
        lax.fori_loop(0, sub // group, lambda k, _: products(k, False), 0, unroll=min(4, sub // group))

    back[...] = dot(ready[...], inverse_ref[...])
    for step in range(half):
        outs[step][...] = back[rows_at(jnp.bitwise_xor(own, step) * sub, sub, sub), :].astype(BF16)


def cross_half(layout, tables, own, filt, signal):
    half, sub, span = layout.half, layout.sub, layout.span
    all_rows = layout.parts * sub
    rows = half * sub
    found = run(
        cross_body,
        layout,
        (*tables, own, *filt, *signal),
        [jax.ShapeDtypeStruct((sub, span), BF16)] * half
        + [jax.ShapeDtypeStruct((r, 2 * span), F32) for r in (all_rows, rows)],
        [
            pltpu.VMEM((all_rows, span), BF16),
            pltpu.VMEM((rows, span), BF16),
            pltpu.VMEM((rows, 2 * span), BF16),
            pltpu.VMEM((rows, span), F32),
        ],
        estimate(0.3),
    )
    return found[:half], found[half], found[half + 1]


def hold_body(layout, place_ref, *refs):
    count = (len(refs) - 1) // 2
    for source, target in zip(refs[:count], refs[count + 1 :]):
        target[...] = source[...]


def hold(layout, arrays, after):
    outs = [jax.ShapeDtypeStruct(a.shape, a.dtype) for a in arrays]
    return run(hold_body, layout, [*arrays, after], outs, [], estimate(4.0), in_specs=[HELD] * len(arrays) + [ANYWHERE])


def main_body(layout, place_ref, cols_ref, forward_ref, inverse_ref, known, near_spec, *rest):
    parts, half, sub, span = layout.parts, layout.half, layout.sub, layout.span
    firsts, cross, outs = (rest[k * half : (k + 1) * half] for k in range(3))
    raw, spec, ready, back = rest[3 * half :]
    side, own, _ = where_am_i(place_ref, layout)
    block = parts * sub
    for step in range(half):
        place = jnp.bitwise_xor(own, step)
        raw[rows_at((side * half + place) * sub, sub, sub), :] = firsts[step][1]
        raw[rows_at(((1 - side) * half + place) * sub, sub, sub), :] = cross[step][...]
    chunk = math.gcd(block, 512)

    def transform(index, _):
        forward(raw, spec, index * chunk, index * chunk, chunk, forward_ref)
        return 0

    lax.fori_loop(0, block // chunk, transform, 0, unroll=True)
    group = 16
    zero = (jnp.zeros((group, span), F32),) * 2

    def products(index, first_half):
        def filt(k):
            return spectrum_at(known, k * sub + index * group, group, span)

        def near(k):
            return spectrum_at(near_spec, k * sub + index * group, group, span)

        def far(k):
            return spectrum_at(spec, k * sub + index * group, group, span)

        def store(kind, place, value):
            store_spectrum(ready, (kind * half + place) * sub + index * group, value, group, span)

        before = None
        if first_half:
            for place in range(half):
                total = loop(place + 1, lambda k, t, p=place: add_product(t, filt(k), near(p - k)), zero)
                store(0, place, total if before is None else turned_sum(total, before, 1))
                before = total
            before = None
            for place in range(half, -1, -1):
                total = loop(parts - place, lambda k, t, p=place: add_conjugate(t, filt(k), far(p + k)), zero)
                if before is not None:
                    store(1, place, turned_sum(total, before, -1))
                before = total
        else:
            for place in range(half - 1, -1, -1):
                total = loop(half - place, lambda k, t, p=place: add_conjugate(t, filt(k), near(p + k)), zero)
                store(0, place, total if before is None else turned_sum(total, before, -1))
                before = total
            before = None
            for place in range(half - 1, parts):
                total = loop(place + 1, lambda k, t, p=place: add_product(t, filt(k), far(p - k)), zero)
                if before is not None:
                    store(1, place - half, turned_sum(total, before, 1))
                before = total
        return 0

    @pl.when(side == 0)
    def _():
        lax.fori_loop(0, sub // group, lambda k, _: products(k, True), 0, unroll=min(4, sub // group))

    @pl.when(side == 1)
    def _():
        lax.fori_loop(0, sub // group, lambda k, _: products(k, False), 0, unroll=min(4, sub // group))

    back[...] = dot(ready[...], inverse_ref[...])
    begin = channel_block(place_ref, layout, 0, 0) * sub
    skip = cols_ref[rows_at(begin, sub, sub), 9:10]
    for step in range(half):
        place = jnp.bitwise_xor(own, step)
        for kind in range(2):
            value = back[rows_at((kind * half + place) * sub, sub, sub), :]
            direct = firsts[step][kind].astype(F32)
            outs[step][kind] = (value + skip * direct).astype(BF16)


def main_half(layout, cols, tables, known, near, firsts, cross):
    half, sub, span, parts = layout.half, layout.sub, layout.span, layout.parts
    rows = parts * sub
    return run(
        main_body,
        layout,
        (cols, *tables, known, near, *firsts, *cross),
        [jax.ShapeDtypeStruct((2, sub, span), BF16)] * half,
        [
            pltpu.VMEM((rows, span), BF16),
            pltpu.VMEM((rows, 2 * span), F32),
            pltpu.VMEM((2 * half * sub, 2 * span), BF16),
            pltpu.VMEM((2 * half * sub, span), F32),
        ],
        estimate(10.0),
    )


def pick_first(value):
    row = lax.broadcasted_iota(jnp.int32, (16, 128), 0)
    lane = lax.broadcasted_iota(jnp.int32, (16, 128), 1)
    table = jnp.where((row == lane) & (row < 2), 1.0, 0.0).astype(BF16)
    dims = (((1,), (1,)), ((), ()))
    return lax.dot_general(table, value, dims, preferred_element_type=F32).astype(BF16)


def other_body(layout, place_ref, cols_ref, forward_ref, inverse_ref, filt_ref, other_ref, *rest):
    parts, half, sub, span = layout.parts, layout.half, layout.sub, layout.span
    seconds, leads, outs = (rest[k * half : (k + 1) * half] for k in range(3))
    raw, spec, ready, back = rest[3 * half :]
    side, own, _ = where_am_i(place_ref, layout)
    rank = place_ref[0]
    block, kind_rows = parts * sub, half * sub
    begin = channel_block(place_ref, layout, 0, 1) * sub
    raw[rows_at(rank * sub, sub, sub), :] = filt_ref[...]
    for step in range(1, parts):
        place = rows_at(jnp.bitwise_xor(rank, step) * sub, sub, sub)
        raw[place, :] = other_ref[(step - 1) * sub : step * sub, :]
    for step in range(half):
        place = block + jnp.bitwise_xor(own, step) * sub
        raw[rows_at(place + side * kind_rows, sub, sub), :] = seconds[step][0]
        raw[rows_at(place + (1 - side) * kind_rows, sub, sub), :] = seconds[step][1]

    def transform(kind, _):
        source = jnp.where(kind == 0, 0, block + (kind - 1) * kind_rows)
        forward(raw, spec, source, kind * kind_rows, kind_rows, forward_ref)
        return 0

    lax.fori_loop(0, 3, transform, 0, unroll=True)
    group = 16
    zero = (jnp.zeros((group, span), F32),) * 2

    def products(index, _):
        def read(kind, k):
            return spectrum_at(spec, (kind * half + k) * sub + index * group, group, span)

        def store(kind, k, value):
            store_spectrum(ready, (kind * half + k) * sub + index * group, value, group, span)

        before = None
        for place in range(half):
            total = loop(place + 1, lambda k, t, p=place: add_product(t, read(0, k), read(1, p - k)), zero)
            store(0, place, total if before is None else turned_sum(total, before, 1))
            before = total
        before = None
        for place in range(half - 1, -1, -1):
            total = loop(half - place, lambda k, t, p=place: add_conjugate(t, read(0, k), read(2, p + k)), zero)
            store(1, place, total if before is None else turned_sum(total, before, -1))
            before = total
        return 0

    lax.fori_loop(0, sub // group, products, 0, unroll=min(4, sub // group))
    back[...] = dot(ready[...], inverse_ref[...])
    skip = cols_ref[rows_at(begin, sub, sub), 9:10]
    for step in range(half):
        place = jnp.bitwise_xor(own, step) * sub
        for kind in range(2):
            source = jnp.where(side == kind, 0, 1) * kind_rows + place
            value = back[rows_at(source, sub, sub), :]
            direct = seconds[step][kind].astype(F32)
            found = (value + skip * direct).astype(BF16)
            outs[step][kind] = found
            leads[step][kind] = pick_first(found[:, :128])


def other_half(layout, cols, tables, filters, other, seconds):
    half, sub, span, parts = layout.half, layout.sub, layout.span, layout.parts
    rows = 3 * half * sub
    found = run(
        other_body,
        layout,
        (cols, *tables, filters, other, *seconds),
        [jax.ShapeDtypeStruct((2, 16, sub), BF16)] * half + [jax.ShapeDtypeStruct((2, sub, span), BF16)] * half,
        [
            pltpu.VMEM(((parts + 2 * half) * sub, span), BF16),
            pltpu.VMEM((rows, 2 * span), F32),
            pltpu.VMEM((2 * half * sub, 2 * span), BF16),
            pltpu.VMEM((2 * half * sub, span), F32),
        ],
        estimate(8.0),
    )
    return found[:half], found[half:]


def results(side, plain, mixed, crossed):
    if crossed is not None:
        mixed = (mixed.astype(F32) + crossed.astype(F32)).astype(BF16)
    return jnp.where(side == 0, plain, mixed), jnp.where(side == 0, mixed, plain)


def first_body(layout, place_ref, qkv_main, dout_main, qkv_other, dout_other, *refs):
    half, sub = layout.half, layout.sub
    main, rest, crossed = (refs[k * half : (k + 1) * half] for k in range(3))
    out_ref, grads = refs[3 * half :]
    side, _, _ = where_am_i(place_ref, layout)
    for turn in range(half):
        for other in range(2):
            place = rows_at(channel_block(place_ref, layout, turn, other) * sub, sub, sub)
            qkv, dout_ref = (qkv_other, dout_other) if other else (qkv_main, dout_main)
            source = (rest if other else main)[turn]
            if other and turn:
                fill = jnp.zeros((112, sub), F32)
                pair = [jnp.concatenate([source[k].astype(F32), fill], axis=0).T.astype(BF16) for k in range(2)]
            else:
                pair = [source[k, :, 0:128] for k in range(2)]
            pair = results(side, *pair, crossed[turn][:, 0:128] if other else None)
            y_out, dmixed = (f.astype(F32) for f in pair)
            grads[0, place, :] = dout_ref[turn, :, 0:128].astype(F32) * y_out
            grads[1, place, :] = dmixed * qkv[turn, 2, :, 0:128].astype(F32)
            grads[2, place, :] = dmixed * qkv[turn, 1, :, 0:128].astype(F32)
    out_ref[...] = jnp.zeros(out_ref.shape, F32)
    for which in range(3):
        out_ref[2 * which : 2 * which + 2, :] = grads[which].T[0:2, :]


def first_grads(layout, gated, main, rest, crossed):
    channels = layout.channels
    return run(
        first_body,
        layout,
        (*gated, *main, *rest, *crossed),
        jax.ShapeDtypeStruct((8, channels), F32),
        [pltpu.VMEM((3, channels, 128), F32)],
        estimate(6.0),
    )


def final_body(blocks, chained, layout, place_ref, qkv_main, dout_main, qkv_other, dout_other, split_ref, lanes_ref, keep_ref, *refs, wait=True):
    rows, span = layout.sub, layout.span
    found = []
    for _, other in blocks:
        count = 2 if other else 1
        found.append(refs[:count])
        refs = refs[count:]
    refs = refs[1 + 2 * chained :]
    out_hbm, dfeat_hbm, partial, out_ref, dfeat_ref, spread, sems = refs
    most = span - 128
    side, _, _ = where_am_i(place_ref, layout)
    group = min(64, rows)
    keep = [keep_ref[2 + j : 3 + j, :] for j in range(2)]
    copies = []
    for k, (turn, other) in enumerate(blocks):
        block = rows_at(channel_block(place_ref, layout, turn, other) * rows, rows, rows)
        qkv, dout_ref = (qkv_other, dout_other) if other else (qkv_main, dout_main)
        source, crossed = found[k] if other else (found[k][0], None)
        spread[...] = dot(split_ref[block, :], lanes_ref[...])

        def tile(index, _, k=k, turn=turn, qkv=qkv, dout_ref=dout_ref, source=source, crossed=crossed):
            local_rows = rows_at(index * group, group, group)
            pair = [source[kind, local_rows, :] for kind in range(2)]
            pair = results(side, *pair, None if crossed is None else crossed[local_rows, :])
            out_ref[k, local_rows, :] = qkv[turn, 0, local_rows, :] * pair[0]
            y_out, dmixed = (f.astype(F32) for f in pair)
            grads = (
                dout_ref[turn, local_rows, :].astype(F32) * y_out,
                dmixed * qkv[turn, 2, local_rows, :].astype(F32),
                dmixed * qkv[turn, 1, local_rows, :].astype(F32),
            )
            for which in range(3):
                ahead = [pltpu.roll(grads[which], span - 1 - j, 1) * keep[j] for j in range(2)]
                taps = [spread[local_rows, (3 * which + j) * 128 : (3 * which + j + 1) * 128] for j in range(3)]
                for lane in range(0, span, 128):
                    total = taps[0] * grads[which][:, lane : lane + 128]
                    total = total + taps[1] * ahead[0][:, lane : lane + 128] + taps[2] * ahead[1][:, lane : lane + 128]
                    if lane == most:
                        partial[k, which, local_rows, :] = total
                    else:
                        dfeat_ref[k, which, local_rows, lane : lane + 128] = total.astype(BF16)
            return 0

        lax.fori_loop(0, rows // group, tile, 0, unroll=rows // group)
        copies.append(pltpu.make_async_copy(out_ref.at[k], out_hbm.at[block, :], sems.at[k, 0]))
        copies.append(pltpu.make_async_copy(dfeat_ref.at[k], dfeat_hbm.at[:, block, pl.ds(0, most)], sems.at[k, 1]))
        for copy in copies[-2:]:
            copy.start()
    if not wait:
        return copies
    for copy in copies:
        copy.wait()


def final(blocks, layout, gated, shared, found, after, earlier):
    span, channels, rows, count = layout.span, layout.channels, layout.sub, len(blocks)
    operands = [*gated, *shared]
    for turn, other in blocks:
        main, rest, crossed = (f[turn] for f in found)
        operands += [rest, crossed] if other else [main]
    in_specs = [HELD] * len(operands) + [ANYWHERE]
    operands.append(after)
    aliases = {}
    if earlier:
        operands += earlier
        in_specs += [IN_HBM] * 2
        aliases = {len(operands) - 2: 0, len(operands) - 1: 1}
    return run(
        functools.partial(final_body, blocks, bool(earlier)),
        layout,
        operands,
        [
            jax.ShapeDtypeStruct((channels, span), BF16),
            jax.ShapeDtypeStruct((3, channels, span), BF16),
            jax.ShapeDtypeStruct((count, 3, rows, 128), F32),
        ],
        [
            pltpu.VMEM((count, rows, span), BF16),
            pltpu.VMEM((count, 3, rows, span - 128), BF16),
            pltpu.VMEM((rows, 9 * 128), F32),
            pltpu.SemaphoreType.DMA((count, 2)),
        ],
        estimate(1.2 * count),
        in_specs=in_specs,
        out_specs=[IN_HBM, IN_HBM, HELD],
        aliases=aliases,
    )


def finish_body(lists, layout, place_ref, ahead_ref, taps_ref, edge_ref, *refs):
    partials, refs = refs[: len(lists)], refs[len(lists) + 1 :]
    dfeat_hbm, rows_ref, placed, dfeat_ref, sems = refs
    rows, span = layout.sub, layout.span
    for which in range(3):
        first, second = (ahead_ref[2 * which + k : 2 * which + k + 1, :] for k in range(2))
        one, two = (taps_ref[3 * which + k : 3 * which + k + 1, :] for k in (1, 2))
        for k, value in enumerate((one * first, two * second, two * first)):
            rows_ref[3 * which + k : 3 * which + k + 1, :] = value
    rows_ref[9:16, :] = jnp.zeros((7, layout.channels), F32)
    split = jnp.concatenate(three_parts(rows_ref[...]), axis=0).T.astype(BF16)
    placed[...] = dot(split, edge_ref[...])
    copies = []
    for blocks, partial in zip(lists, partials):
        for k, (turn, other) in enumerate(blocks):
            block = rows_at(channel_block(place_ref, layout, turn, other) * rows, rows, rows)
            for which in range(3):
                value = partial[k, which] + placed[block, which * 128 : (which + 1) * 128]
                dfeat_ref[which, block, :] = value.astype(BF16)
            target = dfeat_hbm.at[:, block, pl.ds(span - 128, 128)]
            copies.append(pltpu.make_async_copy(dfeat_ref.at[:, block, :], target, sems.at[len(copies)]))
            copies[-1].start()
    for copy in copies:
        copy.wait()


def last_body(lists, layout, place_ref, *refs):
    count = 7 + 2 * len(lists[-1])
    given, refs = refs[:count], refs[count:]
    edge, partials, earlier, outs, refs = refs[:3], refs[3:5], refs[5:7], refs[7:9], refs[9:]
    scratch, partial = refs[1:5], refs[0]
    copies = final_body(lists[-1], True, layout, place_ref, *given, None, *earlier, *outs, partial, *scratch, wait=False)
    finish_body(lists, layout, place_ref, *edge, *partials, partial, None, outs[1], *refs[5:])
    for copy in copies:
        copy.wait()


def last(lists, layout, gated, shared, found, edge, partials, earlier):
    span, channels, rows, count = layout.span, layout.channels, layout.sub, len(lists[-1])
    operands = [*gated, *shared]
    for turn, _ in lists[-1]:
        operands += [found[1][turn], found[2][turn]]
    operands += [*edge, *partials]
    in_specs = [HELD] * len(operands) + [IN_HBM] * 2
    operands += earlier
    return run(
        functools.partial(last_body, lists),
        layout,
        operands,
        [jax.ShapeDtypeStruct((channels, span), BF16), jax.ShapeDtypeStruct((3, channels, span), BF16)],
        [
            pltpu.VMEM((count, 3, rows, 128), F32),
            pltpu.VMEM((count, rows, span), BF16),
            pltpu.VMEM((count, 3, rows, span - 128), BF16),
            pltpu.VMEM((rows, 9 * 128), F32),
            pltpu.SemaphoreType.DMA((count, 2)),
            pltpu.VMEM((16, channels), F32),
            pltpu.VMEM((channels, 384), F32),
            pltpu.VMEM((3, channels, 128), BF16),
            pltpu.SemaphoreType.DMA((layout.parts,)),
        ],
        estimate(3.0),
        in_specs=in_specs,
        out_specs=[IN_HBM, IN_HBM],
        aliases={len(operands) - 2: 0, len(operands) - 1: 1},
    )


def swap(value, step, parts, axis="seq"):
    return lax.ppermute(value, axis, [(source, source ^ step) for source in range(parts)])


def around(value, steps, parts):
    return lax.ppermute(value, "seq", [(source, (source + steps) % parts) for source in range(parts)])


def local(features, dout, filters, taps, skip, lengths):
    parts = lax.axis_size("seq")
    _, channels, span = features.shape
    layout = Layout(parts, channels, span)
    half = layout.half
    tables = [jnp.asarray(t) for t in block_tables(span)]

    features, dout, filters = (pltpu.with_memory_space_constraint(a, pltpu.HBM) for a in (features, dout, filters))

    halo, own_filt, filt = pack(layout, features, filters)
    halo = around(halo, 1, parts)
    filt = [swap(filt[step - 1], step, parts) for step in range(1, parts)]
    other = swap(jnp.concatenate(filt, axis=0), 1, 2, "groups")
    first_given = (halo, lengths.reshape(1, -1), taps, skip.reshape(1, channels))
    gated_main, firsts, shared = gate(0, layout, features, dout, *first_given)
    cols, split, keep, last_edge, taps_rows, lanes, first_edge, ends_of = shared
    gated_other, seconds, cross = gate(1, layout, features, dout, split, keep, lanes, first_edge, ends_of)
    firsts = [firsts[0]] + [swap(firsts[step], step, parts) for step in range(1, half)]
    cross = [swap(cross[step], step + half, parts) for step in range(half)]
    seconds = [seconds[0]] + [swap(seconds[step], step, parts) for step in range(1, half)]

    sent, known, near = cross_half(layout, tables, own_filt[0], filt, firsts)
    crossed = [swap(sent[step], step + half, parts) for step in range(half)]
    main = main_half(layout, cols, tables, known, near, firsts, cross)
    main = [main[0]] + [swap(main[step], step, parts) for step in range(1, half)]
    leads, rest = other_half(layout, cols, tables, own_filt[1], other, seconds)
    crossed = hold(layout, crossed, leads[0])
    leads = [swap(leads[step], step, parts) for step in range(1, half)]
    rest = [rest[0]] + [swap(rest[step], step, parts) for step in range(1, half)]

    gated = (*gated_main, *gated_other)
    found = (main, rest, crossed)
    shared = (split, lanes, keep)
    lists = [[(0, 0), (0, 1)], [(turn, 0) for turn in range(1, half)], [(turn, 1) for turn in range(1, half)]]
    ahead = around(first_grads(layout, gated, main, [rest[0], *leads], crossed), -1, parts)
    done, partials, after = (), [], crossed[0]
    for blocks in lists[:2]:
        *done, partial = final(blocks, layout, gated, shared, found, after, done)
        partials.append(partial)
        after = partial
    return tuple(last(lists, layout, gated, shared, found, (ahead, taps_rows, last_edge), partials, done))


def solution(mesh):
    in_specs = (
        P(None, ("chan", "sub"), ("groups", "seq")),
        P(("chan", "sub"), ("groups", "seq")),
        P(("chan", "sub"), "seq"),
        P(None, None, ("chan", "sub")),
        P(("chan", "sub")),
        P("groups"),
    )
    out_specs = (P(("chan", "sub"), ("groups", "seq")), P(None, ("chan", "sub"), ("groups", "seq")))
    return jax.shard_map(local, mesh=mesh, in_specs=in_specs, out_specs=out_specs, check_vma=False)
```
